32 devices in a mesh: dp: 16 (over z, x, core), mp: 2 (over y).
Axes of the slice: x: 2, y: 2, z: 4, core: 2. Of those that a mesh axis runs over, the one named last changes fastest.
Arguments:
- x_in: bfloat16 [128, 1024, 512], P('dp', 'mp'), may hold values from -6 to 6
- d_in: bfloat16 [128, 1024, 512], P('dp', 'mp'), may hold values from -6 to 6
- segments: int32 [128, 1024], P('dp'), may hold values from 0 to 65, as said below
- cot_x: bfloat16 [128, 1024, 512], P('dp', 'mp'), may hold values from -6 to 6
- cot_d: bfloat16 [128, 1024, 512], P('dp', 'mp'), may hold values from -6 to 6
- w_qkv: float32 [512, 3, 512], P('dp', None, 'mp'), may hold values from -0.25 to 0.25
- w_out: float32 [512, 512], P('mp', 'dp'), may hold values from -2 to 2
- w_in: float32 [512, 2048], P('dp', 'mp'), may hold values from -0.25 to 0.25
- w_back: float32 [2048, 512], P('mp', 'dp'), may hold values from -0.125 to 0.125
- norms: float32 [4, 512], P(None, 'dp'), as said below
- qkv_mom: float32 [512, 3, 512], P('dp', None, 'mp'), may hold values from -4096 to 4096
- qkv_sec: float32 [512, 3, 512], P('dp', None, 'mp'), may hold values from 524288 to 2097152
- out_mom: float32 [512, 512], P('mp', 'dp'), may hold values from -640 to 640
- out_sec: float32 [512, 512], P('mp', 'dp'), may hold values from 11796.48 to 47185.92
- in_mom: float32 [512, 2048], P('dp', 'mp'), may hold values from -896 to 896
- in_sec: float32 [512, 2048], P('dp', 'mp'), may hold values from 20971.52 to 83886.08
- back_mom: float32 [2048, 512], P('mp', 'dp'), may hold values from -2048 to 2048
- back_sec: float32 [2048, 512], P('mp', 'dp'), may hold values from 131072 to 524288
- norm_mom: float32 [4, 512], P(None, 'dp'), may hold values from -3072 to 3072
- norm_sec: float32 [4, 512], P(None, 'dp'), may hold values from 294912 to 1179648
Outputs:
- x_out: bfloat16 [128, 1024, 512], P('dp', 'mp')
- d_out: bfloat16 [128, 1024, 512], P('dp', 'mp')
- x_grad: float32 [128, 1024, 512], P('dp', 'mp')
- qkv_mom_new: float32 [512, 3, 512], P('dp', None, 'mp')
- qkv_sec_new: float32 [512, 3, 512], P('dp', None, 'mp')
- qkv_new: float32 [512, 3, 512], P('dp', None, 'mp')
- out_mom_new: float32 [512, 512], P('mp', 'dp')
- out_sec_new: float32 [512, 512], P('mp', 'dp')
- out_new: float32 [512, 512], P('mp', 'dp')
- in_mom_new: float32 [512, 2048], P('dp', 'mp')
- in_sec_new: float32 [512, 2048], P('dp', 'mp')
- in_new: float32 [512, 2048], P('dp', 'mp')
- back_mom_new: float32 [2048, 512], P('mp', 'dp')
- back_sec_new: float32 [2048, 512], P('mp', 'dp')
- back_new: float32 [2048, 512], P('mp', 'dp')
- norm_mom_new: float32 [4, 512], P(None, 'dp')
- norm_sec_new: float32 [4, 512], P(None, 'dp')
- norm_new: float32 [4, 512], P(None, 'dp')
The draws below stay inside these ranges and needn't reach their ends.
Inputs may be any that keep to these rules, and one draw needn't show every extreme that they name: `segments`: segment ids start at 0, never fall along a sequence, rise by at most one from a position to the next, and the last id of every sequence is exactly max(128, 2) // 2 + 1. `norms`: rows 0 and 2 are gains, rows 1 and 3 biases.
All inputs are finite; a program needn't handle non-finite values.
Results may differ from the reference program's by a relative error of at most 0.012.
The reference program's roundings to bfloat16 on the way count: a program that leaves them out, or rounds other values in their place, can miss the bound.
Values may be sent and summed in bfloat16 or wider, within the bound.
No kernel may reach another device: no remote copies, remote signals or barrier semaphores. Data moves between devices by JAX's collectives and lax.ppermute only.
A program may use at most 320 MiB of HBM per device.

```python
import math
import jax
import jax.numpy as jnp
from jax import lax

D = 512
H = 8
FF = 2048
LEN = 1024
STEP = 5
HD = 64
SEQS = 128
TOKENS = 131072


def draw_segments(key, part):
    key = jax.random.fold_in(key, 7)
    key_start, key_finish, key_marks = jax.random.split(key, 3)
    edge = max(LEN // 8, 2)
    extra = edge // 2
    start = jax.random.randint(key_start, (SEQS, 1), 1, edge)
    finish = jax.random.randint(key_finish, (SEQS, 1), LEN - edge, LEN - extra)
    position = jnp.arange(LEN)[None, :]
    inside = (position > start) & (position <= finish)
    eligible = jnp.logical_not(inside) & (position > 0) & (position != start)
    noise = jax.random.randint(key_marks, (SEQS, LEN), 0, 65536)
    scores = jnp.where(eligible, noise * LEN + position, -1)
    chosen = lax_top(scores, extra)
    picked = jnp.any(position[:, :, None] == chosen[:, None, :], axis=2)
    marks = picked | (position == start)
    return jnp.cumsum(marks.astype(jnp.int32), axis=1).astype(jnp.int32)


def lax_top(scores, count):
    return jax.lax.top_k(scores, count)[1].astype(jnp.int32)


def draw_norms(key, part):
    key = jax.random.fold_in(key, 11)
    key_gain, key_bias = jax.random.split(key)
    gain_vals = jax.random.uniform(key_gain, (4, D), jnp.float32, 0.6, 1.4)
    offsets = 0.3 * jax.random.normal(key_bias, (4, D), jnp.float32)
    row_index = jnp.arange(4)[:, None]
    return jnp.where(row_index % 2 == 0, gain_vals, offsets)


def level_of(stream_key, dims, shards, smallest, largest):
    gain, own = 1.0, jax.random.fold_in(stream_key, 6)
    for axis_at, shards_of in shards:
        steps = jnp.exp(jax.random.uniform(jax.random.fold_in(own, axis_at), (shards_of,), jnp.float32, smallest / len(shards), largest / len(shards)))
        gain = gain * jnp.repeat(steps, dims[axis_at] // shards_of).reshape([-1 if axis == axis_at else 1 for axis in range(len(dims))])
    return gain


def bell_draw(rng, dims, deviation, most, cuts=(), kind=jnp.bfloat16):
    loudness = level_of(rng, dims, cuts, -0.22, 0.18) if cuts else 1.0
    values = jax.random.normal(rng, dims, jnp.float32) * deviation * loudness
    return jnp.minimum(jnp.maximum(values, -most), most).astype(kind)


def setup_inputs(seed: int = 0) -> dict:
    arg_keys = jax.random.split(jax.random.key(seed), 21)
    x_in = bell_draw(arg_keys[0], (SEQS, LEN, D), 1.0, 6.0, ((0, 16), (1, 2)))
    d_in = bell_draw(arg_keys[1], (SEQS, LEN, D), 1.0, 6.0, ((0, 16), (1, 2)))
    segments = draw_segments(jax.random.fold_in(arg_keys[20], 71), 0)
    cot_x = bell_draw(arg_keys[3], (SEQS, LEN, D), 1.0, 6.0, ((0, 16), (1, 2)))
    cot_d = bell_draw(arg_keys[4], (SEQS, LEN, D), 1.0, 6.0, ((0, 16), (1, 2)))
    w_qkv = bell_draw(arg_keys[5], (D, 3, D), D ** -0.5, 0.25, ((0, 16), (2, 2)), jnp.float32)
    w_out = bell_draw(arg_keys[6], (D, D), (D // 64) ** -0.5, 2.0, ((0, 2), (1, 16)), jnp.float32)
    w_in = bell_draw(arg_keys[7], (D, FF), D ** -0.5, 0.25, ((0, 16), (1, 2)), jnp.float32)
    w_back = bell_draw(arg_keys[8], (FF, D), FF ** -0.5, 0.125, ((0, 2), (1, 16)), jnp.float32)
    norms = draw_norms(jax.random.fold_in(arg_keys[20], 71), 0)
    qkv_mom = bell_draw(arg_keys[10], (D, 3, D), (2.0 * TOKENS ** 0.5), 4096.0, ((0, 16), (2, 2)), jnp.float32)
    qkv_sec = jnp.clip(jnp.exp(math.log(2097152) - 1.3862944 * jax.random.uniform(arg_keys[11], (D, 3, D), jnp.float32) ** level_of(arg_keys[11], (D, 3, D), ((0, 16), (2, 2)), -0.2, 0.2)), 524288.0, 2097152)
    out_mom = bell_draw(arg_keys[12], (D, D), (0.3 * TOKENS ** 0.5), 640.0, ((0, 2), (1, 16)), jnp.float32)
    out_sec = jnp.clip(jnp.exp(math.log(47185.92) - 1.3862944 * jax.random.uniform(arg_keys[13], (D, D), jnp.float32) ** level_of(arg_keys[13], (D, D), ((0, 2), (1, 16)), -0.2, 0.2)), 11796.48, 47185.92)
    in_mom = bell_draw(arg_keys[14], (D, FF), (0.4 * TOKENS ** 0.5), 896.0, ((0, 16), (1, 2)), jnp.float32)
    in_sec = jnp.clip(jnp.exp(math.log(83886.08) - 1.3862944 * jax.random.uniform(arg_keys[15], (D, FF), jnp.float32) ** level_of(arg_keys[15], (D, FF), ((0, 16), (1, 2)), -0.2, 0.2)), 20971.52, 83886.08)
    back_mom = bell_draw(arg_keys[16], (FF, D), (1.0 * TOKENS ** 0.5), 2048.0, ((0, 2), (1, 16)), jnp.float32)
    back_sec = jnp.clip(jnp.exp(math.log(524288.0) - 1.3862944 * jax.random.uniform(arg_keys[17], (FF, D), jnp.float32) ** level_of(arg_keys[17], (FF, D), ((0, 2), (1, 16)), -0.2, 0.2)), 131072.0, 524288.0)
    norm_mom = bell_draw(arg_keys[18], (4, D), (1.5 * TOKENS ** 0.5), 3072.0, ((1, 16),), jnp.float32)
    norm_sec = jnp.clip(jnp.exp(math.log(1179648) - 1.3862944 * jax.random.uniform(arg_keys[19], (4, D), jnp.float32) ** level_of(arg_keys[19], (4, D), ((1, 16),), -0.2, 0.2)), 294912.0, 1179648)
    return dict(x_in=x_in, d_in=d_in, segments=segments, cot_x=cot_x, cot_d=cot_d, w_qkv=w_qkv, w_out=w_out, w_in=w_in, w_back=w_back, norms=norms, qkv_mom=qkv_mom, qkv_sec=qkv_sec, out_mom=out_mom, out_sec=out_sec, in_mom=in_mom, in_sec=in_sec, back_mom=back_mom, back_sec=back_sec, norm_mom=norm_mom, norm_sec=norm_sec)


@jax.custom_vjp
def lower_residual(v):
    return lax.optimization_barrier(v.astype(jnp.bfloat16)).astype(jnp.float32)

@jax.custom_vjp
def lower_residual_backward(v):
    return v

def low_keep(v):
    return (lower_residual(v), None)

def low_pass(kept, grad):
    return (grad,)

def back_keep(v):
    return (v, None)

def back_low(kept, grad):
    return (lower_residual(grad),)
lower_residual.defvjp(low_keep, low_pass)
lower_residual_backward.defvjp(back_keep, back_low)
highest_precision = lax.Precision.HIGHEST
neg_fill = -1000000000.0
norm_eps = 1e-05
beta_first = 0.5
beta_second = 0.5
adam_eps = 1e-08
decay_rate = 0.01

def layer_norm(resid, gain_vals, bias_vals):
    center = resid - lax.optimization_barrier(jnp.mean(resid, axis=-1, keepdims=True))
    spread = lax.optimization_barrier(jnp.mean(center * center, axis=-1, keepdims=True))
    return center * lax.rsqrt(spread + norm_eps) * gain_vals + bias_vals

def gelu_exact(value):
    return jax.nn.gelu(value, approximate=False)

def attend(pieces):
    query_rows, key_rows, value_rows, segment_ids = pieces
    scores = jnp.einsum('qhe,khe->hqk', query_rows, key_rows, precision=highest_precision) * HD ** (-0.5)
    scores = lower_residual_backward(scores)
    position = jnp.arange(segment_ids.shape[0])
    allowed = (position[None, :] <= position[:, None]) & (segment_ids[None, :] == segment_ids[:, None])
    scores = jnp.where(allowed[None], scores, neg_fill)
    row_max = lax.optimization_barrier(jnp.max(scores, axis=-1, keepdims=True))
    exponent = jnp.exp(scores - row_max)
    probabilities = lower_residual(exponent / lax.optimization_barrier(jnp.sum(exponent, axis=-1, keepdims=True)))
    return jnp.einsum('hqk,khe->qhe', probabilities, value_rows, precision=highest_precision)

def block_forward(residual_state, dual, query_key_value_weight, output_weight, input_weight, backproj_weight, gain_rows, segment_ids):
    block_size = residual_state.shape[0]
    projected_rows = jnp.einsum('xor,rnq->xonq', residual_state, query_key_value_weight, precision=highest_precision)
    query_rows = lower_residual_backward(lower_residual(projected_rows[:, :, 0])).reshape(block_size, LEN, H, HD)
    key_rows = lower_residual_backward(lower_residual(projected_rows[:, :, 1])).reshape(block_size, LEN, H, HD)
    value_rows = lower_residual_backward(lower_residual(projected_rows[:, :, 2])).reshape(block_size, LEN, H, HD)
    mixture_rows = lax.map(jax.checkpoint(attend), (query_rows, key_rows, value_rows, segment_ids))
    mixture_rows = lower_residual_backward(lower_residual(mixture_rows.reshape(block_size, LEN, D)))
    attended_rows = lower_residual_backward(jnp.einsum('mbi,iy->mby', mixture_rows, output_weight, precision=highest_precision))
    first_input = layer_norm(residual_state + attended_rows, gain_rows[0], gain_rows[1])
    d_one = dual + attended_rows
    hidden_input = lower_residual_backward(jnp.einsum('eot,tv->eov', lower_residual(first_input), input_weight, precision=highest_precision))
    active_values = lower_residual(gelu_exact(hidden_input))
    feedforward_output = lower_residual_backward(jnp.einsum('mbi,iy->mby', active_values, backproj_weight, precision=highest_precision))
    x_two = layer_norm(first_input + feedforward_output, gain_rows[2], gain_rows[3])
    return (x_two, d_one + feedforward_output)

def adam_update(weight, grad, mom, sec, rate):
    mom_new = beta_first * mom + (1.0 - beta_first) * grad
    sec_new = beta_second * sec + (1.0 - beta_second) * grad * grad
    scaled = mom_new / (1.0 - beta_first ** STEP) / (jnp.sqrt(sec_new / (1.0 - beta_second ** STEP)) + adam_eps)
    return (mom_new, sec_new, weight - rate * (scaled + decay_rate * weight))

def reference(x_in, d_in, segments, cot_x, cot_d, w_qkv, w_out, w_in, w_back, norms, qkv_mom, qkv_sec, out_mom, out_sec, in_mom, in_sec, back_mom, back_sec, norm_mom, norm_sec):
    copies = (lower_residual(w_qkv), lower_residual(w_out), lower_residual(w_in), lower_residual(w_back), lower_residual(norms))
    block_size = math.gcd(SEQS, 4)
    block_count = SEQS // block_size

    def blocks(array):
        return array.reshape((block_count, block_size) + array.shape[1:])

    def one_block(totals, item):
        residual_state, dual, cot_stream, cot_dual, segment_ids = item

        def forward(stream_in, query_key_value_weight, output_weight, input_weight, backproj_weight, gain_rows):
            return block_forward(stream_in, dual, query_key_value_weight, output_weight, input_weight, backproj_weight, gain_rows, segment_ids)
        outputs, pullback = jax.vjp(forward, residual_state, copies[0], copies[1], copies[2], copies[3], copies[4])
        grads = pullback((cot_stream, cot_dual))
        totals = tuple((total + grad for total, grad in zip(totals, grads[1:])))
        return (totals, (outputs[0], outputs[1], grads[0]))
    zeros = tuple((jnp.zeros(item.shape, jnp.float32) for item in copies))
    inputs = (blocks(x_in.astype(jnp.float32)), blocks(d_in.astype(jnp.float32)), blocks(cot_x.astype(jnp.float32)), blocks(cot_d.astype(jnp.float32)), blocks(segments))
    sums, (stream_out, dual_out, stream_grad) = lax.scan(one_block, zeros, inputs)
    full_shape = (SEQS, LEN, D)
    x_out = stream_out.reshape(full_shape).astype(jnp.bfloat16)
    d_out = dual_out.reshape(full_shape).astype(jnp.bfloat16)
    x_grad = stream_grad.reshape(full_shape)
    qkv_state = adam_update(w_qkv, sums[0], qkv_mom, qkv_sec, 0.05)
    out_state = adam_update(w_out, sums[1], out_mom, out_sec, 0.3)
    in_state = adam_update(w_in, sums[2], in_mom, in_sec, 0.05)
    back_state = adam_update(w_back, sums[3], back_mom, back_sec, 0.025)
    norm_state = adam_update(norms, sums[4], norm_mom, norm_sec, 0.1)
    return (x_out, d_out, x_grad, qkv_state[0], qkv_state[1], qkv_state[2], out_state[0], out_state[1], out_state[2], in_state[0], in_state[1], in_state[2], back_state[0], back_state[1], back_state[2], norm_state[0], norm_state[1], norm_state[2])
```

```python
import functools

import jax
import jax.numpy as jnp
from jax import lax
from jax.experimental import pallas as pl
from jax.experimental.pallas import tpu as pltpu
from jax.sharding import PartitionSpec as P

STEP = 5
HD = 64
PAIR = 2 * HD
BLOCK = 256
CHUNK = 512
VMEM = 60 * 1024 * 1024

norm_eps = 1e-05
beta_first = 0.5
beta_second = 0.5
adam_eps = 1e-08
decay_rate = 0.01

FAR = 2.0**40
BITS = 7
EXTRA = 16
HEADS = 8

bf16 = jnp.bfloat16
f32 = jnp.float32


def dot_nn(a, b):
    return lax.dot_general(a, b, (((1,), (0,)), ((), ())), preferred_element_type=f32)


def dot_nt(a, b):
    return lax.dot_general(a, b, (((1,), (1,)), ((), ())), preferred_element_type=f32)


def dot_tn(a, b):
    return lax.dot_general(a, b, (((0,), (0,)), ((), ())), preferred_element_type=f32)


def params(**kw):
    return pltpu.CompilerParams(vmem_limit_bytes=VMEM, **kw)


def split_three(value):
    high = value.astype(bf16).astype(f32)
    rest = value - high
    middle = rest.astype(bf16).astype(f32)
    return high, middle, (rest - middle).astype(bf16).astype(f32)


def document_codes(segments):
    lane = jnp.arange(PAIR) % HD
    bit = (segments[..., None] >> (lane % BITS)) & 1
    low, high = lane < BITS, (lane >= BITS) & (lane < 2 * BITS)
    query = jnp.where(low, bit, jnp.where(high, 1 - bit, 0)).astype(bf16)
    key = jnp.where(low, 1 - bit, jnp.where(high, bit, 0)).astype(f32) * -FAR
    return query, key.astype(bf16)


def first_half(shape, axis):
    return lax.broadcasted_iota(jnp.int32, shape, axis) < HD


def head_lanes(head):
    lane = lax.broadcasted_iota(jnp.int32, (1, PAIR), 1) % HD
    mine = (lane == EXTRA + head) | (lane == EXTRA + HEADS + head) | (lane == EXTRA + 2 * HEADS + head)
    return mine.astype(f32).astype(bf16)


def attend_forward_kernel(x_ref, w_ref, qc_ref, kc_ref, q_ref, k_ref, v_ref, a_ref, mix_ref, lse_ref):
    length, width = x_ref.shape[1], x_ref.shape[2]
    x = x_ref[0]
    q = dot_nn(x, w_ref[:, 0:width]).astype(bf16)
    q_ref[0] = q * jnp.asarray(HD**-0.5, bf16)
    k_ref[0] = dot_nn(x, w_ref[:, width : 2 * width]).astype(bf16)
    v_ref[0] = dot_nn(x, w_ref[:, 2 * width : 3 * width]).astype(bf16)
    block = min(BLOCK, length)
    heads = width // HD

    @pl.loop(0, width // PAIR)
    def _(pair):
        lanes = pl.ds(pl.multiple_of(pair * PAIR, PAIR), PAIR)
        q_pair, k_pair, v_pair = q_ref[0, :, lanes], k_ref[0, :, lanes], v_ref[0, :, lanes]
        q_code, k_code = qc_ref[0], kc_ref[0]
        v_turned = v_pair.T
        one = jnp.ones_like(v_turned)
        lane_half = first_half((length, PAIR), 1)
        row_half = first_half((PAIR, length), 0)
        out_half = first_half((PAIR, block), 0)
        causal = lax.broadcasted_iota(jnp.int32, (block, block), 0) <= lax.broadcasted_iota(
            jnp.int32, (block, block), 1
        )
        parts = []
        for odd in (0, 1):
            if odd:
                qa, ka = jnp.where(lane_half, q_code, q_pair), jnp.where(lane_half, k_code, k_pair)
                va = jnp.where(row_half, one, v_turned)
            else:
                qa, ka = jnp.where(lane_half, q_pair, q_code), jnp.where(lane_half, k_pair, k_code)
                va = jnp.where(row_half, v_turned, one)
            outs, logs = [], []
            for start in range(0, length, block):
                stop = start + block
                scores = dot_nt(ka[:stop], qa[start:stop])
                last = jnp.where(causal, scores[start:], -FAR)
                scores = jnp.concatenate([scores[:start], last], axis=0) if start else last
                top = jnp.max(scores, axis=0, keepdims=True)
                weights = jnp.exp(scores - top).astype(bf16)
                out = dot_nn(va[:, :stop], weights)
                total = out[0:1] if odd else out[HD : HD + 1]
                outs.append(out * (1.0 / total))
                logs.append(top + jnp.log(total))
            lse_ref[pl.ds(2 * pair + odd, 1), :] = jnp.concatenate(logs, axis=1)
            parts.append(outs)
        for at, (even, odd) in enumerate(zip(*parts)):
            mixed = jnp.where(out_half, even, odd)
            mix_ref[0, at * block : (at + 1) * block, lanes] = mixed.T.astype(bf16)

    high, middle, low = split_three(-lse_ref[...])
    edge = jnp.zeros((EXTRA, length), f32)
    tail = jnp.zeros((HD - EXTRA - 3 * heads, length), f32)
    rows = jnp.concatenate([edge, high, middle, low, tail], axis=0)
    a_ref[0] = (jnp.concatenate([rows, rows], axis=0).T + qc_ref[0].astype(f32)).astype(bf16)


def attend_forward(x, w, q_code, k_code):
    count, length, width = x.shape
    whole = lambda s: (0, 0)
    row = lambda s: (s, 0, 0)
    wide, narrow = pl.BlockSpec((1, length, width), row), pl.BlockSpec((1, length, PAIR), row)
    shape = jax.ShapeDtypeStruct((count, length, width), bf16)
    return pl.pallas_call(
        attend_forward_kernel,
        grid=(count,),
        in_specs=[wide, pl.BlockSpec(w.shape, whole), narrow, narrow],
        out_specs=[wide, wide, wide, narrow, wide],
        out_shape=[shape, shape, shape, jax.ShapeDtypeStruct((count, length, PAIR), bf16), shape],
        scratch_shapes=[pltpu.VMEM((width // HD, length), f32)],
        compiler_params=params(),
        name="attend_forward",
    )(x, w, q_code, k_code)


def attend_backward_kernel(
    x_ref, w_ref, kc_ref, q_ref, k_ref, v_ref, a_ref, mix_ref, go_ref, dx_ref, dw_ref, grads, delta_ref, dq_ref
):
    length, width = x_ref.shape[1], x_ref.shape[2]
    block = min(BLOCK, length)

    @pl.when(pl.program_id(0) == 0)
    def _():
        dw_ref[...] = jnp.zeros_like(dw_ref)

    product = go_ref[0].astype(f32) * mix_ref[0].astype(f32)
    high = product.astype(bf16)
    low = (product - high.astype(f32)).astype(bf16)
    lane = lax.broadcasted_iota(jnp.int32, (width, PAIR), 1) % HD
    head = lax.broadcasted_iota(jnp.int32, (width, PAIR), 0) // HD
    third = lane - EXTRA - head
    picks = ((third == 0) | (third == HEADS) | (third == 2 * HEADS)).astype(f32).astype(bf16)
    delta = -(dot_nn(high, picks) + dot_nn(low, picks))
    high, middle, low = split_three(delta)
    lane = lax.broadcasted_iota(jnp.int32, (length, PAIR), 1) % HD
    delta_ref[...] = jnp.where(
        lane < EXTRA + HEADS, high, jnp.where(lane < EXTRA + 2 * HEADS, middle, low)
    ).astype(bf16)

    @pl.loop(0, width // PAIR)
    def _(pair):
        lanes = pl.ds(pl.multiple_of(pair * PAIR, PAIR), PAIR)
        q_pair, k_pair, v_pair, go_pair = (r[0, :, lanes] for r in (q_ref, k_ref, v_ref, go_ref))
        a, k_code, minus = a_ref[0], kc_ref[0], delta_ref[...]
        q_turned, go_turned = q_pair.T, go_pair.T
        lane_half = first_half((length, PAIR), 1)
        row_half = first_half((PAIR, block), 0)
        causal = lax.broadcasted_iota(jnp.int32, (block, block), 0) >= lax.broadcasted_iota(
            jnp.int32, (block, block), 1
        )
        dk, dv = [], []
        for odd in (0, 1):
            mine = head_lanes(2 * pair + odd)
            sides = ((q_pair, a), (k_pair, k_code + mine), (v_pair, jnp.broadcast_to(mine, v_pair.shape)), (go_pair, minus))
            qa, ka, va, ga = (
                jnp.where(lane_half, other, own) if odd else jnp.where(lane_half, own, other) for own, other in sides
            )
            for at, start in enumerate(range(0, length, block)):
                stop = start + block
                scores = dot_nt(qa[start:], ka[start:stop])
                first = jnp.where(causal, scores[:block], -FAR)
                scores = jnp.concatenate([first, scores[block:]], axis=0) if stop < length else first
                probs = jnp.exp(scores)
                dscores = (probs * dot_nt(ga[start:], va[start:stop])).astype(bf16)
                dv_at = dot_nn(go_turned[:, start:], probs.astype(bf16))
                dk_at = dot_nn(q_turned[:, start:], dscores)
                dq_at = dot_nn(dscores, k_pair[start:stop])
                if at:
                    dq_ref[odd, start:, :] += dq_at
                else:
                    dq_ref[odd] = dq_at
                if odd:
                    dv[at] = jnp.where(row_half, dv[at], dv_at)
                    dk[at] = jnp.where(row_half, dk[at], dk_at)
                else:
                    dv.append(dv_at)
                    dk.append(dk_at)
        dq = jnp.where(lane_half, dq_ref[0], dq_ref[1]) * HD**-0.5
        grads[:, lanes] = dq.astype(bf16)
        k_lanes = pl.ds(pl.multiple_of(width + pair * PAIR, PAIR), PAIR)
        v_lanes = pl.ds(pl.multiple_of(2 * width + pair * PAIR, PAIR), PAIR)
        for at, start in enumerate(range(0, length, block)):
            grads[start : start + block, k_lanes] = dk[at].T.astype(bf16)
            grads[start : start + block, v_lanes] = dv[at].T.astype(bf16)

    dx_ref[0] = dot_nt(grads[...], w_ref[...]).astype(bf16)
    dw_ref[...] += dot_tn(x_ref[0], grads[...])


def attend_backward(x, w, k_code, q, k, v, a, mix, go):
    count, length, width = x.shape
    whole = lambda s: (0, 0)
    row = lambda s: (s, 0, 0)
    wide, narrow = pl.BlockSpec((1, length, width), row), pl.BlockSpec((1, length, PAIR), row)
    return pl.pallas_call(
        attend_backward_kernel,
        grid=(count,),
        in_specs=[wide, pl.BlockSpec(w.shape, whole), narrow, wide, wide, wide, narrow, wide, wide],
        out_specs=[wide, pl.BlockSpec(w.shape, whole)],
        out_shape=[jax.ShapeDtypeStruct((count, length, width), bf16), jax.ShapeDtypeStruct(w.shape, f32)],
        scratch_shapes=[
            pltpu.VMEM((length, 3 * width), bf16),
            pltpu.VMEM((length, PAIR), bf16),
            pltpu.VMEM((2, length, PAIR), f32),
        ],
        compiler_params=params(),
        name="attend_backward",
    )(x, w, k_code, q, k, v, a, mix, go)


def normalize(rows):
    center = rows - jnp.mean(rows, axis=-1, keepdims=True)
    rstd = lax.rsqrt(jnp.mean(center * center, axis=-1, keepdims=True) + norm_eps)
    return center * rstd, rstd


def normalize_back(grad, xhat, rstd, gain):
    scaled = grad * gain
    return rstd * (
        scaled - jnp.mean(scaled, axis=-1, keepdims=True) - xhat * jnp.mean(scaled * xhat, axis=-1, keepdims=True)
    )


def token_kernel(n_prev, *refs):
    ids_ref, x_ref, d_ref, cx_ref, cd_ref, mix_ref, out_ref, in_ref, back_ref, norm_ref = refs[:10]
    xo_ref, do_ref, gr_ref, act_ref, gh_ref, xb_ref, gf_ref, gb_ref, mo_ref, gm_ref, ng_ref, slope = refs[10 + n_prev :]
    hidden = in_ref.shape[1]
    chunk = min(CHUNK, hidden)

    @pl.when(pl.program_id(0) == 0)
    def _():
        ng_ref[...] = jnp.zeros_like(ng_ref)

    g1, b1, g2, b2 = (norm_ref[i : i + 1] for i in range(4))
    mix = mix_ref[0]
    mo_ref[0] = mix
    attended = dot_nt(mix, out_ref[...])
    xhat1, rstd1 = normalize(x_ref[0].astype(f32) + attended)
    x_one = xhat1 * g1 + b1
    xb = x_one.astype(bf16)
    xb_ref[0] = xb
    feed = None
    for at in range(0, hidden, chunk):
        cols = slice(at, at + chunk)
        h = dot_nn(xb, in_ref[:, cols])
        cdf = 0.5 * lax.erf(h * 0.7071067811865476) + 0.5
        active = (h * cdf).astype(bf16)
        act_ref[0, :, cols] = active
        slope[:, cols] = cdf + h * (jnp.exp(-0.5 * (h * h)) * 0.3989422804014327)
        part = dot_nt(active, back_ref[:, cols])
        feed = part if feed is None else feed + part
    xhat2, rstd2 = normalize(x_one + feed)
    xo_ref[0] = (xhat2 * g2 + b2).astype(bf16)
    do_ref[0] = (d_ref[0].astype(f32) + attended + feed).astype(bf16)
    cx, cd = cx_ref[0].astype(f32), cd_ref[0].astype(f32)
    grad_r2 = normalize_back(cx, xhat2, rstd2, g2)
    dg2, db2 = jnp.sum(cx * xhat2, axis=0, keepdims=True), jnp.sum(cx, axis=0, keepdims=True)
    gf = (grad_r2 + cd).astype(bf16)
    gf_ref[0] = gf
    grad_x1 = grad_r2
    for at in range(0, hidden, chunk):
        cols = slice(at, at + chunk)
        gh = (dot_nn(gf, back_ref[:, cols]) * slope[:, cols]).astype(bf16)
        gh_ref[0, :, cols] = gh
        grad_x1 = grad_x1 + dot_nt(gh, in_ref[:, cols])
    grad_r1 = normalize_back(grad_x1, xhat1, rstd1, g1)
    gr_ref[0] = grad_r1
    dg1, db1 = jnp.sum(grad_x1 * xhat1, axis=0, keepdims=True), jnp.sum(grad_x1, axis=0, keepdims=True)
    ng_ref[...] += jnp.concatenate([dg1, db1, dg2, db2, jnp.zeros((4, dg1.shape[1]), f32)], axis=0)
    gb = (grad_r1 + cd).astype(bf16)
    gb_ref[0] = gb
    gm_ref[0] = dot_nn(gb, out_ref[...]).astype(bf16)


def token_block(ids, first, mix, x, d, cot_x, cot_d, out_turned, w_in, back_turned, norms, prev):
    count, rows, width = mix.shape
    total, hidden = x.shape[0], w_in.shape[1]
    there = lambda s, ids: (ids[s], 0, 0)
    here = lambda s, ids: (s, 0, 0)
    after = lambda s, ids: (s + first, 0, 0)
    whole = lambda s, ids: (0, 0)
    one = (1, rows, width)
    full = lambda n, dtype: jax.ShapeDtypeStruct((total, rows, n), dtype)
    shapes = [
        full(width, bf16),
        full(width, bf16),
        full(width, f32),
        full(hidden, bf16),
        full(hidden, bf16),
        full(width, bf16),
        full(width, bf16),
        full(width, bf16),
        full(width, bf16),
    ]
    specs = [pl.BlockSpec(one, there)] * 3
    specs += [pl.BlockSpec((1, rows, hidden), after)] * 2 + [pl.BlockSpec(one, after)] * 4
    weights = [pl.BlockSpec(w.shape, whole) for w in (out_turned, w_in, back_turned, norms)]
    out = pl.pallas_call(
        functools.partial(token_kernel, len(prev)),
        grid_spec=pltpu.PrefetchScalarGridSpec(
            num_scalar_prefetch=1,
            grid=(count,),
            in_specs=[pl.BlockSpec(one, there)] * 4
            + [pl.BlockSpec(one, here)]
            + weights
            + [pl.BlockSpec(memory_space=pl.ANY)] * len(prev),
            out_specs=specs + [pl.BlockSpec(one, here), pl.BlockSpec((8, width), whole)],
            scratch_shapes=[pltpu.VMEM((rows, hidden), f32)],
        ),
        out_shape=shapes
        + [jax.ShapeDtypeStruct((count, rows, width), bf16), jax.ShapeDtypeStruct((8, width), f32)],
        input_output_aliases={10 + i: i for i in range(len(prev))},
        compiler_params=params(),
        name="token_block",
    )(ids, x, d, cot_x, cot_d, mix, out_turned, w_in, back_turned, norms, *prev)
    return out[:9], out[9], out[10]


def weight_kernel(act_ref, gh_ref, xb_ref, gf_ref, gb_ref, mo_ref, out_ref, in_ref, back_ref):
    @pl.when(pl.program_id(0) == 0)
    def _():
        out_ref[...] = jnp.zeros_like(out_ref)
        in_ref[...] = jnp.zeros_like(in_ref)
        back_ref[...] = jnp.zeros_like(back_ref)

    back_ref[...] += dot_tn(gf_ref[0], act_ref[0])
    in_ref[...] += dot_tn(xb_ref[0], gh_ref[0])
    out_ref[...] += dot_tn(gb_ref[0], mo_ref[0])


def weight_gradients(act, gh, xb, gf, gb, mo):
    total, rows, hidden = act.shape
    width = xb.shape[2]
    row = lambda s: (s, 0, 0)
    whole = lambda s: (0, 0)
    wide, narrow = pl.BlockSpec((1, rows, hidden), row), pl.BlockSpec((1, rows, width), row)
    shapes = [(width, width), (width, hidden), (width, hidden)]
    return pl.pallas_call(
        weight_kernel,
        grid=(total,),
        in_specs=[wide, wide, narrow, narrow, narrow, narrow],
        out_specs=[pl.BlockSpec(s, whole) for s in shapes],
        out_shape=[jax.ShapeDtypeStruct(s, f32) for s in shapes],
        compiler_params=params(),
        name="weight_gradients",
    )(act, gh, xb, gf, gb, mo)


def adam_update(weight, grad, mom, sec, rate):
    mom_new = beta_first * mom + (1.0 - beta_first) * grad
    sec_new = beta_second * sec + (1.0 - beta_second) * grad * grad
    scaled = (
        mom_new
        / (1.0 - beta_first**STEP)
        / (jnp.sqrt(sec_new / (1.0 - beta_second**STEP)) + adam_eps)
    )
    return (mom_new, sec_new, weight - rate * (scaled + decay_rate * weight))


def swap(value):
    return lax.ppermute(value, "mp", [(0, 1), (1, 0)])


def on_device(
    x_in,
    d_in,
    segments,
    cot_x,
    cot_d,
    w_qkv,
    w_out,
    w_in,
    w_back,
    norms,
    qkv_mom,
    qkv_sec,
    out_mom,
    out_sec,
    in_mom,
    in_sec,
    back_mom,
    back_sec,
    norm_mom,
    norm_sec,
):
    parts, owners = lax.axis_size("mp"), lax.axis_size("dp")
    me = lax.axis_index("mp")
    total, rows, width = x_in.shape
    mine = total // parts
    length = rows * parts
    own_rows = w_qkv.shape[0]
    here = lambda v, start, count: lax.dynamic_slice_in_dim(v, start, count, axis=0)

    def gather(shard):
        got = lax.all_gather(shard.astype(bf16), ("dp", "mp"), axis=0)
        return got.reshape((owners, parts) + shard.shape)

    qkv = gather(w_qkv).transpose(0, 2, 3, 1, 4).reshape(width, 3 * width)
    n_out, n_in, n_back = w_out.shape[0], w_in.shape[1], w_back.shape[0]
    rest = gather(jnp.concatenate([w_out.T, w_in, w_back.T], axis=1)).transpose(0, 2, 1, 3)
    rest = rest.reshape(width, parts, n_out + n_in + n_back)
    out_turned = rest[:, :, :n_out].reshape(width, parts * n_out)
    in_whole = rest[:, :, n_out : n_out + n_in].reshape(width, parts * n_in)
    back_turned = rest[:, :, n_out + n_in :].reshape(width, parts * n_back)
    gain_rows = lax.all_gather(norms.astype(bf16), "dp", axis=1, tiled=True).astype(f32)

    q_code, k_code = document_codes(here(segments, me * mine, mine))

    def tokens(ids, first, mix, prev):
        return token_block(
            ids, first, mix, x_in, d_in, cot_x, cot_d, out_turned, in_whole, back_turned, gain_rows, prev
        )

    if parts == 2:
        other = 1 - me
        step = max(mine // 2, 1)
        chunks = list(range(0, mine, step))

        def join(own, got):
            return jnp.where(me == 0, jnp.concatenate([own, got], axis=1), jnp.concatenate([got, own], axis=1))

        forward = []
        for at in chunks:
            got = swap(here(x_in, other * mine + at, step))
            x_whole = join(here(x_in, me * mine + at, step), got)
            q, k, v, a, mix = attend_forward(x_whole, qkv, q_code[at : at + step], k_code[at : at + step])
            halves = mix.reshape(step, parts, rows, width)
            pick = lambda i, halves=halves: lax.dynamic_index_in_dim(halves, i, axis=1, keepdims=False)
            forward.append((x_whole, q, k, v, a, mix, pick(me), swap(pick(other))))
        spread = jnp.arange(mine, dtype=jnp.int32)
        own_mix = jnp.concatenate([f[6] for f in forward], axis=0)
        prev, own_gm, norm_grad = tokens(me * mine + spread, 0, own_mix, ())
        got_gm = []
        for i, at in enumerate(chunks):
            prev, gm, ng = tokens(other * mine + at + spread[:step], mine + at, forward[i][7], prev)
            norm_grad = norm_grad + ng
            got_gm.append(swap(gm))
        x_out, d_out, grad_r1, act, gh, xb, gf, gb, mo = prev
        token_grads = weight_gradients(act, gh, xb, gf, gb, mo)
        qkv_grad, own_dx, got_dx = 0.0, [], []
        for i, at in enumerate(chunks):
            x_whole, q, k, v, a, mix = forward[i][:6]
            go = join(own_gm[at : at + step], got_gm[i])
            dx, dw = attend_backward(x_whole, qkv, k_code[at : at + step], q, k, v, a, mix, go)
            halves = dx.reshape(step, parts, rows, width)
            pick = lambda i, halves=halves: lax.dynamic_index_in_dim(halves, i, axis=1, keepdims=False)
            own_dx.append(pick(me))
            got_dx.append(swap(pick(other)))
            qkv_grad = qkv_grad + dw
        own_dx, got_dx = jnp.concatenate(own_dx, axis=0), jnp.concatenate(got_dx, axis=0)
        dx = jnp.where(
            me == 0, jnp.concatenate([own_dx, got_dx], axis=0), jnp.concatenate([got_dx, own_dx], axis=0)
        )
    else:

        def to_sequences(v):
            got = lax.all_to_all(v.reshape(parts, mine, rows, width), "mp", 0, 0)
            return got.transpose(1, 0, 2, 3).reshape(mine, length, width)

        def to_positions(v):
            sent = v.reshape(mine, parts, rows, width).transpose(1, 0, 2, 3)
            return lax.all_to_all(sent, "mp", 0, 0).reshape(total, rows, width)

        x_whole = to_sequences(x_in)
        q, k, v, a, mix = attend_forward(x_whole, qkv, q_code, k_code)
        prev, gm, norm_grad = tokens(jnp.arange(total, dtype=jnp.int32), 0, to_positions(mix), ())
        x_out, d_out, grad_r1, act, gh, xb, gf, gb, mo = prev
        token_grads = weight_gradients(act, gh, xb, gf, gb, mo)
        dx, qkv_grad = attend_backward(x_whole, qkv, k_code, q, k, v, a, mix, to_sequences(gm))
        dx = to_positions(dx)
    x_grad = grad_r1 + dx.astype(f32)

    def scatter(value):
        n = value.shape[1] // parts
        blocks = value.astype(bf16).reshape(width, parts, n)
        got = lax.psum_scatter(blocks, "dp", scatter_dimension=0, tiled=True)
        return lax.psum_scatter(got, "mp", scatter_dimension=1, tiled=True)[:, 0].astype(f32)

    out_g, in_g, back_g = token_grads
    n_all = n_out + n_in + n_back
    packed = jnp.concatenate(
        [
            out_g.reshape(width, parts, n_out),
            in_g.reshape(width, parts, n_in),
            back_g.reshape(width, parts, n_back),
        ],
        axis=2,
    ).reshape(width, parts * n_all)
    got = scatter(packed)
    out_g, in_g, back_g = got[:, :n_out].T, got[:, n_out : n_out + n_in], got[:, n_out + n_in :].T
    qkv_n = w_qkv.shape[2]
    qkv_packed = qkv_grad.reshape(width, 3, parts, qkv_n).transpose(0, 2, 1, 3).reshape(width, parts * 3 * qkv_n)
    qkv_g = scatter(qkv_packed).reshape(own_rows, 3, qkv_n)
    norm_g = lax.psum_scatter(
        lax.psum(norm_grad[:4], "mp"), "dp", scatter_dimension=1, tiled=True
    )
    qkv_state = adam_update(w_qkv, qkv_g, qkv_mom, qkv_sec, 0.05)
    out_state = adam_update(w_out, out_g, out_mom, out_sec, 0.3)
    in_state = adam_update(w_in, in_g, in_mom, in_sec, 0.05)
    back_state = adam_update(w_back, back_g, back_mom, back_sec, 0.025)
    norm_state = adam_update(norms, norm_g, norm_mom, norm_sec, 0.1)
    return (x_out, d_out, x_grad, *qkv_state, *out_state, *in_state, *back_state, *norm_state)


def solution(mesh):
    stream = P("dp", "mp", None)
    weights = (P("dp", None, "mp"), P("mp", "dp"), P("dp", "mp"), P("mp", "dp"), P(None, "dp"))
    states = tuple(spec for spec in weights for _ in range(2))
    news = tuple(spec for spec in weights for _ in range(3))
    return jax.shard_map(
        on_device,
        mesh=mesh,
        in_specs=(stream, stream, P("dp", None), stream, stream) + weights + states,
        out_specs=(stream, stream, stream) + news,
        check_vma=False,
    )
```

```python
import functools

import jax
import jax.numpy as jnp
from jax import lax
from jax.experimental import pallas as pl
from jax.experimental.pallas import tpu as pltpu
from jax.sharding import PartitionSpec as P

STEP = 5
HD = 64
PAIR = 2 * HD
BLOCK = 256
CHUNK = 512
VMEM = 60 * 1024 * 1024

norm_eps = 1e-05
beta_first = 0.5
beta_second = 0.5
adam_eps = 1e-08
decay_rate = 0.01

FAR = 2.0**40
BITS = 7
EXTRA = 16
HEADS = 8

bf16 = jnp.bfloat16
f32 = jnp.float32


def dot_nn(a, b):
    return lax.dot_general(a, b, (((1,), (0,)), ((), ())), preferred_element_type=f32)


def dot_nt(a, b):
    return lax.dot_general(a, b, (((1,), (1,)), ((), ())), preferred_element_type=f32)


def dot_tn(a, b):
    return lax.dot_general(a, b, (((0,), (0,)), ((), ())), preferred_element_type=f32)


def params(**kw):
    return pltpu.CompilerParams(vmem_limit_bytes=VMEM, **kw)


def work(products, moved, exps=0):
    return pl.CostEstimate(flops=int(2 * products), bytes_accessed=int(moved), transcendentals=int(exps))


def split_three(value):
    high = value.astype(bf16).astype(f32)
    rest = value - high
    middle = rest.astype(bf16).astype(f32)
    return high, middle, (rest - middle).astype(bf16).astype(f32)


def document_codes(segments):
    lane = jnp.arange(PAIR) % HD
    bit = (segments[..., None] >> (lane % BITS)) & 1
    low, high = lane < BITS, (lane >= BITS) & (lane < 2 * BITS)
    query = jnp.where(low, bit, jnp.where(high, 1 - bit, 0)).astype(bf16)
    key = jnp.where(low, 1 - bit, jnp.where(high, bit, 0)).astype(f32) * -FAR
    return query, key.astype(bf16)


def first_half(shape, axis):
    return lax.broadcasted_iota(jnp.int32, shape, axis) < HD


def head_lanes(head):
    lane = lax.broadcasted_iota(jnp.int32, (1, PAIR), 1) % HD
    mine = (lane == EXTRA + head) | (lane == EXTRA + HEADS + head) | (lane == EXTRA + 2 * HEADS + head)
    return mine.astype(f32).astype(bf16)


def gather_pieces(order_ref, refs, held):
    if len(refs) == 1:
        return refs[0]
    rows = refs[0].shape[1]
    for i, ref in enumerate(refs):
        held[0, pl.ds(pl.multiple_of(order_ref[i] * rows, rows), rows), :] = ref[0]
    return held


def spread_pieces(order_ref, refs, value_ref):
    rows = refs[0].shape[1]
    for i, ref in enumerate(refs):
        ref[0] = value_ref[0, pl.ds(pl.multiple_of(order_ref[i] * rows, rows), rows), :]


def attend_forward_kernel(n, begun, *refs):
    order_ref, ids_ref = refs[:2]
    w_ref, qc_ref, kc_ref = refs[2 + n : 5 + n]
    if begun:
        refs = refs[: 5 + n] + refs[6 + n :]
    q_ref, k_ref, v_ref, a_ref = refs[5 + n : 9 + n]
    mix_refs = refs[9 + n : 9 + 2 * n]
    lse_ref, x_held, mix_ref = refs[9 + 2 * n :]
    x_ref = gather_pieces(order_ref, refs[2 : 2 + n], x_held)
    length, width = q_ref.shape[1], q_ref.shape[2]
    x = x_ref[0]
    q = dot_nn(x, w_ref[:, 0:width]).astype(bf16)
    q_ref[0] = q * jnp.asarray(HD**-0.5, bf16)
    k_ref[0] = dot_nn(x, w_ref[:, width : 2 * width]).astype(bf16)
    v_ref[0] = dot_nn(x, w_ref[:, 2 * width : 3 * width]).astype(bf16)
    block = min(BLOCK, length)
    heads = width // HD

    @pl.loop(0, width // PAIR)
    def _(pair):
        lanes = pl.ds(pl.multiple_of(pair * PAIR, PAIR), PAIR)
        q_pair, k_pair, v_pair = q_ref[0, :, lanes], k_ref[0, :, lanes], v_ref[0, :, lanes]
        q_code, k_code = qc_ref[0], kc_ref[0]
        v_turned = v_pair.T
        one = jnp.ones_like(v_turned)
        lane_half = first_half((length, PAIR), 1)
        row_half = first_half((PAIR, length), 0)
        out_half = first_half((PAIR, block), 0)
        causal = lax.broadcasted_iota(jnp.int32, (block, block), 0) <= lax.broadcasted_iota(
            jnp.int32, (block, block), 1
        )
        parts = []
        for odd in (0, 1):
            if odd:
                qa, ka = jnp.where(lane_half, q_code, q_pair), jnp.where(lane_half, k_code, k_pair)
                va = jnp.where(row_half, one, v_turned)
            else:
                qa, ka = jnp.where(lane_half, q_pair, q_code), jnp.where(lane_half, k_pair, k_code)
                va = jnp.where(row_half, v_turned, one)
            outs, logs = [], []
            for start in range(0, length, block):
                stop = start + block
                scores = dot_nt(ka[:stop], qa[start:stop])
                last = jnp.where(causal, scores[start:], -FAR)
                scores = jnp.concatenate([scores[:start], last], axis=0) if start else last
                top = jnp.max(scores, axis=0, keepdims=True)
                weights = jnp.exp(scores - top).astype(bf16)
                out = dot_nn(va[:, :stop], weights)
                total = out[0:1] if odd else out[HD : HD + 1]
                outs.append(out * (1.0 / total))
                logs.append(top + jnp.log(total))
            lse_ref[pl.ds(2 * pair + odd, 1), :] = jnp.concatenate(logs, axis=1)
            parts.append(outs)
        for at, (even, odd) in enumerate(zip(*parts)):
            mixed = jnp.where(out_half, even, odd)
            mix_ref[0, at * block : (at + 1) * block, lanes] = mixed.T.astype(bf16)

    spread_pieces(order_ref, mix_refs, mix_ref)
    high, middle, low = split_three(-lse_ref[...])
    edge = jnp.zeros((EXTRA, length), f32)
    tail = jnp.zeros((HD - EXTRA - 3 * heads, length), f32)
    rows = jnp.concatenate([edge, high, middle, low, tail], axis=0)
    a_ref[0] = (jnp.concatenate([rows, rows], axis=0).T + qc_ref[0].astype(f32)).astype(bf16)


def piece_specs(pieces, width):
    maps = [lambda s, order, ids: (ids[s], 0, 0)] + [lambda s, order, ids: (s, 0, 0)] * (len(pieces) - 1)
    return [pl.BlockSpec((1, p.shape[1], width), m) for p, m in zip(pieces, maps)]


def attend_forward(order, ids, at, total, pieces, w, q_code, k_code, before):
    count, length = ids.shape[0], q_code.shape[1]
    width, n = pieces[0].shape[2], len(pieces)
    whole = lambda s, order, ids: (0, 0)
    row = lambda s, order, ids: (s, 0, 0)
    after = lambda s, order, ids: (s + at, 0, 0)
    wide, narrow = pl.BlockSpec((1, length, width), row), pl.BlockSpec((1, length, PAIR), row)
    code = pl.BlockSpec((1, length, PAIR), after)
    parts = [pl.BlockSpec((1, length // n, width), m) for m in (after, row)[:n]]
    full = lambda count, rows, cols: jax.ShapeDtypeStruct((count, rows, cols), bf16)
    args = [order, ids, *pieces, w, q_code, k_code] + ([] if before is None else [before])
    out = pl.pallas_call(
        functools.partial(attend_forward_kernel, n, before is not None),
        grid_spec=pltpu.PrefetchScalarGridSpec(
            num_scalar_prefetch=2,
            grid=(count,),
            in_specs=piece_specs(pieces, width)
            + [pl.BlockSpec(w.shape, whole), code, code]
            + ([] if before is None else [pl.BlockSpec(memory_space=pl.ANY)]),
            out_specs=[wide, wide, wide, narrow] + parts,
            scratch_shapes=[
                pltpu.VMEM((width // HD, length), f32),
                pltpu.VMEM((1, length, width), bf16),
                pltpu.VMEM((1, length, width), bf16),
            ],
        ),
        out_shape=[full(count, length, width)] * 3
        + [full(count, length, PAIR)]
        + [full(total, length // n, width), full(count, length // n, width)][:n],
        input_output_aliases={} if before is None else {len(args) - 1: 4},
        cost_estimate=work(count * length * width * (3 * width + 8 * length), count * length * width * 12),
        compiler_params=params(),
        name="attend_forward",
    )(*args)
    return out[:4], out[4:]


def attend_backward_kernel(n, begun, last, *refs):
    order_ref, ids_ref = refs[:2]
    x_refs, mix_refs, go_refs = (refs[2 + i * n : 2 + (i + 1) * n] for i in range(3))
    w_ref, kc_ref, q_ref, k_ref, v_ref, a_ref = refs[2 + 3 * n : 8 + 3 * n]
    refs = refs[8 + 3 * n :]
    if n == 2:
        gr_ref, refs = refs[0], refs[1:]
    if begun:
        before_ref, refs = refs[0], refs[1:]
    dx_refs, refs = refs[:n], refs[n:]
    dw_ref, grads, delta_ref, dq_ref, x_held, mix_held, go_held, dw_sum, dx_held = refs
    x_ref = gather_pieces(order_ref, x_refs, x_held)
    mix_ref = gather_pieces(order_ref, mix_refs, mix_held)
    go_ref = gather_pieces(order_ref, go_refs, go_held)
    length, width = q_ref.shape[1], q_ref.shape[2]
    block = min(BLOCK, length)

    @pl.when(pl.program_id(0) == 0)
    def _():
        dw_sum[...] = before_ref[...] if begun else jnp.zeros_like(dw_sum)

    product = go_ref[0].astype(f32) * mix_ref[0].astype(f32)
    high = product.astype(bf16)
    low = (product - high.astype(f32)).astype(bf16)
    lane = lax.broadcasted_iota(jnp.int32, (width, PAIR), 1) % HD
    head = lax.broadcasted_iota(jnp.int32, (width, PAIR), 0) // HD
    third = lane - EXTRA - head
    picks = ((third == 0) | (third == HEADS) | (third == 2 * HEADS)).astype(f32).astype(bf16)
    delta = -(dot_nn(high, picks) + dot_nn(low, picks))
    high, middle, low = split_three(delta)
    lane = lax.broadcasted_iota(jnp.int32, (length, PAIR), 1) % HD
    delta_ref[...] = jnp.where(
        lane < EXTRA + HEADS, high, jnp.where(lane < EXTRA + 2 * HEADS, middle, low)
    ).astype(bf16)

    @pl.loop(0, width // PAIR)
    def _(pair):
        lanes = pl.ds(pl.multiple_of(pair * PAIR, PAIR), PAIR)
        q_pair, k_pair, v_pair, go_pair = (r[0, :, lanes] for r in (q_ref, k_ref, v_ref, go_ref))
        a, k_code, minus = a_ref[0], kc_ref[0], delta_ref[...]
        q_turned, go_turned = q_pair.T, go_pair.T
        lane_half = first_half((length, PAIR), 1)
        row_half = first_half((PAIR, block), 0)
        causal = lax.broadcasted_iota(jnp.int32, (block, block), 0) >= lax.broadcasted_iota(
            jnp.int32, (block, block), 1
        )
        dk, dv = [], []
        for odd in (0, 1):
            mine = head_lanes(2 * pair + odd)
            sides = ((q_pair, a), (k_pair, k_code + mine), (v_pair, jnp.broadcast_to(mine, v_pair.shape)), (go_pair, minus))
            qa, ka, va, ga = (
                jnp.where(lane_half, other, own) if odd else jnp.where(lane_half, own, other) for own, other in sides
            )
            for at, start in enumerate(range(0, length, block)):
                stop = start + block
                scores = dot_nt(qa[start:], ka[start:stop])
                first = jnp.where(causal, scores[:block], -FAR)
                scores = jnp.concatenate([first, scores[block:]], axis=0) if stop < length else first
                probs = jnp.exp(scores)
                dscores = (probs * dot_nt(ga[start:], va[start:stop])).astype(bf16)
                dv_at = dot_nn(go_turned[:, start:], probs.astype(bf16))
                dk_at = dot_nn(q_turned[:, start:], dscores)
                dq_at = dot_nn(dscores, k_pair[start:stop])
                if at:
                    dq_ref[odd, start:, :] += dq_at
                else:
                    dq_ref[odd] = dq_at
                if odd:
                    dv[at] = jnp.where(row_half, dv[at], dv_at)
                    dk[at] = jnp.where(row_half, dk[at], dk_at)
                else:
                    dv.append(dv_at)
                    dk.append(dk_at)
        dq = jnp.where(lane_half, dq_ref[0], dq_ref[1]) * HD**-0.5
        grads[:, lanes] = dq.astype(bf16)
        k_lanes = pl.ds(pl.multiple_of(width + pair * PAIR, PAIR), PAIR)
        v_lanes = pl.ds(pl.multiple_of(2 * width + pair * PAIR, PAIR), PAIR)
        for at, start in enumerate(range(0, length, block)):
            grads[start : start + block, k_lanes] = dk[at].T.astype(bf16)
            grads[start : start + block, v_lanes] = dv[at].T.astype(bf16)

    dw_sum[...] += dot_tn(x_ref[0], grads[...])
    dx_held[0] = dot_nt(grads[...], w_ref[...])
    if n == 2:
        rows = length // n
        pick = lambda i: dx_held[0, pl.ds(pl.multiple_of(order_ref[i] * rows, rows), rows), :]
        dx_refs[0][0] = gr_ref[0] + pick(0)
        dx_refs[1][0] = pick(1).astype(bf16)
    else:
        dx_refs[0][0] = dx_held[0].astype(bf16)

    @pl.when(pl.program_id(0) == pl.num_programs(0) - 1)
    def _():
        if last:
            owners, parts, rows, cols = dw_ref.shape
            cols //= 3
            for part in range(parts):
                for third in range(3):
                    start = third * width + part * cols
                    block = dw_sum[:, start : start + cols].astype(bf16)
                    dw_ref[:, part, :, third * cols : (third + 1) * cols] = block.reshape(owners, rows, cols)
        else:
            dw_ref[...] = dw_sum[...]


def attend_backward(order, ids, at, x, mix, go, w, k_code, kept, grad_r1, before, last):
    count, length = ids.shape[0], k_code.shape[1]
    width, n = w.shape[0], len(x)
    whole = lambda s, order, ids: (0, 0)
    row = lambda s, order, ids: (s, 0, 0)
    there = lambda s, order, ids: (ids[s], 0, 0)
    wide, narrow = pl.BlockSpec((1, length, width), row), pl.BlockSpec((1, length, PAIR), row)
    weight = pl.BlockSpec(w.shape, whole)
    part = pl.BlockSpec((1, length // n, width), row)
    args = [order, ids, *x, *mix, *go, w, k_code, *kept]
    own = pl.BlockSpec((1, length // n, width), lambda s, order, ids: (s + at, 0, 0))
    code = pl.BlockSpec((1, length, PAIR), lambda s, order, ids: (s + at, 0, 0))
    specs = piece_specs(x, width) + [own, part][:n] * 2 + [weight, code, wide, wide, wide, narrow]
    weight_out, dw_shape = weight, jax.ShapeDtypeStruct(w.shape, f32)
    if last:
        weight_out = pl.BlockSpec(last, lambda s, order, ids: (0, 0, 0, 0))
        dw_shape = jax.ShapeDtypeStruct(last, bf16)
    dx_specs, dx_shapes = [part], [jax.ShapeDtypeStruct((count, length // n, width), bf16)]
    alias = {}
    if n == 2:
        held = pl.BlockSpec((1, length // n, width), there)
        alias[len(args)] = 0
        args.append(grad_r1)
        specs.append(held)
        dx_specs, dx_shapes = [held] + dx_specs, [jax.ShapeDtypeStruct(grad_r1.shape, f32)] + dx_shapes
    if before is not None:
        args.append(before)
        specs.append(weight)
    out = pl.pallas_call(
        functools.partial(attend_backward_kernel, n, before is not None, last),
        grid_spec=pltpu.PrefetchScalarGridSpec(
            num_scalar_prefetch=2,
            grid=(count,),
            in_specs=specs,
            out_specs=dx_specs + [weight_out],
            scratch_shapes=[
                pltpu.VMEM((length, 3 * width), bf16),
                pltpu.VMEM((length, PAIR), bf16),
                pltpu.VMEM((2, length, PAIR), f32),
                pltpu.VMEM((1, length, width), bf16),
                pltpu.VMEM((1, length, width), bf16),
                pltpu.VMEM((1, length, width), bf16),
                pltpu.VMEM(w.shape, f32),
                pltpu.VMEM((1, length, width), f32),
            ],
        ),
        out_shape=dx_shapes + [dw_shape],
        input_output_aliases=alias,
        cost_estimate=work(count * length * width * (6 * width + 16 * length), count * length * width * 20),
        compiler_params=params(),
        name="attend_backward",
    )(*args)
    return out[:n], out[n]


def normalize(rows):
    center = rows - jnp.mean(rows, axis=-1, keepdims=True)
    rstd = lax.rsqrt(jnp.mean(center * center, axis=-1, keepdims=True) + norm_eps)
    return center * rstd, rstd


def normalize_back(grad, xhat, rstd, gain):
    scaled = grad * gain
    return rstd * (
        scaled - jnp.mean(scaled, axis=-1, keepdims=True) - xhat * jnp.mean(scaled * xhat, axis=-1, keepdims=True)
    )


def token_kernel(n_prev, *refs):
    ids_ref, x_ref, d_ref, cx_ref, cd_ref, mix_ref, weights_ref = refs[:7]
    xo_ref, do_ref, gr_ref, act_ref, gh_ref, xb_ref, gf_ref, gb_ref, mo_ref, gm_ref, ng_ref = refs[7 + n_prev : 18 + n_prev]
    slope, in_ref, back_ref, norm_ref, out_ref = refs[18 + n_prev :]
    hidden = in_ref.shape[1]
    chunk = min(CHUNK, hidden)

    @pl.when(pl.program_id(0) == 0)
    def _():
        ng_ref[...] = jnp.zeros_like(ng_ref)
        owners, parts, rows, _ = weights_ref.shape
        for part in range(parts):
            at = 0
            for ref in (in_ref, back_ref, norm_ref, out_ref):
                size = PAIR if ref is norm_ref else ref.shape[1] // parts
                to = 0 if ref is norm_ref else part * size
                block = weights_ref[:, part, :, at : at + size]
                ref[:, to : to + size] = block.reshape(owners * rows, size)
                at += size

    turned = norm_ref[...].astype(f32).T
    g1, b1, g2, b2 = (turned[i : i + 1] for i in range(4))
    mix = mix_ref[0]
    mo_ref[0] = mix
    attended = dot_nt(mix, out_ref[...])
    xhat1, rstd1 = normalize(x_ref[0].astype(f32) + attended)
    x_one = xhat1 * g1 + b1
    xb = x_one.astype(bf16)
    xb_ref[0] = xb
    feed = None
    for at in range(0, hidden, chunk):
        cols = slice(at, at + chunk)
        h = dot_nn(xb, in_ref[:, cols])
        cdf = 0.5 * lax.erf(h * 0.7071067811865476) + 0.5
        active = (h * cdf).astype(bf16)
        act_ref[0, :, cols] = active
        slope[:, cols] = cdf + h * (jnp.exp(-0.5 * (h * h)) * 0.3989422804014327)
        part = dot_nt(active, back_ref[:, cols])
        feed = part if feed is None else feed + part
    xhat2, rstd2 = normalize(x_one + feed)
    xo_ref[0] = (xhat2 * g2 + b2).astype(bf16)
    do_ref[0] = (d_ref[0].astype(f32) + attended + feed).astype(bf16)
    cx, cd = cx_ref[0].astype(f32), cd_ref[0].astype(f32)
    grad_r2 = normalize_back(cx, xhat2, rstd2, g2)
    dg2, db2 = jnp.sum(cx * xhat2, axis=0, keepdims=True), jnp.sum(cx, axis=0, keepdims=True)
    gf = (grad_r2 + cd).astype(bf16)
    gf_ref[0] = gf
    grad_x1 = grad_r2
    for at in range(0, hidden, chunk):
        cols = slice(at, at + chunk)
        gh = (dot_nn(gf, back_ref[:, cols]) * slope[:, cols]).astype(bf16)
        gh_ref[0, :, cols] = gh
        grad_x1 = grad_x1 + dot_nt(gh, in_ref[:, cols])
    grad_r1 = normalize_back(grad_x1, xhat1, rstd1, g1)
    gr_ref[0] = grad_r1
    dg1, db1 = jnp.sum(grad_x1 * xhat1, axis=0, keepdims=True), jnp.sum(grad_x1, axis=0, keepdims=True)
    ng_ref[...] += jnp.concatenate([dg1, db1, dg2, db2, jnp.zeros((4, dg1.shape[1]), f32)], axis=0)
    gb = (grad_r1 + cd).astype(bf16)
    gb_ref[0] = gb
    gm_ref[0] = dot_nn(gb, out_ref[...]).astype(bf16)


def token_block(ids, first, mix, x, d, cot_x, cot_d, weights, hidden, prev):
    count, rows, width = mix.shape
    total = x.shape[0]
    there = lambda s, ids: (ids[s], 0, 0)
    here = lambda s, ids: (s, 0, 0)
    after = lambda s, ids: (s + first, 0, 0)
    whole = lambda s, ids: (0, 0)
    one = (1, rows, width)
    full = lambda n, dtype: jax.ShapeDtypeStruct((total, rows, n), dtype)
    shapes = [
        full(width, bf16),
        full(width, bf16),
        full(width, f32),
        full(hidden, bf16),
        full(hidden, bf16),
        full(width, bf16),
        full(width, bf16),
        full(width, bf16),
        full(width, bf16),
    ]
    specs = [pl.BlockSpec(one, there)] * 3
    specs += [pl.BlockSpec((1, rows, hidden), after)] * 2 + [pl.BlockSpec(one, after)] * 4
    out = pl.pallas_call(
        functools.partial(token_kernel, len(prev)),
        grid_spec=pltpu.PrefetchScalarGridSpec(
            num_scalar_prefetch=1,
            grid=(count,),
            in_specs=[pl.BlockSpec(one, there)] * 4
            + [pl.BlockSpec(one, here)]
            + [pl.BlockSpec(weights.shape, lambda s, ids: (0, 0, 0, 0))]
            + [pl.BlockSpec(memory_space=pl.ANY)] * len(prev),
            out_specs=specs + [pl.BlockSpec(one, here), pl.BlockSpec((8, width), whole)],
            scratch_shapes=[pltpu.VMEM((rows, hidden), f32)]
            + [pltpu.VMEM((width, cols), bf16) for cols in (hidden, hidden, PAIR, width)],
        ),
        out_shape=shapes
        + [jax.ShapeDtypeStruct((count, rows, width), bf16), jax.ShapeDtypeStruct((8, width), f32)],
        input_output_aliases={7 + i: i for i in range(len(prev))},
        cost_estimate=work(count * rows * width * (6 * hidden + 2 * width), count * rows * (40 * width + 4 * hidden)),
        compiler_params=params(),
        name="token_block",
    )(ids, x, d, cot_x, cot_d, mix, weights, *prev)
    return out[:9], out[9], out[10]


def weight_kernel(parts, act_ref, gh_ref, xb_ref, gf_ref, gb_ref, mo_ref, ng_ref, packed_ref, out_ref, in_ref, back_ref):
    @pl.when(pl.program_id(0) == 0)
    def _():
        out_ref[...] = jnp.zeros_like(out_ref)
        in_ref[...] = jnp.zeros_like(in_ref)
        back_ref[...] = jnp.zeros_like(back_ref)

    back_ref[...] += dot_tn(gf_ref[0], act_ref[0])
    in_ref[...] += dot_tn(xb_ref[0], gh_ref[0])
    out_ref[...] += dot_tn(gb_ref[0], mo_ref[0])

    @pl.when(pl.program_id(0) == pl.num_programs(0) - 1)
    def _():
        width, hidden = in_ref.shape
        n_hidden, n_out = hidden // parts, width // parts
        rest = jnp.zeros((PAIR - ng_ref.shape[0], width), f32)
        norms = jnp.concatenate([ng_ref[...], rest], axis=0).T.astype(bf16)
        for part in range(parts):
            cols = slice(part * n_hidden, (part + 1) * n_hidden)
            packed_ref[part, :, :n_hidden] = in_ref[:, cols].astype(bf16)
            packed_ref[part, :, n_hidden : 2 * n_hidden] = back_ref[:, cols].astype(bf16)
            at = 2 * n_hidden
            packed_ref[part, :, at : at + PAIR] = norms
            at += PAIR
            packed_ref[part, :, at : at + n_out] = out_ref[:, part * n_out : (part + 1) * n_out].astype(bf16)


def weight_gradients(parts, act, gh, xb, gf, gb, mo, norm_grad):
    total, rows, hidden = act.shape
    width = xb.shape[2]
    row = lambda s: (s, 0, 0)
    whole = lambda s: (0, 0)
    wide, narrow = pl.BlockSpec((1, rows, hidden), row), pl.BlockSpec((1, rows, width), row)
    n_out = -(-(width // parts) // PAIR) * PAIR
    packed = (parts, width, 2 * hidden // parts + PAIR + n_out)
    return pl.pallas_call(
        functools.partial(weight_kernel, parts),
        grid=(total,),
        in_specs=[wide, wide, narrow, narrow, narrow, narrow, pl.BlockSpec(norm_grad.shape, whole)],
        out_specs=pl.BlockSpec(packed, lambda s: (0, 0, 0)),
        out_shape=jax.ShapeDtypeStruct(packed, bf16),
        scratch_shapes=[pltpu.VMEM(s, f32) for s in ((width, width), (width, hidden), (width, hidden))],
        cost_estimate=work(total * rows * width * (3 * hidden + width), total * rows * (8 * width + 4 * hidden)),
        compiler_params=params(),
        name="weight_gradients",
    )(act, gh, xb, gf, gb, mo, norm_grad)


def exchange(value, over_dp, over_mp):
    perm = [(i, i ^ (2 * over_dp + over_mp)) for i in range(32)]
    return lax.ppermute(value, ("dp", "mp"), perm)


PLANE = ((0, 0), (2, 0), (0, 1), (2, 1))


def place():
    dp, mp = lax.axis_index("dp"), lax.axis_index("mp")
    return dp >> 2, (dp >> 1) & 1, dp & 1, mp


def order_kernel(at_ref, own_ref, got_ref, w_ref):
    z0, x0, c0, m0 = (at_ref[i] for i in range(4))
    rows, cols = own_ref.shape[2], own_ref.shape[3] // 3
    for c in range(2):
        for source, here in ((own_ref, c0), (got_ref, 1 - c0)):

            @pl.when(here == c)
            def _(source=source, c=c):
                for z in range(4):
                    for x in range(2):
                        for m in range(2):
                            block = source[z ^ z0, (x ^ x0) + 2 * (m ^ m0)]
                            at = ((z * 2 + x) * 2 + c) * rows
                            for third in range(3):
                                to = third * 2 * cols + m * cols
                                w_ref[at : at + rows, to : to + cols] = block[:, third * cols : (third + 1) * cols]


def gather_by_steps(shard, early):
    rows, cols = shard.shape
    plane = jnp.stack([shard] + [exchange(shard, *step) for step in PLANE[1:]])
    plane = jnp.stack([plane] + [exchange(plane, 4 * k, 0) for k in (1, 2, 3)])
    got, early = lax.optimization_barrier((exchange(plane, 1, 0), early))
    w = pl.pallas_call(
        order_kernel,
        in_specs=[pl.BlockSpec(memory_space=pltpu.SMEM)] + [pl.BlockSpec(memory_space=pltpu.VMEM)] * 2,
        out_specs=pl.BlockSpec(memory_space=pltpu.VMEM),
        out_shape=jax.ShapeDtypeStruct((16 * rows, 2 * cols), bf16),
        compiler_params=params(),
        name="order_rows",
    )(jnp.stack(place()).astype(jnp.int32), plane, got)
    return w, early


def scatter_by_steps(value, early):
    z, x, c, m = place()
    rows, cols = value.shape[2:]
    pick = lambda v, i, axis: lax.dynamic_index_in_dim(v, i, axis=axis, keepdims=False)
    value = value.reshape(4, 2, 2, 2, rows, cols)
    total = pick(value, c, 2).astype(f32) + exchange(pick(value, 1 - c, 2), 1, 0).astype(f32)
    total = pick(total, x, 1) + exchange(pick(total, 1 - x, 1).astype(bf16), 2, 0).astype(f32)
    got = [exchange(pick(total, z ^ k, 0).astype(bf16), 4 * k, 0) for k in (1, 2, 3)]
    total = sum((g.astype(f32) for g in got), pick(total, z, 0))
    total, early = lax.optimization_barrier((total, early))
    return pick(total, m, 0) + exchange(pick(total, 1 - m, 0).astype(bf16), 0, 1).astype(f32), early


def adam_update(weight, grad, mom, sec, rate):
    mom_new = beta_first * mom + (1.0 - beta_first) * grad
    sec_new = beta_second * sec + (1.0 - beta_second) * grad * grad
    scaled = (
        mom_new
        / (1.0 - beta_first**STEP)
        / (jnp.sqrt(sec_new / (1.0 - beta_second**STEP)) + adam_eps)
    )
    return (mom_new, sec_new, weight - rate * (scaled + decay_rate * weight))


def swap(value):
    return lax.ppermute(value, "mp", [(0, 1), (1, 0)])


def on_device(
    x_in,
    d_in,
    segments,
    cot_x,
    cot_d,
    w_qkv,
    w_out,
    w_in,
    w_back,
    norms,
    qkv_mom,
    qkv_sec,
    out_mom,
    out_sec,
    in_mom,
    in_sec,
    back_mom,
    back_sec,
    norm_mom,
    norm_sec,
):
    parts, owners = lax.axis_size("mp"), lax.axis_size("dp")
    me = lax.axis_index("mp")
    total, rows, width = x_in.shape
    mine = total // parts
    length = rows * parts
    own_rows, _, qkv_n = w_qkv.shape
    n_out, n_in, n_back = w_out.shape[0], w_in.shape[1], w_back.shape[0]
    hidden = parts * n_in
    here = lambda v, start, count: lax.dynamic_slice_in_dim(v, start, count, axis=0)
    by_steps = (owners, parts) == (16, 2)

    q_code, k_code = document_codes(here(segments, me * mine, mine))
    spread = jnp.arange(total, dtype=jnp.int32)

    if parts == 2:
        other = 1 - me
        step = max(mine // 2, 1)
        chunks = list(range(0, mine, step))
        got_x = [swap(here(x_in, other * mine + at, step)) for at in chunks]
        order = jnp.stack([me, other]).astype(jnp.int32)
        ids = [me * mine + at + spread[:step] for at in chunks]
    if by_steps:
        early = got_x[0], q_code, k_code, order, ids
        qkv, early = gather_by_steps(w_qkv.astype(bf16).reshape(own_rows, 3 * qkv_n), early)
        got_x[0], q_code, k_code, order, ids = early
    else:
        got = lax.all_gather(w_qkv.astype(bf16), ("dp", "mp"), axis=0)
        got = got.reshape(owners, parts, own_rows, 3, qkv_n)
        qkv = got.transpose(0, 2, 3, 1, 4).reshape(width, 3 * width)
    turned = jnp.pad(norms.T, ((0, 0), (0, PAIR - norms.shape[0])))
    shard = jnp.concatenate([w_in, w_back.T, turned, w_out.T], axis=1).astype(bf16)
    shard, qkv = lax.optimization_barrier((shard, qkv))
    weights = lax.all_gather(shard, ("dp", "mp"), axis=0)
    weights = weights.reshape(owners, parts, own_rows, shard.shape[1])
    if n_out % PAIR:
        weights = weights.transpose(0, 2, 1, 3).reshape(1, 1, width, parts, shard.shape[1])
        weights = [weights[..., a:b] for a, b in ((0, n_in), (n_in, n_in + n_back), (n_in + n_back + PAIR, shard.shape[1]))]
        weights = [w.reshape(1, 1, width, -1) for w in weights]
        norm_part = jnp.pad(lax.all_gather(norms.T.astype(bf16), "dp", axis=0, tiled=True), ((0, 0), (0, PAIR - norms.shape[0])))
        weights = jnp.concatenate(weights[:2] + [norm_part.reshape(1, 1, width, PAIR)] + weights[2:], axis=3)

    qkv_shape = (owners, parts, own_rows, 3 * qkv_n)

    def tokens(ids, first, mix, prev):
        return token_block(ids, first, mix, x_in, d_in, cot_x, cot_d, weights, hidden, prev)

    if parts == 2:
        forward, own_mix = [], None
        for i, at in enumerate(chunks):
            x = (x_in, got_x[i])
            kept, (own_mix, sent) = attend_forward(order, ids[i], at, mine, x, qkv, q_code, k_code, own_mix)
            forward.append((x, kept, sent, swap(sent)))
        prev, own_gm, norm_grad = tokens(me * mine + spread[:mine], 0, own_mix, ())
        got_gm = []
        for i, at in enumerate(chunks):
            prev, gm, ng = tokens(other * mine + at + spread[:step], mine + at, forward[i][3], prev)
            norm_grad = norm_grad + ng
            got_gm.append(swap(gm))
        x_out, d_out, x_grad, *saved = prev
        packed = weight_gradients(parts, *saved, norm_grad)
        packed, own_gm = lax.optimization_barrier((packed, own_gm))
        qkv_grad, got_dx = None, []
        for i, at in enumerate(chunks):
            x, kept, sent, _ = forward[i]
            last = qkv_shape if i == len(chunks) - 1 else None
            (x_grad, dx), qkv_grad = attend_backward(
                order, ids[i], at, x, (own_mix, sent), (own_gm, got_gm[i]), qkv, k_code, kept, x_grad, qkv_grad, last
            )
            if got_dx:
                qkv_grad, got_dx[-1] = lax.optimization_barrier((qkv_grad, got_dx[-1]))
            got_dx.append(swap(dx))
        for at, dx in zip(chunks, got_dx):
            start = other * mine + at
            added = here(x_grad, start, step) + dx.astype(f32)
            x_grad = lax.dynamic_update_slice_in_dim(x_grad, added, start, axis=0)
    else:

        def to_sequences(v):
            got = lax.all_to_all(v.reshape(parts, mine, rows, width), "mp", 0, 0)
            return got.transpose(1, 0, 2, 3).reshape(mine, length, width)

        def to_positions(v):
            sent = v.reshape(mine, parts, rows, width).transpose(1, 0, 2, 3)
            return lax.all_to_all(sent, "mp", 0, 0).reshape(total, rows, width)

        order, ids = jnp.zeros((1,), jnp.int32), spread[:mine]
        x = (to_sequences(x_in),)
        kept, (mix,) = attend_forward(order, ids, 0, mine, x, qkv, q_code, k_code, None)
        prev, gm, norm_grad = tokens(spread, 0, to_positions(mix), ())
        x_out, d_out, grad_r1, *saved = prev
        packed = weight_gradients(parts, *saved, norm_grad)
        go = (to_sequences(gm),)
        (dx,), qkv_grad = attend_backward(order, ids, 0, x, (mix,), go, qkv, k_code, kept, None, None, qkv_shape)
        x_grad = grad_r1 + to_positions(dx).astype(f32)

    got = lax.psum_scatter(packed, "dp", scatter_dimension=1, tiled=True)
    got = lax.psum_scatter(got, "mp", scatter_dimension=0, tiled=True)[0].astype(f32)
    in_g, back_g, norm_g, out_g = jnp.split(got, [n_in, n_in + n_back, n_in + n_back + PAIR], axis=1)
    back_g, norm_g, out_g = back_g.T, norm_g[:, : norms.shape[0]].T, out_g[:, :n_out].T
    states = (
        adam_update(w_out, out_g, out_mom, out_sec, 0.3)
        + adam_update(w_in, in_g, in_mom, in_sec, 0.05)
        + adam_update(w_back, back_g, back_mom, back_sec, 0.025)
        + adam_update(norms, norm_g, norm_mom, norm_sec, 0.1)
    )
    if by_steps:
        qkv_g, states = scatter_by_steps(qkv_grad, states)
    else:
        got = lax.psum_scatter(qkv_grad.reshape(owners, -1), "dp", scatter_dimension=0, tiled=True)
        qkv_g = lax.psum_scatter(got, "mp", scatter_dimension=1, tiled=True).astype(f32)
    qkv_g = qkv_g.reshape(own_rows, 3, qkv_n)
    qkv_state = adam_update(w_qkv, qkv_g, qkv_mom, qkv_sec, 0.05)
    return (x_out, d_out, x_grad, *qkv_state, *states)


def solution(mesh):
    stream = P("dp", "mp", None)
    weights = (P("dp", None, "mp"), P("mp", "dp"), P("dp", "mp"), P("mp", "dp"), P(None, "dp"))
    states = tuple(spec for spec in weights for _ in range(2))
    news = tuple(spec for spec in weights for _ in range(3))
    return jax.shard_map(
        on_device,
        mesh=mesh,
        in_specs=(stream, stream, P("dp", None), stream, stream) + weights + states,
        out_specs=(stream, stream, stream) + news,
        check_vma=False,
    )
```

```python
import functools

import jax
import jax.numpy as jnp
from jax import lax
from jax.experimental import pallas as pl
from jax.experimental.pallas import tpu as pltpu
from jax.sharding import PartitionSpec as P

STEP = 5
HD = 64
PAIR = 2 * HD
BLOCK = 256
CHUNK = 512
AHEAD = 3
BACK_AHEAD = 2
VMEM = 60 * 1024 * 1024

norm_eps = 1e-05
beta_first = 0.5
beta_second = 0.5
adam_eps = 1e-08
decay_rate = 0.01

FAR = 2.0**40
BITS = 7
EXTRA = 16
HEADS = 8

bf16 = jnp.bfloat16
f32 = jnp.float32


def dot_nn(a, b):
    return lax.dot_general(a, b, (((1,), (0,)), ((), ())), preferred_element_type=f32)


def dot_nt(a, b):
    return lax.dot_general(a, b, (((1,), (1,)), ((), ())), preferred_element_type=f32)


def dot_tn(a, b):
    return lax.dot_general(a, b, (((0,), (0,)), ((), ())), preferred_element_type=f32)


def params(**kw):
    return pltpu.CompilerParams(vmem_limit_bytes=VMEM, **kw)


def work(products, moved, exps=0):
    return pl.CostEstimate(flops=int(2 * products), bytes_accessed=int(moved), transcendentals=int(exps))


def split_three(value):
    high = value.astype(bf16).astype(f32)
    rest = value - high
    middle = rest.astype(bf16).astype(f32)
    return high, middle, (rest - middle).astype(bf16).astype(f32)


def document_rows(segments):
    row = lax.broadcasted_iota(jnp.int32, (EXTRA, segments.shape[1]), 0)
    bit = (segments >> jnp.where(row < BITS, row, row - BITS)) & 1
    used = row < 2 * BITS
    query = jnp.where(used, jnp.where(row < BITS, bit, 1 - bit), 0)
    key = jnp.where(used, jnp.where(row < BITS, 1 - bit, bit), 0)
    return query.astype(f32), key.astype(f32) * -FAR


def turned_rows(rows):
    rows = jnp.concatenate([rows, jnp.zeros((HD - rows.shape[0], rows.shape[1]), f32)], axis=0)
    return jnp.concatenate([rows, rows], axis=0).T.astype(bf16)


def first_half(shape, axis):
    return lax.broadcasted_iota(jnp.int32, shape, axis) < HD


def head_lanes(head):
    lane = lax.broadcasted_iota(jnp.int32, (1, PAIR), 1) % HD
    mine = (lane == EXTRA + head) | (lane == EXTRA + HEADS + head) | (lane == EXTRA + 2 * HEADS + head)
    return mine.astype(f32).astype(bf16)


def gather_pieces(order_ref, refs, held):
    if len(refs) == 1:
        return refs[0]
    rows = refs[0].shape[1]
    for i, ref in enumerate(refs):
        held[0, pl.ds(pl.multiple_of(order_ref[i] * rows, rows), rows), :] = ref[0]
    return held


def spread_pieces(order_ref, refs, value_ref):
    rows = refs[0].shape[1]
    for i, ref in enumerate(refs):
        ref[0] = value_ref[0, pl.ds(pl.multiple_of(order_ref[i] * rows, rows), rows), :]


def order_rows(order_ref, own_ref, got_ref, w_ref):
    z0, x0, c0, m0 = (order_ref[2 + i] for i in range(4))
    rows, cols = own_ref.shape[2], own_ref.shape[3] // 3
    for c in range(2):
        for source, here in ((own_ref, c0), (got_ref, 1 - c0)):

            @pl.when(here == c)
            def _(source=source, c=c):
                for z in range(4):
                    for x in range(2):
                        for m in range(2):
                            block = source[z ^ z0, (x ^ x0) + 2 * (m ^ m0)]
                            at = ((z * 2 + x) * 2 + c) * rows
                            for third in range(3):
                                to = third * 2 * cols + m * cols
                                w_ref[at : at + rows, to : to + cols] = block[:, third * cols : (third + 1) * cols]


def attend_forward_kernel(n, n_w, begun, *refs):
    order_ref, refs = refs[0], refs[1:]
    x_refs, w_refs, seg_ref = refs[:n], refs[n : n + n_w], refs[n + n_w]
    refs = refs[1 + n + n_w + begun :]
    q_ref, k_ref, v_ref, a_ref, kc_ref = refs[:5]
    mix_refs, refs = refs[5 : 5 + n], refs[5 + n :]
    w_ref = w_refs[0]
    if n_w == 2:
        w_ref, refs = refs[0], refs[1:]

        @pl.when(pl.program_id(0) == 0)
        def _():
            order_rows(order_ref, *w_refs, w_ref)

    lse_ref, x_held, mix_ref, qc_ref = refs
    x_ref = gather_pieces(order_ref, x_refs, x_held)
    length, width = q_ref.shape[1], q_ref.shape[2]
    query_rows, key_rows = document_rows(seg_ref[0])
    qc_ref[0], kc_ref[0] = turned_rows(query_rows), turned_rows(key_rows)
    x = x_ref[0]
    q = dot_nn(x, w_ref[:, 0:width]).astype(bf16)
    q_ref[0] = q * jnp.asarray(HD**-0.5, bf16)
    k_ref[0] = dot_nn(x, w_ref[:, width : 2 * width]).astype(bf16)
    v_ref[0] = dot_nn(x, w_ref[:, 2 * width : 3 * width]).astype(bf16)
    block = min(BLOCK, length)
    heads = width // HD

    @pl.loop(0, width // PAIR, unroll=width // PAIR)
    def _(pair):
        lanes = pl.ds(pl.multiple_of(pair * PAIR, PAIR), PAIR)
        q_pair, k_pair, v_pair = q_ref[0, :, lanes], k_ref[0, :, lanes], v_ref[0, :, lanes]
        q_code, k_code = qc_ref[0], kc_ref[0]
        v_turned = v_pair.T
        one = jnp.ones_like(v_turned)
        lane_half = first_half((length, PAIR), 1)
        row_half = first_half((PAIR, length), 0)
        out_half = first_half((PAIR, block), 0)
        causal = lax.broadcasted_iota(jnp.int32, (block, block), 0) <= lax.broadcasted_iota(
            jnp.int32, (block, block), 1
        )
        sides = []
        for odd in (0, 1):
            if odd:
                qa, ka = jnp.where(lane_half, q_code, q_pair), jnp.where(lane_half, k_code, k_pair)
                va = jnp.where(row_half, one, v_turned)
            else:
                qa, ka = jnp.where(lane_half, q_pair, q_code), jnp.where(lane_half, k_pair, k_code)
                va = jnp.where(row_half, v_turned, one)
            sides.append((qa, ka, va))
        steps = [(start, odd) for start in range(0, length, block) for odd in (0, 1)]

        def scores_of(step):
            start, odd = step
            qa, ka, _ = sides[odd]
            return dot_nt(ka[: start + block], qa[start : start + block])

        parts, logs, ahead = ([], []), ([], []), [scores_of(s) for s in steps[:AHEAD]]
        for i, (start, odd) in enumerate(steps):
            if i + AHEAD < len(steps):
                ahead.append(scores_of(steps[i + AHEAD]))
            scores = ahead.pop(0)
            last = jnp.where(causal, scores[start:], -FAR)
            scores = jnp.concatenate([scores[:start], last], axis=0) if start else last
            top = jnp.max(scores, axis=0, keepdims=True)
            weights = jnp.exp(scores - top).astype(bf16)
            out = dot_nn(sides[odd][2][:, : start + block], weights)
            total = out[0:1] if odd else out[HD : HD + 1]
            parts[odd].append(out * (1.0 / total))
            logs[odd].append(top + jnp.log(total))
        for odd in (0, 1):
            lse_ref[pl.ds(2 * pair + odd, 1), :] = jnp.concatenate(logs[odd], axis=1)
        for at, (even, odd) in enumerate(zip(*parts)):
            mixed = jnp.where(out_half, even, odd)
            mix_ref[0, at * block : (at + 1) * block, lanes] = mixed.T.astype(bf16)

    spread_pieces(order_ref, mix_refs, mix_ref)
    a_ref[0] = turned_rows(jnp.concatenate([query_rows, *split_three(-lse_ref[...])], axis=0))


def own_place(mine, n, at):
    return lambda s, order: ((order[0] * mine if n == 2 else 0) + at + s, 0, 0)


def attend_forward(order, at, count, pieces, w, segments, before):
    total, _, length = segments.shape
    width, n = pieces[0].shape[2], len(pieces)
    whole = lambda s, order: (0, 0)
    row = lambda s, order: (s, 0, 0)
    after = lambda s, order: (s + at, 0, 0)
    wide, narrow = pl.BlockSpec((1, length, width), row), pl.BlockSpec((1, length, PAIR), row)
    piece = lambda m: pl.BlockSpec((1, length // n, width), m)
    parts = [pl.BlockSpec((1, length // n, width), m) for m in (after, row)[:n]]
    full = lambda count, rows, cols: jax.ShapeDtypeStruct((count, rows, cols), bf16)
    ws = list(w) if isinstance(w, tuple) else [w]
    w_shape = (width, 3 * width)
    args = [order, *pieces, *ws, segments] + ([] if before is None else [before])
    out = pl.pallas_call(
        functools.partial(attend_forward_kernel, n, len(ws), before is not None),
        grid_spec=pltpu.PrefetchScalarGridSpec(
            num_scalar_prefetch=1,
            grid=(count,),
            in_specs=[piece(own_place(total, n, at)), piece(row)][:n]
            + [pl.BlockSpec(v.shape, lambda s, order, v=v: (0,) * v.ndim) for v in ws]
            + [pl.BlockSpec((1, 1, length), after)]
            + ([] if before is None else [pl.BlockSpec(memory_space=pl.ANY)]),
            out_specs=[wide, wide, wide, narrow, narrow] + parts + [pl.BlockSpec(w_shape, whole)] * (len(ws) - 1),
            scratch_shapes=[
                pltpu.VMEM((width // HD, length), f32),
                pltpu.VMEM((1, length, width), bf16),
                pltpu.VMEM((1, length, width), bf16),
                pltpu.VMEM((1, length, PAIR), bf16),
            ],
        ),
        out_shape=[full(count, length, width)] * 3
        + [full(count, length, PAIR)] * 2
        + [full(total, length // n, width), full(count, length // n, width)][:n]
        + [jax.ShapeDtypeStruct(w_shape, bf16)] * (len(ws) - 1),
        input_output_aliases={} if before is None else {len(args) - 1: 5},
        cost_estimate=work(count * length * width * (3 * width + 8 * length), count * length * width * 12),
        compiler_params=params(),
        name="attend_forward",
    )(*args)
    return out[:5], out[5:]


def attend_backward_kernel(n, begun, last, *refs):
    order_ref, refs = refs[0], refs[1:]
    x_refs, mix_refs, go_refs = (refs[i * n : (i + 1) * n] for i in range(3))
    w_ref, q_ref, k_ref, v_ref, a_ref, kc_ref = refs[3 * n : 6 + 3 * n]
    refs = refs[6 + 3 * n :]
    if n == 2:
        gr_ref, refs = refs[0], refs[1:]
    if begun:
        before_ref, refs = refs[0], refs[1:]
    dx_refs, refs = refs[:n], refs[n:]
    dw_ref, grads, delta_ref, dq_ref, x_held, mix_held, go_held, dw_sum, dx_held, w_held, sems = refs
    step = pl.program_id(0)
    fetched = [pltpu.make_async_copy(w_ref, w_held, sems.at[0])]
    if begun:
        fetched.append(pltpu.make_async_copy(before_ref, dw_sum, sems.at[1]))

    @pl.when(step == 0)
    def _():
        for copy in fetched:
            copy.start()
        if not begun:
            dw_sum[...] = jnp.zeros_like(dw_sum)

    x_ref = gather_pieces(order_ref, x_refs, x_held)
    mix_ref = gather_pieces(order_ref, mix_refs, mix_held)
    go_ref = gather_pieces(order_ref, go_refs, go_held)
    length, width = q_ref.shape[1], q_ref.shape[2]
    block = min(BLOCK, length)

    product = go_ref[0].astype(f32) * mix_ref[0].astype(f32)
    high = product.astype(bf16)
    low = (product - high.astype(f32)).astype(bf16)
    lane = lax.broadcasted_iota(jnp.int32, (width, PAIR), 1) % HD
    head = lax.broadcasted_iota(jnp.int32, (width, PAIR), 0) // HD
    third = lane - EXTRA - head
    picks = ((third == 0) | (third == HEADS) | (third == 2 * HEADS)).astype(f32).astype(bf16)
    delta = -(dot_nn(high, picks) + dot_nn(low, picks))
    high, middle, low = split_three(delta)
    lane = lax.broadcasted_iota(jnp.int32, (length, PAIR), 1) % HD
    delta_ref[...] = jnp.where(
        lane < EXTRA + HEADS, high, jnp.where(lane < EXTRA + 2 * HEADS, middle, low)
    ).astype(bf16)

    @pl.loop(0, width // PAIR, unroll=width // PAIR)
    def _(pair):
        lanes = pl.ds(pl.multiple_of(pair * PAIR, PAIR), PAIR)
        q_pair, k_pair, v_pair, go_pair = (r[0, :, lanes] for r in (q_ref, k_ref, v_ref, go_ref))
        a, k_code, minus = a_ref[0], kc_ref[0], delta_ref[...]
        q_turned, go_turned = q_pair.T, go_pair.T
        lane_half = first_half((length, PAIR), 1)
        row_half = first_half((PAIR, block), 0)
        causal = lax.broadcasted_iota(jnp.int32, (block, block), 0) >= lax.broadcasted_iota(
            jnp.int32, (block, block), 1
        )
        sides = []
        for odd in (0, 1):
            mine = head_lanes(2 * pair + odd)
            both = ((q_pair, a), (k_pair, k_code + mine), (v_pair, jnp.broadcast_to(mine, v_pair.shape)), (go_pair, minus))
            sides.append([jnp.where(lane_half, other, own) if odd else jnp.where(lane_half, own, other) for own, other in both])
        steps = [(start, odd) for start in range(0, length, block) for odd in (0, 1)]

        def products_of(step):
            start, odd = step
            qa, ka, va, ga = sides[odd]
            stop = start + block
            return dot_nt(qa[start:], ka[start:stop]), dot_nt(ga[start:], va[start:stop])

        dk, dv, ahead = ([], []), ([], []), [products_of(s) for s in steps[:BACK_AHEAD]]
        for i, (start, odd) in enumerate(steps):
            if i + BACK_AHEAD < len(steps):
                ahead.append(products_of(steps[i + BACK_AHEAD]))
            scores, dprobs = ahead.pop(0)
            stop = start + block
            first = jnp.where(causal, scores[:block], -FAR)
            scores = jnp.concatenate([first, scores[block:]], axis=0) if stop < length else first
            probs = jnp.exp(scores)
            dscores = (probs * dprobs).astype(bf16)
            dv[odd].append(dot_nn(go_turned[:, start:], probs.astype(bf16)))
            dk[odd].append(dot_nn(q_turned[:, start:], dscores))
            dq_at = dot_nn(dscores, k_pair[start:stop])
            if start:
                dq_ref[odd, start:, :] += dq_at
            else:
                dq_ref[odd] = dq_at
        dk, dv = ([jnp.where(row_half, even, odd) for even, odd in zip(*d)] for d in (dk, dv))
        dq = jnp.where(lane_half, dq_ref[0], dq_ref[1]) * HD**-0.5
        grads[:, lanes] = dq.astype(bf16)
        k_lanes = pl.ds(pl.multiple_of(width + pair * PAIR, PAIR), PAIR)
        v_lanes = pl.ds(pl.multiple_of(2 * width + pair * PAIR, PAIR), PAIR)
        for at, start in enumerate(range(0, length, block)):
            grads[start : start + block, k_lanes] = dk[at].T.astype(bf16)
            grads[start : start + block, v_lanes] = dv[at].T.astype(bf16)

    @pl.when(step == 0)
    def _():
        for copy in fetched:
            copy.wait()

    dw_sum[...] += dot_tn(x_ref[0], grads[...])
    dx_held[0] = dot_nt(grads[...], w_held[...])
    if n == 2:
        rows = length // n
        pick = lambda i: dx_held[0, pl.ds(pl.multiple_of(order_ref[i] * rows, rows), rows), :]
        dx_refs[0][0] = gr_ref[0] + pick(0)
        dx_refs[1][0] = pick(1).astype(bf16)
    else:
        dx_refs[0][0] = dx_held[0].astype(bf16)

    @pl.when(step == pl.num_programs(0) - 1)
    def _():
        if last:
            owners, parts, rows, cols = dw_ref.shape
            cols //= 3
            for part in range(parts):
                for third in range(3):
                    start = third * width + part * cols
                    block = dw_sum[:, start : start + cols].astype(bf16)
                    dw_ref[:, part, :, third * cols : (third + 1) * cols] = block.reshape(owners, rows, cols)
        else:
            copy = pltpu.make_async_copy(dw_sum, dw_ref, sems.at[1])
            copy.start()
            copy.wait()


def attend_backward(order, at, mine, x, mix, go, w, kept, grad_r1, before, last):
    count, length = kept[0].shape[:2]
    width, n = w.shape[0], len(x)
    row = lambda s, order: (s, 0, 0)
    wide, narrow = pl.BlockSpec((1, length, width), row), pl.BlockSpec((1, length, PAIR), row)
    anywhere = pl.BlockSpec(memory_space=pl.ANY)
    piece = lambda m: pl.BlockSpec((1, length // n, width), m)
    part, held, own = piece(row), piece(own_place(mine, n, at)), piece(lambda s, order: (s + at, 0, 0))
    args = [order, *x, *mix, *go, w, *kept]
    specs = [held, part][:n] + [own, part][:n] * 2 + [anywhere, wide, wide, wide, narrow, narrow]
    weight_out, dw_shape = anywhere, jax.ShapeDtypeStruct(w.shape, f32)
    if last:
        weight_out = pl.BlockSpec(last, lambda s, order: (0, 0, 0, 0))
        dw_shape = jax.ShapeDtypeStruct(last, bf16)
    dx_specs, dx_shapes = [part], [jax.ShapeDtypeStruct((count, length // n, width), bf16)]
    alias = {}
    if n == 2:
        alias[len(args)] = 0
        args.append(grad_r1)
        specs.append(held)
        dx_specs, dx_shapes = [held] + dx_specs, [jax.ShapeDtypeStruct(grad_r1.shape, f32)] + dx_shapes
    if before is not None:
        args.append(before)
        specs.append(anywhere)
    out = pl.pallas_call(
        functools.partial(attend_backward_kernel, n, before is not None, last),
        grid_spec=pltpu.PrefetchScalarGridSpec(
            num_scalar_prefetch=1,
            grid=(count,),
            in_specs=specs,
            out_specs=dx_specs + [weight_out],
            scratch_shapes=[
                pltpu.VMEM((length, 3 * width), bf16),
                pltpu.VMEM((length, PAIR), bf16),
                pltpu.VMEM((2, length, PAIR), f32),
                pltpu.VMEM((1, length, width), bf16),
                pltpu.VMEM((1, length, width), bf16),
                pltpu.VMEM((1, length, width), bf16),
                pltpu.VMEM(w.shape, f32),
                pltpu.VMEM((1, length, width), f32),
                pltpu.VMEM(w.shape, bf16),
                pltpu.SemaphoreType.DMA((2,)),
            ],
        ),
        out_shape=dx_shapes + [dw_shape],
        input_output_aliases=alias,
        cost_estimate=work(count * length * width * (6 * width + 16 * length), count * length * width * 20),
        compiler_params=params(),
        name="attend_backward",
    )(*args)
    return out[:n], out[n]


def normalize(rows):
    center = rows - jnp.mean(rows, axis=-1, keepdims=True)
    rstd = lax.rsqrt(jnp.mean(center * center, axis=-1, keepdims=True) + norm_eps)
    return center * rstd, rstd


def normalize_back(grad, xhat, rstd, gain):
    scaled = grad * gain
    return rstd * (
        scaled - jnp.mean(scaled, axis=-1, keepdims=True) - xhat * jnp.mean(scaled * xhat, axis=-1, keepdims=True)
    )


def token_kernel(sizes, parts, begun, last, *refs):
    n, step = len(sizes), pl.program_id(0)
    order_ref, x_ref, d_ref, cx_ref, cd_ref = refs[:5]
    mix_refs, (in_ref, back_ref, out_parts_ref, norm_ref), refs = refs[5 : 5 + n], refs[5 + n : 9 + n], refs[9 + n :]
    if begun:
        sums_in, ng_in, refs = refs[3], refs[4], refs[5:]
    xo_ref, do_ref, gr_ref = refs[:3]
    gm_refs, refs = refs[3 : 3 + n], refs[3 + n :]
    if last:
        packed_ref, refs = refs[0], refs[1:]
    else:
        sums_out, ng_out, refs = refs[0], refs[1], refs[2:]
    act_ref, slope, out_ref, sums, ng_ref, sem = refs
    width, hidden = in_ref.shape
    n_out = width // parts
    chunk = min(CHUNK, hidden)
    columns = [slice(at, at + chunk) for at in range(0, hidden, chunk)]
    back_columns = [slice(hidden + at, hidden + at + chunk) for at in range(0, hidden, chunk)]
    out_columns = slice(2 * hidden, 2 * hidden + width)
    starts = [sum(sizes[:i]) for i in range(n)]

    @pl.when(step == 0)
    def _():
        if begun:
            pltpu.make_async_copy(sums_in, sums, sem).start()
            ng_ref[...] = ng_in[...]
        else:
            sums[...] = jnp.zeros_like(sums)
            ng_ref[...] = jnp.zeros_like(ng_ref)
        for i in range(parts):
            if n_out % PAIR:
                out_ref[:, i * n_out : (i + 1) * n_out] = out_parts_ref[:, i * n_out : (i + 1) * n_out]
            else:
                to = pl.ds(pl.multiple_of(order_ref[i] * n_out, PAIR), n_out)
                out_ref[:, to] = out_parts_ref[:, i * n_out : (i + 1) * n_out]
    turned = norm_ref[...].astype(f32).T
    g1, b1, g2, b2 = (turned[i : i + 1] for i in range(4))
    mix = mix_refs[0][0]
    for ref, start in zip(mix_refs[1:], starts[1:]):
        mix = jnp.where(step >= start, ref[0], mix)
    attended = dot_nt(mix, out_ref[...])
    xhat1, rstd1 = normalize(x_ref[0].astype(f32) + attended)
    x_one = xhat1 * g1 + b1
    xb = x_one.astype(bf16)
    feed, h = None, dot_nn(xb, in_ref[:, columns[0]])
    for i, cols in enumerate(columns):
        ahead = dot_nn(xb, in_ref[:, columns[i + 1]]) if i + 1 < len(columns) else None
        cdf = 0.5 * lax.erf(h * 0.7071067811865476) + 0.5
        active = (h * cdf).astype(bf16)
        act_ref[:, cols] = active
        slope[:, cols] = cdf + h * (jnp.exp(-0.5 * (h * h)) * 0.3989422804014327)
        product = dot_nt(active, back_ref[:, cols])
        feed = product if feed is None else feed + product
        h = ahead
    xhat2, rstd2 = normalize(x_one + feed)
    xo_ref[0] = (xhat2 * g2 + b2).astype(bf16)
    do_ref[0] = (d_ref[0].astype(f32) + attended + feed).astype(bf16)
    cx, cd = cx_ref[0].astype(f32), cd_ref[0].astype(f32)
    grad_r2 = normalize_back(cx, xhat2, rstd2, g2)
    dg2, db2 = jnp.sum(cx * xhat2, axis=0, keepdims=True), jnp.sum(cx, axis=0, keepdims=True)
    gf = (grad_r2 + cd).astype(bf16)

    if begun:

        @pl.when(step == 0)
        def _():
            pltpu.make_async_copy(sums_in, sums, sem).wait()

    gf_turned, xb_turned = gf.T, xb.T
    grad_x1, ga = grad_r2, dot_nn(gf, back_ref[:, columns[0]])
    for i, cols in enumerate(columns):
        ahead = dot_nn(gf, back_ref[:, columns[i + 1]]) if i + 1 < len(columns) else None
        gh = (ga * slope[:, cols]).astype(bf16)
        grad_x1 = grad_x1 + dot_nt(gh, in_ref[:, cols])
        sums[:, cols] += dot_nn(xb_turned, gh)
        ga = ahead
    for cols, to in zip(columns, back_columns):
        sums[:, to] += dot_nn(gf_turned, act_ref[:, cols])
    grad_r1 = normalize_back(grad_x1, xhat1, rstd1, g1)
    gr_ref[0] = grad_r1
    dg1, db1 = jnp.sum(grad_x1 * xhat1, axis=0, keepdims=True), jnp.sum(grad_x1, axis=0, keepdims=True)
    ng_ref[...] += jnp.concatenate([dg1, db1, dg2, db2, jnp.zeros((4, dg1.shape[1]), f32)], axis=0)
    gb = (grad_r1 + cd).astype(bf16)
    gm = dot_nn(gb, out_ref[...]).astype(bf16)
    sums[:, out_columns] += dot_tn(gb, mix)
    for ref, start, size in zip(gm_refs, starts, sizes):

        @pl.when((step >= start) & (step < start + size))
        def _(ref=ref):
            ref[0] = gm

    @pl.when(step == pl.num_programs(0) - 1)
    def _():
        if last:
            n_hidden = hidden // parts
            rest = jnp.zeros((PAIR - ng_ref.shape[0], width), f32)
            norms = jnp.concatenate([ng_ref[...], rest], axis=0).T
            for i in range(parts):
                to = 0
                own = lambda start, size: sums[:, start + i * size : start + (i + 1) * size]
                if n_out % PAIR:
                    out = own(2 * hidden, n_out)
                else:
                    out = sums[:, pl.ds(pl.multiple_of(2 * hidden + order_ref[i] * n_out, PAIR), n_out)]
                for value in (own(0, n_hidden), own(hidden, n_hidden), norms, out):
                    size = value.shape[1]
                    packed_ref[i, :, to : to + size] = value.astype(bf16)
                    to += size
        else:
            ng_out[...] = ng_ref[...]
            copy = pltpu.make_async_copy(sums, sums_out, sem)
            copy.start()
            copy.wait()


def token_block(order, places, mixes, x, d, cot_x, cot_d, weights, hidden, parts, before, last):
    (total, rows, width), sizes = x.shape, [m.shape[0] for m in mixes]
    n_hidden, n_out = hidden // parts, width // parts
    starts = [sum(sizes[:i]) for i in range(len(sizes))]

    def there(s, order):
        at = places[0](order) + s
        for start, place in zip(starts[1:], places[1:]):
            at = jnp.where(s < start, at, place(order) + s - start)
        return at, 0, 0

    whole = lambda s, order: (0, 0)
    one = (1, rows, width)
    full = lambda count, dtype: jax.ShapeDtypeStruct((count, rows, width), dtype)

    def within(i):
        return pl.BlockSpec(one, lambda s, order: (jnp.clip(s - starts[i], 0, sizes[i] - 1), 0, 0))

    anywhere, ng = pl.BlockSpec(memory_space=pl.ANY), pl.BlockSpec((8, width), whole)
    mix_specs = [within(i) for i in range(len(mixes))]
    sums = jax.ShapeDtypeStruct((width, 2 * hidden + width), f32)
    packed = (parts, width, 2 * n_hidden + PAIR + -(-n_out // PAIR) * PAIR)
    if last:
        sum_specs, sum_shapes = [pl.BlockSpec(packed, lambda s, order: (0, 0, 0))], [jax.ShapeDtypeStruct(packed, bf16)]
    else:
        sum_specs, sum_shapes = [anywhere, ng], [sums, jax.ShapeDtypeStruct((8, width), f32)]
    window = lambda cols, at: pl.BlockSpec((width, cols), lambda s, order: (0, at // cols))
    windows = [window(hidden, 0), window(hidden, hidden), window(width, 2 * hidden), window(PAIR, 2 * hidden + width)]
    at = 9 + len(mixes)
    count = sum(sizes)
    out = pl.pallas_call(
        functools.partial(token_kernel, tuple(sizes), parts, bool(before), last),
        grid_spec=pltpu.PrefetchScalarGridSpec(
            num_scalar_prefetch=1,
            grid=(count,),
            in_specs=[pl.BlockSpec(one, there)] * 4
            + mix_specs
            + windows
            + ([anywhere] * 4 + [ng] if before else []),
            out_specs=[pl.BlockSpec(one, there)] * 3 + mix_specs + sum_specs,
            scratch_shapes=[pltpu.VMEM((rows, hidden), bf16), pltpu.VMEM((rows, hidden), f32)]
            + [pltpu.VMEM((width, width), bf16), pltpu.VMEM(sums.shape, f32), pltpu.VMEM((8, width), f32), pltpu.SemaphoreType.DMA],
        ),
        out_shape=[full(total, bf16), full(total, bf16), full(total, f32)] + [full(c, bf16) for c in sizes] + sum_shapes,
        input_output_aliases={at + i: i for i in range(3)} if before else {},
        cost_estimate=work(count * rows * width * (9 * hidden + 3 * width), count * rows * width * 20),
        compiler_params=params(),
        name="token_block",
    )(order, x, d, cot_x, cot_d, *mixes, *[weights] * 4, *before)
    return out[:3] + out[3 + len(mixes) :], out[3 : 3 + len(mixes)]


def exchange(value, over_dp, over_mp):
    perm = [(i, i ^ (2 * over_dp + over_mp)) for i in range(32)]
    return lax.ppermute(value, ("dp", "mp"), perm)


PLANE = ((0, 0), (2, 0), (0, 1), (2, 1))


def place():
    dp, mp = lax.axis_index("dp"), lax.axis_index("mp")
    return dp >> 2, (dp >> 1) & 1, dp & 1, mp


def gather_by_steps(shard, sends, first, arrange, early):
    plane = jnp.stack([shard] + [exchange(shard, *step) for step in PLANE[1:]])
    plane, sends, first = lax.optimization_barrier((plane, sends, swap(first)))
    first = arrange(first)
    got = swap(sends[0])
    line = [exchange(plane, 4 * k, 0) for k in (1, 2, 3)]
    plane, got, first, early = lax.optimization_barrier((jnp.stack([plane] + line), got, first, early))
    return plane, exchange(plane, 1, 0), [got] + [swap(v) for v in sends[1:]], first, early


def scatter_by_steps(value, dx, last):
    z, x, c, m = place()
    rows, cols = value.shape[2:]
    pick = lambda v, i, axis: lax.dynamic_index_in_dim(v, i, axis=axis, keepdims=False)
    value = value.reshape(4, 2, 2, 2, rows, cols)
    got, dx = lax.optimization_barrier((exchange(pick(value, 1 - c, 2), 1, 0), dx))
    dx = swap(dx)
    total = pick(value, c, 2).astype(f32) + got.astype(f32)
    total = pick(total, x, 1) + exchange(pick(total, 1 - x, 1).astype(bf16), 2, 0).astype(f32)
    got = [exchange(pick(total, z ^ k, 0).astype(bf16), 4 * k, 0) for k in (1, 2, 3)]
    total = sum((g.astype(f32) for g in got), pick(total, z, 0))
    total, dx = lax.optimization_barrier((total, dx))
    sent = jnp.concatenate([pick(total, 1 - m, 0).astype(bf16), last], axis=1)
    return pick(total, m, 0), swap(sent), dx


RATES = (0.05, 0.3, 0.05, 0.025, 0.1)


def update_kernel(own_ref, token_ref, got_ref, *refs):
    states, outs = refs[:15], refs[15:]
    cols = own_ref.shape[1]
    n_in, n_back, n_out = states[6].shape[1], states[9].shape[1], states[3].shape[1]
    qkv = own_ref[...] + got_ref[:, :cols].astype(f32)
    token = lambda at, size: token_ref[0, :, at : at + size].astype(f32) + got_ref[:, cols + at : cols + at + size].astype(f32)
    norm_at = n_in + n_back
    grads = (
        qkv,
        token(norm_at + PAIR, n_out),
        token(0, n_in),
        token(n_in, n_back),
        token(norm_at, PAIR).T[: states[12].shape[0]],
    )
    for i, (grad, rate) in enumerate(zip(grads, RATES)):
        weight, mom, sec = states[3 * i : 3 * i + 3]
        mine = outs[3 * i : 3 * i + 3]
        if i:
            for ref, value in zip(mine, adam_update(weight[...], grad, mom[...], sec[...], rate)):
                ref[...] = value
        else:
            size = cols // 3
            for third in range(3):
                part = grad[:, third * size : (third + 1) * size]
                for ref, value in zip(mine, adam_update(weight[third], part, mom[third], sec[third], rate)):
                    ref[third] = value


def update(own, token, got, states):
    vmem = pl.BlockSpec(memory_space=pltpu.VMEM)
    return pl.pallas_call(
        update_kernel,
        in_specs=[vmem] * (3 + len(states)),
        out_specs=[vmem] * len(states),
        out_shape=[jax.ShapeDtypeStruct(v.shape, f32) for v in states],
        compiler_params=params(),
        name="update",
    )(own, token, got, *states)


def adam_update(weight, grad, mom, sec, rate):
    mom_new = beta_first * mom + (1.0 - beta_first) * grad
    sec_new = beta_second * sec + (1.0 - beta_second) * grad * grad
    scaled = (
        mom_new
        / (1.0 - beta_first**STEP)
        / (jnp.sqrt(sec_new / (1.0 - beta_second**STEP)) + adam_eps)
    )
    return (mom_new, sec_new, weight - rate * (scaled + decay_rate * weight))


def swap(value):
    return lax.ppermute(value, "mp", [(0, 1), (1, 0)])


def on_device(
    x_in,
    d_in,
    segments,
    cot_x,
    cot_d,
    w_qkv,
    w_out,
    w_in,
    w_back,
    norms,
    qkv_mom,
    qkv_sec,
    out_mom,
    out_sec,
    in_mom,
    in_sec,
    back_mom,
    back_sec,
    norm_mom,
    norm_sec,
):
    parts, owners = lax.axis_size("mp"), lax.axis_size("dp")
    me = lax.axis_index("mp")
    total, rows, width = x_in.shape
    mine = total // parts
    length = rows * parts
    own_rows, _, qkv_n = w_qkv.shape
    n_out, n_in, n_back = w_out.shape[0], w_in.shape[1], w_back.shape[0]
    hidden = parts * n_in
    here = lambda v, start, count: lax.dynamic_slice_in_dim(v, start, count, axis=0)
    by_steps = (owners, parts) == (16, 2)

    order = jnp.arange(parts, dtype=jnp.int32)
    own_segments = here(segments, me * mine, mine).reshape(mine, 1, length)

    if parts == 2:
        other = 1 - me
        step = max(mine // 2, 1)
        chunks = list(range(0, mine, step))
        send_x = [here(x_in, other * mine + at, step) for at in chunks]
        order = jnp.stack([me, other, *place()]).astype(jnp.int32)
    shard = jnp.concatenate([w_in, w_back.T, w_out.T], axis=1).astype(bf16)

    def arrange(shards):
        columns = zip(*(jnp.split(v, [n_in, n_in + n_back], axis=1) for v in shards))
        columns = [c for kind in columns for c in kind]
        columns.append(jnp.pad(norms.T.astype(bf16), ((0, 0), (0, PAIR - norms.shape[0]))))
        return jnp.concatenate(columns, axis=1)

    if by_steps:
        shard_qkv = w_qkv.astype(bf16).reshape(own_rows, 3 * qkv_n)
        early = own_segments, order
        plane, got, got_x, columns, early = gather_by_steps(
            shard_qkv, send_x, shard, lambda theirs: arrange([shard, theirs]), early
        )
        qkv, (own_segments, order) = (plane, got), early
    else:
        got = lax.all_gather(w_qkv.astype(bf16), ("dp", "mp"), axis=0)
        got = got.reshape(owners, parts, own_rows, 3, qkv_n)
        qkv = got.transpose(0, 2, 3, 1, 4).reshape(width, 3 * width)
        got_x = [swap(v) for v in send_x] if parts == 2 else None
        columns = arrange([shard, swap(shard)] if parts == 2 else list(lax.all_gather(shard, "mp", axis=0)))
    weights = lax.all_gather(columns, "dp", axis=0, tiled=True)

    qkv_shape = (owners, parts, own_rows, 3 * qkv_n)

    def tokens(places, mixes, before, last):
        return token_block(order, places, mixes, x_in, d_in, cot_x, cot_d, weights, hidden, parts, before, last)

    if parts == 2:
        forward, own_mix = [], None
        for i, at in enumerate(chunks):
            x = (x_in, got_x[i])
            kept, (own_mix, sent, *made) = attend_forward(order, at, step, x, qkv, own_segments, own_mix)
            qkv = made[0] if made else qkv
            forward.append((x, kept, sent, swap(sent)))
        before, got_gm = (), []
        for i, at in enumerate(chunks):
            mixes, places = [forward[i][3]], [lambda order, at=at: order[1] * mine + at]
            if i == 0:
                mixes, places = [own_mix] + mixes, [lambda order: order[0] * mine] + places
            before, gms = tokens(places, mixes, before, i == len(chunks) - 1)
            own_gm = gms[0] if i == 0 else own_gm
            got_gm.append(swap(gms[-1]))
        x_out, d_out, x_grad, packed = before
        qkv_grad, got_dx = None, []
        for i, at in enumerate(chunks):
            x, kept, sent, _ = forward[i]
            last = qkv_shape if i == len(chunks) - 1 else None
            (x_grad, dx), qkv_grad = attend_backward(
                order, at, mine, x, (own_mix, sent), (own_gm, got_gm[i]), qkv, kept, x_grad, qkv_grad, last
            )
            if got_dx:
                qkv_grad, got_dx[-1] = lax.optimization_barrier((qkv_grad, got_dx[-1]))
            got_dx.append(dx if last else swap(dx))
    else:

        def to_sequences(v):
            got = lax.all_to_all(v.reshape(parts, mine, rows, width), "mp", 0, 0)
            return got.transpose(1, 0, 2, 3).reshape(mine, length, width)

        def to_positions(v):
            sent = v.reshape(mine, parts, rows, width).transpose(1, 0, 2, 3)
            return lax.all_to_all(sent, "mp", 0, 0).reshape(total, rows, width)

        x = (to_sequences(x_in),)
        kept, (mix,) = attend_forward(order, 0, mine, x, qkv, own_segments, None)
        (x_out, d_out, grad_r1, packed), (gm,) = tokens([lambda order: 0], [to_positions(mix)], (), True)
        go = (to_sequences(gm),)
        (dx,), qkv_grad = attend_backward(order, 0, mine, x, (mix,), go, qkv, kept, None, None, qkv_shape)
        x_grad = grad_r1 + to_positions(dx).astype(f32)

    got = lax.psum_scatter(packed, "dp", scatter_dimension=1, tiled=True)

    states = (
        (w_qkv, qkv_mom, qkv_sec),
        (w_out, out_mom, out_sec),
        (w_in, in_mom, in_sec),
        (w_back, back_mom, back_sec),
        (norms, norm_mom, norm_sec),
    )
    if by_steps:
        own, theirs, got_dx[-1] = scatter_by_steps(qkv_grad, got_dx[-1], got[1])
        turns = ((1, 0, 2), (1, 0), (0, 1), (1, 0), (0, 1))
        turned = [v.transpose(turn) for state, turn in zip(states, turns) for v in state]
        new = update(own, got, theirs, turned)
        new = [v.transpose(turns[i // 3]) for i, v in enumerate(new)]
    else:
        if parts == 2:
            got_dx[-1] = swap(got_dx[-1])
            grads = got[0].astype(f32) + swap(got[1]).astype(f32)
        else:
            grads = lax.psum_scatter(got, "mp", scatter_dimension=0, tiled=True)[0].astype(f32)
        in_g, back_g, norm_g, out_g = jnp.split(grads, [n_in, n_in + n_back, n_in + n_back + PAIR], axis=1)
        got = lax.psum_scatter(qkv_grad.reshape(owners, -1), "dp", scatter_dimension=0, tiled=True)
        qkv_g = lax.psum_scatter(got, "mp", scatter_dimension=1, tiled=True).astype(f32)
        grads = (qkv_g.reshape(own_rows, 3, qkv_n), out_g[:, :n_out].T, in_g, back_g.T, norm_g[:, : norms.shape[0]].T)
        new = [v for (w, m, v), g, rate in zip(states, grads, RATES) for v in adam_update(w, g, m, v, rate)]
    if parts == 2:
        for at, dx in zip(chunks, got_dx):
            at = other * mine + at
            added = here(x_grad, at, step) + dx.astype(f32)
            x_grad = lax.dynamic_update_slice_in_dim(x_grad, added, at, axis=0)
    return (x_out, d_out, x_grad, *new)


def solution(mesh):
    stream = P("dp", "mp", None)
    weights = (P("dp", None, "mp"), P("mp", "dp"), P("dp", "mp"), P("mp", "dp"), P(None, "dp"))
    states = tuple(spec for spec in weights for _ in range(2))
    news = tuple(spec for spec in weights for _ in range(3))
    return jax.shard_map(
        on_device,
        mesh=mesh,
        in_specs=(stream, stream, P("dp", None), stream, stream) + weights + states,
        out_specs=(stream, stream, stream) + news,
        check_vma=False,
    )
```

```python
import functools

import jax
import jax.numpy as jnp
from jax import lax
from jax.experimental import pallas as pl
from jax.experimental.pallas import tpu as pltpu
from jax.sharding import PartitionSpec as P

STEP = 5
HD = 64
PAIR = 2 * HD
BLOCK = 256
CHUNK = 512
AHEAD = 4
BACK_AHEAD = 2
VMEM = 60 * 1024 * 1024

norm_eps = 1e-05
beta_first = 0.5
beta_second = 0.5
adam_eps = 1e-08
decay_rate = 0.01

FAR = 2.0**40
BITS = 7
EXTRA = 16
HEADS = 8

bf16 = jnp.bfloat16
f32 = jnp.float32


def dot_nn(a, b):
    return lax.dot_general(a, b, (((1,), (0,)), ((), ())), preferred_element_type=f32)


def dot_nt(a, b):
    return lax.dot_general(a, b, (((1,), (1,)), ((), ())), preferred_element_type=f32)


def dot_tn(a, b):
    return lax.dot_general(a, b, (((0,), (0,)), ((), ())), preferred_element_type=f32)


def params(**kw):
    return pltpu.CompilerParams(vmem_limit_bytes=VMEM, **kw)


def work(products, moved, exps=0):
    return pl.CostEstimate(flops=int(2 * products), bytes_accessed=int(moved), transcendentals=int(exps))


def split_three(value):
    high = value.astype(bf16).astype(f32)
    rest = value - high
    middle = rest.astype(bf16).astype(f32)
    return high, middle, (rest - middle).astype(bf16).astype(f32)


def document_rows(segments):
    row = lax.broadcasted_iota(jnp.int32, (EXTRA, segments.shape[1]), 0)
    bit = (segments >> jnp.where(row < BITS, row, row - BITS)) & 1
    used = row < 2 * BITS
    query = jnp.where(used, jnp.where(row < BITS, bit, 1 - bit), 0)
    key = jnp.where(used, jnp.where(row < BITS, 1 - bit, bit), 0)
    return query.astype(f32), key.astype(f32) * -FAR


def turned_rows(rows):
    rows = jnp.concatenate([rows, jnp.zeros((HD - rows.shape[0], rows.shape[1]), f32)], axis=0)
    return jnp.concatenate([rows, rows], axis=0).T.astype(bf16)


def first_half(shape, axis):
    return lax.broadcasted_iota(jnp.int32, shape, axis) < HD


def head_lanes(head):
    lane = lax.broadcasted_iota(jnp.int32, (1, PAIR), 1) % HD
    mine = (lane == EXTRA + head) | (lane == EXTRA + HEADS + head) | (lane == EXTRA + 2 * HEADS + head)
    return mine.astype(f32).astype(bf16)


def gather_pieces(order_ref, refs, held):
    if len(refs) == 1:
        return refs[0]
    rows = refs[0].shape[1]
    for i, ref in enumerate(refs):
        held[0, pl.ds(pl.multiple_of(order_ref[i] * rows, rows), rows), :] = ref[0]
    return held


def spread_pieces(order_ref, refs, value_ref):
    rows = refs[0].shape[1]
    for i, ref in enumerate(refs):
        ref[0] = value_ref[0, pl.ds(pl.multiple_of(order_ref[i] * rows, rows), rows), :]


def order_rows(order_ref, own_ref, got_ref, w_ref):
    z0, x0, c0, m0 = (order_ref[2 + i] for i in range(4))
    rows, cols = own_ref.shape[2], own_ref.shape[3] // 3
    for c in range(2):
        for source, here in ((own_ref, c0), (got_ref, 1 - c0)):

            @pl.when(here == c)
            def _(source=source, c=c):
                for z in range(4):
                    for x in range(2):
                        for m in range(2):
                            block = source[z ^ z0, (x ^ x0) + 2 * (m ^ m0)]
                            at = ((z * 2 + x) * 2 + c) * rows
                            for third in range(3):
                                to = third * 2 * cols + m * cols
                                w_ref[at : at + rows, to : to + cols] = block[:, third * cols : (third + 1) * cols]


def attend_forward_kernel(n, n_w, begun, *refs):
    order_ref, refs = refs[0], refs[1:]
    x_refs, w_refs, seg_ref = refs[:n], refs[n : n + n_w], refs[n + n_w]
    refs = refs[1 + n + n_w + begun :]
    q_ref, k_ref, v_ref, a_ref, kc_ref = refs[:5]
    mix_refs, refs = refs[5 : 5 + n], refs[5 + n :]
    w_ref = w_refs[0]
    if n_w == 2:
        w_ref, refs = refs[0], refs[1:]

        @pl.when(pl.program_id(0) == 0)
        def _():
            order_rows(order_ref, *w_refs, w_ref)

    lse_ref, x_held, mix_ref, qc_ref = refs
    x_ref = gather_pieces(order_ref, x_refs, x_held)
    length, width = q_ref.shape[1], q_ref.shape[2]
    query_rows, key_rows = document_rows(seg_ref[0])
    qc_ref[0], kc_ref[0] = turned_rows(query_rows), turned_rows(key_rows)
    x = x_ref[0]
    q = dot_nn(x, w_ref[:, 0:width]).astype(bf16)
    q_ref[0] = q * jnp.asarray(HD**-0.5, bf16)
    k_ref[0] = dot_nn(x, w_ref[:, width : 2 * width]).astype(bf16)
    v_ref[0] = dot_nn(x, w_ref[:, 2 * width : 3 * width]).astype(bf16)
    block = min(BLOCK, length)
    heads = width // HD

    q_code, k_code = qc_ref[0], kc_ref[0]
    lane_half = first_half((length, PAIR), 1)
    row_half = first_half((PAIR, length), 0)
    out_half = first_half((PAIR, block), 0)
    causal = lax.broadcasted_iota(jnp.int32, (block, block), 0) <= lax.broadcasted_iota(jnp.int32, (block, block), 1)
    steps = [(pair, start, odd) for pair in range(width // PAIR) for start in range(0, length, block) for odd in (0, 1)]

    def sides_of(pair):
        lanes = slice(pair * PAIR, (pair + 1) * PAIR)
        q_pair, k_pair, v_pair = q_ref[0, :, lanes], k_ref[0, :, lanes], v_ref[0, :, lanes]
        v_turned = v_pair.T
        one = jnp.ones_like(v_turned)
        even = jnp.where(lane_half, q_pair, q_code), jnp.where(lane_half, k_pair, k_code), jnp.where(row_half, v_turned, one)
        odd = jnp.where(lane_half, q_code, q_pair), jnp.where(lane_half, k_code, k_pair), jnp.where(row_half, one, v_turned)
        return even, odd

    sides, ahead = {}, []

    def start_scores(step):
        pair, start, odd = step
        if pair not in sides:
            sides[pair] = sides_of(pair)
        qa, ka, _ = sides[pair][odd]
        ahead.append(dot_nt(ka[: start + block], qa[start : start + block]))

    for step in steps[:AHEAD]:
        start_scores(step)
    parts, logs = ([], []), ([], [])
    for i, (pair, start, odd) in enumerate(steps):
        if i + AHEAD < len(steps):
            start_scores(steps[i + AHEAD])
        scores = ahead.pop(0)
        last = jnp.where(causal, scores[start:], -FAR)
        scores = jnp.concatenate([scores[:start], last], axis=0) if start else last
        top = jnp.max(scores, axis=0, keepdims=True)
        weights = jnp.exp(scores - top).astype(bf16)
        out = dot_nn(sides[pair][odd][2][:, : start + block], weights)
        total = out[0:1] if odd else out[HD : HD + 1]
        parts[odd].append(out * (1.0 / total))
        logs[odd].append(top + jnp.log(total))
        if odd and start + block == length:
            for odd in (0, 1):
                lse_ref[2 * pair + odd : 2 * pair + odd + 1, :] = jnp.concatenate(logs[odd], axis=1)
            for at, (even, odd) in enumerate(zip(*parts)):
                mixed = jnp.where(out_half, even, odd)
                mix_ref[0, at * block : (at + 1) * block, pair * PAIR : (pair + 1) * PAIR] = mixed.T.astype(bf16)
            parts, logs = ([], []), ([], [])

    spread_pieces(order_ref, mix_refs, mix_ref)
    a_ref[0] = turned_rows(jnp.concatenate([query_rows, *split_three(-lse_ref[...])], axis=0))


def own_place(mine, n, at):
    return lambda s, order: ((order[0] * mine if n == 2 else 0) + at + s, 0, 0)


def attend_forward(order, at, count, pieces, w, segments, before):
    total, _, length = segments.shape
    width, n = pieces[0].shape[2], len(pieces)
    whole = lambda s, order: (0, 0)
    row = lambda s, order: (s, 0, 0)
    after = lambda s, order: (s + at, 0, 0)
    wide, narrow = pl.BlockSpec((1, length, width), row), pl.BlockSpec((1, length, PAIR), row)
    piece = lambda m: pl.BlockSpec((1, length // n, width), m)
    parts = [pl.BlockSpec((1, length // n, width), m) for m in (after, row)[:n]]
    full = lambda count, rows, cols: jax.ShapeDtypeStruct((count, rows, cols), bf16)
    ws = list(w) if isinstance(w, tuple) else [w]
    w_shape = (width, 3 * width)
    args = [order, *pieces, *ws, segments] + ([] if before is None else [before])
    out = pl.pallas_call(
        functools.partial(attend_forward_kernel, n, len(ws), before is not None),
        grid_spec=pltpu.PrefetchScalarGridSpec(
            num_scalar_prefetch=1,
            grid=(count,),
            in_specs=[piece(own_place(total, n, at)), piece(row)][:n]
            + [pl.BlockSpec(v.shape, lambda s, order, v=v: (0,) * v.ndim) for v in ws]
            + [pl.BlockSpec((1, 1, length), after)]
            + ([] if before is None else [pl.BlockSpec(memory_space=pl.ANY)]),
            out_specs=[wide, wide, wide, narrow, narrow] + parts + [pl.BlockSpec(w_shape, whole)] * (len(ws) - 1),
            scratch_shapes=[
                pltpu.VMEM((width // HD, length), f32),
                pltpu.VMEM((1, length, width), bf16),
                pltpu.VMEM((1, length, width), bf16),
                pltpu.VMEM((1, length, PAIR), bf16),
            ],
        ),
        out_shape=[full(count, length, width)] * 3
        + [full(count, length, PAIR)] * 2
        + [full(total, length // n, width), full(count, length // n, width)][:n]
        + [jax.ShapeDtypeStruct(w_shape, bf16)] * (len(ws) - 1),
        input_output_aliases={} if before is None else {len(args) - 1: 5},
        cost_estimate=work(count * length * width * (3 * width + 8 * length), count * length * width * 12),
        compiler_params=params(),
        name="attend_forward",
    )(*args)
    return out[:5], out[5:]


def attend_backward_kernel(n, begun, last, halves, *refs):
    order_ref, refs = refs[0], refs[1:]
    x_refs, mix_refs, go_refs = (refs[i * n : (i + 1) * n] for i in range(3))
    w_ref, q_ref, k_ref, v_ref, a_ref, kc_ref = refs[3 * n : 6 + 3 * n]
    refs = refs[6 + 3 * n :]
    if n == 2:
        gr_ref, refs = refs[0], refs[1:]
    if begun:
        before_ref, refs = refs[0], refs[1:]
    dx_refs, refs = refs[:n], refs[n:]
    if halves:
        kept_ref, refs = refs[0], refs[1:]
    dw_ref, grads, delta_ref, dq_ref, x_held, mix_held, go_held, dw_sum, dx_held, w_held, sems = refs
    step = pl.program_id(0)
    fetched = [pltpu.make_async_copy(w_ref, w_held, sems.at[0])]
    if begun:
        fetched.append(pltpu.make_async_copy(before_ref, dw_sum, sems.at[1]))

    @pl.when(step == 0)
    def _():
        for copy in fetched:
            copy.start()
        if not begun:
            dw_sum[...] = jnp.zeros_like(dw_sum)

    x_ref = gather_pieces(order_ref, x_refs, x_held)
    mix_ref = gather_pieces(order_ref, mix_refs, mix_held)
    go_ref = gather_pieces(order_ref, go_refs, go_held)
    length, width = q_ref.shape[1], q_ref.shape[2]
    block = min(BLOCK, length)

    product = go_ref[0].astype(f32) * mix_ref[0].astype(f32)
    high = product.astype(bf16)
    low = (product - high.astype(f32)).astype(bf16)
    lane = lax.broadcasted_iota(jnp.int32, (width, PAIR), 1) % HD
    head = lax.broadcasted_iota(jnp.int32, (width, PAIR), 0) // HD
    third = lane - EXTRA - head
    picks = ((third == 0) | (third == HEADS) | (third == 2 * HEADS)).astype(f32).astype(bf16)
    delta = -(dot_nn(high, picks) + dot_nn(low, picks))
    high, middle, low = split_three(delta)
    lane = lax.broadcasted_iota(jnp.int32, (length, PAIR), 1) % HD
    delta_ref[...] = jnp.where(
        lane < EXTRA + HEADS, high, jnp.where(lane < EXTRA + 2 * HEADS, middle, low)
    ).astype(bf16)

    a, k_code, minus = a_ref[0], kc_ref[0], delta_ref[...]
    lane_half = first_half((length, PAIR), 1)
    row_half = first_half((PAIR, block), 0)
    causal = lax.broadcasted_iota(jnp.int32, (block, block), 0) >= lax.broadcasted_iota(jnp.int32, (block, block), 1)
    blocks = [(pair, start, odd) for pair in range(width // PAIR) for start in range(0, length, block) for odd in (0, 1)]

    def sides_of(pair):
        lanes = slice(pair * PAIR, (pair + 1) * PAIR)
        q_pair, k_pair, v_pair, go_pair = (r[0, :, lanes] for r in (q_ref, k_ref, v_ref, go_ref))
        sides = []
        for odd in (0, 1):
            mine = head_lanes(2 * pair + odd)
            both = ((q_pair, a), (k_pair, k_code + mine), (v_pair, jnp.broadcast_to(mine, v_pair.shape)), (go_pair, minus))
            sides.append([jnp.where(lane_half, other, own) if odd else jnp.where(lane_half, own, other) for own, other in both])
        return sides, q_pair.T, go_pair.T, k_pair

    sides, ahead = {}, []

    def start_products(at):
        pair, start, odd = at
        if pair not in sides:
            sides[pair] = sides_of(pair)
        qa, ka, va, ga = sides[pair][0][odd]
        stop = start + block
        ahead.append((dot_nt(qa[start:], ka[start:stop]), dot_nt(ga[start:], va[start:stop])))

    for at in blocks[:BACK_AHEAD]:
        start_products(at)
    dk, dv = ([], []), ([], [])
    for i, (pair, start, odd) in enumerate(blocks):
        if i + BACK_AHEAD < len(blocks):
            start_products(blocks[i + BACK_AHEAD])
        scores, dprobs = ahead.pop(0)
        _, q_turned, go_turned, k_pair = sides[pair]
        stop = start + block
        first = jnp.where(causal, scores[:block], -FAR)
        scores = jnp.concatenate([first, scores[block:]], axis=0) if stop < length else first
        probs = jnp.exp(scores)
        dscores = (probs * dprobs).astype(bf16)
        dv[odd].append(dot_nn(go_turned[:, start:], probs.astype(bf16)))
        dk[odd].append(dot_nn(q_turned[:, start:], dscores))
        dq_at = dot_nn(dscores, k_pair[start:stop])
        slot = 2 * (pair % 2) + odd
        if start:
            dq_ref[slot, start:, :] += dq_at
        else:
            dq_ref[slot] = dq_at
        if odd and stop == length:
            lanes = pair * PAIR
            dq = jnp.where(lane_half, dq_ref[slot - 1], dq_ref[slot]) * HD**-0.5
            grads[:, lanes : lanes + PAIR] = dq.astype(bf16)
            for value, third in ((dk, 1), (dv, 2)):
                to = third * width + lanes
                for at, (even, odd) in enumerate(zip(*value)):
                    turned = jnp.where(row_half, even, odd).T.astype(bf16)
                    grads[at * block : (at + 1) * block, to : to + PAIR] = turned
            dk, dv = ([], []), ([], [])

    @pl.when(step == 0)
    def _():
        for copy in fetched:
            copy.wait()

    dw_sum[...] += dot_tn(x_ref[0], grads[...])
    dx_held[0] = dot_nt(grads[...], w_held[...])
    if n == 2:
        rows = length // n
        pick = lambda i: dx_held[0, pl.ds(pl.multiple_of(order_ref[i] * rows, rows), rows), :]
        dx_refs[0][0] = gr_ref[0] + pick(0)
        dx_refs[1][0] = pick(1).astype(bf16)
    else:
        dx_refs[0][0] = dx_held[0].astype(bf16)

    @pl.when(step == pl.num_programs(0) - 1)
    def _():
        if halves:
            pairs, parts, rows, cols = dw_ref.shape
            cols //= 3
            for ref, core in ((kept_ref, order_ref[4]), (dw_ref, 1 - order_ref[4])):
                for i in range(pairs):
                    at = pl.ds(pl.multiple_of((2 * i + core) * rows, rows), rows)
                    for part in range(parts):
                        for third in range(3):
                            start = third * width + part * cols
                            block = dw_sum[at, start : start + cols].astype(bf16)
                            ref[i, part, :, third * cols : (third + 1) * cols] = block
        elif last:
            owners, parts, rows, cols = dw_ref.shape
            cols //= 3
            for part in range(parts):
                for third in range(3):
                    start = third * width + part * cols
                    block = dw_sum[:, start : start + cols].astype(bf16)
                    dw_ref[:, part, :, third * cols : (third + 1) * cols] = block.reshape(owners, rows, cols)
        else:
            copy = pltpu.make_async_copy(dw_sum, dw_ref, sems.at[1])
            copy.start()
            copy.wait()


def attend_backward(order, at, mine, x, mix, go, w, kept, grad_r1, before, last, halves=False):
    count, length = kept[0].shape[:2]
    width, n = w.shape[0], len(x)
    row = lambda s, order: (s, 0, 0)
    wide, narrow = pl.BlockSpec((1, length, width), row), pl.BlockSpec((1, length, PAIR), row)
    anywhere = pl.BlockSpec(memory_space=pl.ANY)
    piece = lambda m: pl.BlockSpec((1, length // n, width), m)
    part, held, own = piece(row), piece(own_place(mine, n, at)), piece(lambda s, order: (s + at, 0, 0))
    args = [order, *x, *mix, *go, w, *kept]
    specs = [held, part][:n] + [own, part][:n] * 2 + [anywhere, wide, wide, wide, narrow, narrow]
    weight_out, dw_shape = anywhere, jax.ShapeDtypeStruct(w.shape, f32)
    if last:
        weight_out = pl.BlockSpec(last, lambda s, order: (0, 0, 0, 0))
        dw_shape = jax.ShapeDtypeStruct(last, bf16)
    dw_specs, dw_shapes = [weight_out], [dw_shape]
    if halves:
        half = (last[0] // 2,) + last[1:]
        dw_specs = [pl.BlockSpec(half, lambda s, order: (0, 0, 0, 0))] * 2
        dw_shapes = [jax.ShapeDtypeStruct(half, bf16)] * 2
    dx_specs, dx_shapes = [part], [jax.ShapeDtypeStruct((count, length // n, width), bf16)]
    alias = {}
    if n == 2:
        alias[len(args)] = 0
        args.append(grad_r1)
        specs.append(held)
        dx_specs, dx_shapes = [held] + dx_specs, [jax.ShapeDtypeStruct(grad_r1.shape, f32)] + dx_shapes
    if before is not None:
        args.append(before)
        specs.append(anywhere)
    out = pl.pallas_call(
        functools.partial(attend_backward_kernel, n, before is not None, last, halves),
        grid_spec=pltpu.PrefetchScalarGridSpec(
            num_scalar_prefetch=1,
            grid=(count,),
            in_specs=specs,
            out_specs=dx_specs + dw_specs,
            scratch_shapes=[
                pltpu.VMEM((length, 3 * width), bf16),
                pltpu.VMEM((length, PAIR), bf16),
                pltpu.VMEM((4, length, PAIR), f32),
                pltpu.VMEM((1, length, width), bf16),
                pltpu.VMEM((1, length, width), bf16),
                pltpu.VMEM((1, length, width), bf16),
                pltpu.VMEM(w.shape, f32),
                pltpu.VMEM((1, length, width), f32),
                pltpu.VMEM(w.shape, bf16),
                pltpu.SemaphoreType.DMA((2,)),
            ],
        ),
        out_shape=dx_shapes + dw_shapes,
        input_output_aliases=alias,
        cost_estimate=work(count * length * width * (6 * width + 16 * length), count * length * width * 20),
        compiler_params=params(),
        name="attend_backward",
    )(*args)
    return out[:n], tuple(out[n:]) if halves else out[n]


def normalize(rows):
    center = rows - jnp.mean(rows, axis=-1, keepdims=True)
    rstd = lax.rsqrt(jnp.mean(center * center, axis=-1, keepdims=True) + norm_eps)
    return center * rstd, rstd


def normalize_back(grad, xhat, rstd, gain):
    scaled = grad * gain
    return rstd * (
        scaled - jnp.mean(scaled, axis=-1, keepdims=True) - xhat * jnp.mean(scaled * xhat, axis=-1, keepdims=True)
    )


def token_kernel(sizes, parts, begun, last, *refs):
    n, step = len(sizes), pl.program_id(0)
    order_ref, x_ref, d_ref, cx_ref, cd_ref = refs[:5]
    mix_refs, (in_ref, back_ref, out_parts_ref, norm_ref), refs = refs[5 : 5 + n], refs[5 + n : 9 + n], refs[9 + n :]
    if begun:
        sums_in, ng_in, refs = refs[3], refs[4], refs[5:]
    xo_ref, do_ref, gr_ref = refs[:3]
    gm_refs, refs = refs[3 : 3 + n], refs[3 + n :]
    if last:
        packed_ref, refs = refs[0], refs[1:]
    else:
        sums_out, ng_out, refs = refs[0], refs[1], refs[2:]
    act_ref, slope, out_ref, sums, ng_ref, sems = refs
    width, hidden = in_ref.shape
    n_out = width // parts
    chunk = min(CHUNK, hidden)
    columns = [slice(at, at + chunk) for at in range(0, hidden, chunk)]
    back_columns = [slice(hidden + at, hidden + at + chunk) for at in range(0, hidden, chunk)]
    out_columns = slice(2 * hidden, 2 * hidden + width)
    starts = [sum(sizes[:i]) for i in range(n)]

    @pl.when(step == 0)
    def _():
        if begun:
            pltpu.make_async_copy(sums_in, sums, sems.at[0]).start()
            ng_ref[...] = ng_in[...]
        else:
            sums[...] = jnp.zeros_like(sums)
            ng_ref[...] = jnp.zeros_like(ng_ref)
        for i in range(parts):
            if n_out % PAIR:
                out_ref[:, i * n_out : (i + 1) * n_out] = out_parts_ref[:, i * n_out : (i + 1) * n_out]
            else:
                to = pl.ds(pl.multiple_of(order_ref[i] * n_out, PAIR), n_out)
                out_ref[:, to] = out_parts_ref[:, i * n_out : (i + 1) * n_out]
    turned = norm_ref[...].astype(f32).T
    g1, b1, g2, b2 = (turned[i : i + 1] for i in range(4))
    mix = mix_refs[0][0]
    for ref, start in zip(mix_refs[1:], starts[1:]):
        mix = jnp.where(step >= start, ref[0], mix)
    attended = dot_nt(mix, out_ref[...])
    xhat1, rstd1 = normalize(x_ref[0].astype(f32) + attended)
    x_one = xhat1 * g1 + b1
    xb = x_one.astype(bf16)
    feed, h = None, dot_nn(xb, in_ref[:, columns[0]])
    for i, cols in enumerate(columns):
        ahead = dot_nn(xb, in_ref[:, columns[i + 1]]) if i + 1 < len(columns) else None
        cdf = 0.5 * lax.erf(h * 0.7071067811865476) + 0.5
        active = (h * cdf).astype(bf16)
        act_ref[:, cols] = active
        slope[:, cols] = cdf + h * (jnp.exp(-0.5 * (h * h)) * 0.3989422804014327)
        product = dot_nt(active, back_ref[:, cols])
        feed = product if feed is None else feed + product
        h = ahead
    xhat2, rstd2 = normalize(x_one + feed)
    xo_ref[0] = (xhat2 * g2 + b2).astype(bf16)
    do_ref[0] = (d_ref[0].astype(f32) + attended + feed).astype(bf16)
    cx, cd = cx_ref[0].astype(f32), cd_ref[0].astype(f32)
    grad_r2 = normalize_back(cx, xhat2, rstd2, g2)
    dg2, db2 = jnp.sum(cx * xhat2, axis=0, keepdims=True), jnp.sum(cx, axis=0, keepdims=True)
    gf = (grad_r2 + cd).astype(bf16)

    if begun:

        @pl.when(step == 0)
        def _():
            pltpu.make_async_copy(sums_in, sums, sems.at[0]).wait()

    gf_turned, xb_turned = gf.T, xb.T
    grad_x1, ga = grad_r2, dot_nn(gf, back_ref[:, columns[0]])
    for i, cols in enumerate(columns):
        ahead = dot_nn(gf, back_ref[:, columns[i + 1]]) if i + 1 < len(columns) else None
        gh = (ga * slope[:, cols]).astype(bf16)
        grad_x1 = grad_x1 + dot_nt(gh, in_ref[:, cols])
        sums[:, cols] += dot_nn(xb_turned, gh)
        ga = ahead

    if not last:
        early = pltpu.make_async_copy(sums.at[:, pl.ds(0, hidden)], sums_out.at[:, pl.ds(0, hidden)], sems.at[1])

        @pl.when(step == pl.num_programs(0) - 1)
        def _():
            early.start()

    for cols, to in zip(columns, back_columns):
        sums[:, to] += dot_nn(gf_turned, act_ref[:, cols])
    grad_r1 = normalize_back(grad_x1, xhat1, rstd1, g1)
    gr_ref[0] = grad_r1
    dg1, db1 = jnp.sum(grad_x1 * xhat1, axis=0, keepdims=True), jnp.sum(grad_x1, axis=0, keepdims=True)
    ng_ref[...] += jnp.concatenate([dg1, db1, dg2, db2, jnp.zeros((4, dg1.shape[1]), f32)], axis=0)
    gb = (grad_r1 + cd).astype(bf16)
    gm = dot_nn(gb, out_ref[...]).astype(bf16)
    sums[:, out_columns] += dot_tn(gb, mix)
    for ref, start, size in zip(gm_refs, starts, sizes):

        @pl.when((step >= start) & (step < start + size))
        def _(ref=ref):
            ref[0] = gm

    @pl.when(step == pl.num_programs(0) - 1)
    def _():
        if last:
            n_hidden = hidden // parts
            rest = jnp.zeros((PAIR - ng_ref.shape[0], width), f32)
            norms = jnp.concatenate([ng_ref[...], rest], axis=0).T
            for i in range(parts):
                to = 0
                own = lambda start, size: sums[:, start + i * size : start + (i + 1) * size]
                if n_out % PAIR:
                    out = own(2 * hidden, n_out)
                else:
                    out = sums[:, pl.ds(pl.multiple_of(2 * hidden + order_ref[i] * n_out, PAIR), n_out)]
                for value in (own(0, n_hidden), own(hidden, n_hidden), norms, out):
                    size = value.shape[1]
                    packed_ref[i, :, to : to + size] = value.astype(bf16)
                    to += size
        else:
            ng_out[...] = ng_ref[...]
            rest = pl.ds(hidden, hidden + width)
            copy = pltpu.make_async_copy(sums.at[:, rest], sums_out.at[:, rest], sems.at[0])
            copy.start()
            copy.wait()
            early.wait()


def token_block(order, places, mixes, x, d, cot_x, cot_d, weights, hidden, parts, before, last):
    (total, rows, width), sizes = x.shape, [m.shape[0] for m in mixes]
    n_hidden, n_out = hidden // parts, width // parts
    starts = [sum(sizes[:i]) for i in range(len(sizes))]

    def there(s, order):
        at = places[0](order) + s
        for start, place in zip(starts[1:], places[1:]):
            at = jnp.where(s < start, at, place(order) + s - start)
        return at, 0, 0

    whole = lambda s, order: (0, 0)
    one = (1, rows, width)
    full = lambda count, dtype: jax.ShapeDtypeStruct((count, rows, width), dtype)

    def within(i):
        return pl.BlockSpec(one, lambda s, order: (jnp.clip(s - starts[i], 0, sizes[i] - 1), 0, 0))

    anywhere, ng = pl.BlockSpec(memory_space=pl.ANY), pl.BlockSpec((8, width), whole)
    mix_specs = [within(i) for i in range(len(mixes))]
    sums = jax.ShapeDtypeStruct((width, 2 * hidden + width), f32)
    packed = (parts, width, 2 * n_hidden + PAIR + -(-n_out // PAIR) * PAIR)
    if last:
        sum_specs, sum_shapes = [pl.BlockSpec(packed, lambda s, order: (0, 0, 0))], [jax.ShapeDtypeStruct(packed, bf16)]
    else:
        sum_specs, sum_shapes = [anywhere, ng], [sums, jax.ShapeDtypeStruct((8, width), f32)]
    window = lambda cols, at: pl.BlockSpec((width, cols), lambda s, order: (0, at // cols))
    windows = [window(hidden, 0), window(hidden, hidden), window(width, 2 * hidden), window(PAIR, 2 * hidden + width)]
    at = 9 + len(mixes)
    count = sum(sizes)
    out = pl.pallas_call(
        functools.partial(token_kernel, tuple(sizes), parts, bool(before), last),
        grid_spec=pltpu.PrefetchScalarGridSpec(
            num_scalar_prefetch=1,
            grid=(count,),
            in_specs=[pl.BlockSpec(one, there)] * 4
            + mix_specs
            + windows
            + ([anywhere] * 4 + [ng] if before else []),
            out_specs=[pl.BlockSpec(one, there)] * 3 + mix_specs + sum_specs,
            scratch_shapes=[pltpu.VMEM((rows, hidden), bf16), pltpu.VMEM((rows, hidden), f32)]
            + [pltpu.VMEM((width, width), bf16), pltpu.VMEM(sums.shape, f32), pltpu.VMEM((8, width), f32), pltpu.SemaphoreType.DMA((2,))],
        ),
        out_shape=[full(total, bf16), full(total, bf16), full(total, f32)] + [full(c, bf16) for c in sizes] + sum_shapes,
        input_output_aliases={at + i: i for i in range(3)} if before else {},
        cost_estimate=work(count * rows * width * (9 * hidden + 3 * width), count * rows * width * 20),
        compiler_params=params(),
        name="token_block",
    )(order, x, d, cot_x, cot_d, *mixes, *[weights] * 4, *before)
    return out[:3] + out[3 + len(mixes) :], out[3 : 3 + len(mixes)]


def exchange(value, over_dp, over_mp):
    perm = [(i, i ^ (2 * over_dp + over_mp)) for i in range(32)]
    return lax.ppermute(value, ("dp", "mp"), perm)


PLANE = ((0, 0), (2, 0), (0, 1), (2, 1))


def place():
    dp, mp = lax.axis_index("dp"), lax.axis_index("mp")
    return dp >> 2, (dp >> 1) & 1, dp & 1, mp


def gather_by_steps(shard, sends, first, arrange, early):
    plane = jnp.stack([shard] + [exchange(shard, *step) for step in PLANE[1:]])
    plane, sends, first = lax.optimization_barrier((plane, sends, swap(first)))
    first = arrange(first)
    half = max(sends[0].shape[0] // 2, 1)
    got, rest = swap(sends[0][:half]), [swap(v) for v in (sends[0][half:],) if v.shape[0]]
    line = [exchange(plane, 4 * k, 0) for k in (1, 2, 3)]
    plane, got, first, early = lax.optimization_barrier((jnp.stack([plane] + line), got, first, early))
    other, rest = lax.optimization_barrier((exchange(plane, 1, 0), rest))
    got = jnp.concatenate([got] + rest, axis=0)
    return plane, other, [got] + [swap(v) for v in sends[1:]], first, early


def scatter_by_steps(kept, sent, dx, last):
    z, x, _, m = place()
    rows, cols = kept.shape[2:]
    pick = lambda v, i, axis: lax.dynamic_index_in_dim(v, i, axis=axis, keepdims=False)
    got, dx = lax.optimization_barrier((exchange(sent, 1, 0), dx))
    dx = swap(dx)
    total = (kept.astype(f32) + got.astype(f32)).reshape(4, 2, 2, rows, cols)
    total = pick(total, x, 1) + exchange(pick(total, 1 - x, 1).astype(bf16), 2, 0).astype(f32)
    got = [exchange(pick(total, z ^ k, 0).astype(bf16), 4 * k, 0) for k in (1, 2, 3)]
    total = sum((g.astype(f32) for g in got), pick(total, z, 0))
    total, dx = lax.optimization_barrier((total, dx))
    sent = jnp.concatenate([pick(total, 1 - m, 0).astype(bf16), last], axis=1)
    return pick(total, m, 0), swap(sent), dx


RATES = (0.05, 0.3, 0.05, 0.025, 0.1)


def update_kernel(own_ref, token_ref, got_ref, *refs):
    states, outs = refs[:15], refs[15:]
    cols = own_ref.shape[1]
    n_in, n_back, n_out = states[6].shape[1], states[9].shape[1], states[3].shape[1]
    qkv = own_ref[...] + got_ref[:, :cols].astype(f32)
    token = lambda at, size: token_ref[0, :, at : at + size].astype(f32) + got_ref[:, cols + at : cols + at + size].astype(f32)
    norm_at = n_in + n_back
    grads = (
        qkv,
        token(norm_at + PAIR, n_out),
        token(0, n_in),
        token(n_in, n_back),
        token(norm_at, PAIR).T[: states[12].shape[0]],
    )
    for i, (grad, rate) in enumerate(zip(grads, RATES)):
        weight, mom, sec = states[3 * i : 3 * i + 3]
        mine = outs[3 * i : 3 * i + 3]
        if i:
            for ref, value in zip(mine, adam_update(weight[...], grad, mom[...], sec[...], rate)):
                ref[...] = value
        else:
            size = cols // 3
            for third in range(3):
                part = grad[:, third * size : (third + 1) * size]
                for ref, value in zip(mine, adam_update(weight[third], part, mom[third], sec[third], rate)):
                    ref[third] = value


def update(own, token, got, states):
    vmem = pl.BlockSpec(memory_space=pltpu.VMEM)
    return pl.pallas_call(
        update_kernel,
        in_specs=[vmem] * (3 + len(states)),
        out_specs=[vmem] * len(states),
        out_shape=[jax.ShapeDtypeStruct(v.shape, f32) for v in states],
        compiler_params=params(),
        name="update",
    )(own, token, got, *states)


def adam_update(weight, grad, mom, sec, rate):
    mom_new = beta_first * mom + (1.0 - beta_first) * grad
    sec_new = beta_second * sec + (1.0 - beta_second) * grad * grad
    scaled = (
        mom_new
        / (1.0 - beta_first**STEP)
        / (jnp.sqrt(sec_new / (1.0 - beta_second**STEP)) + adam_eps)
    )
    return (mom_new, sec_new, weight - rate * (scaled + decay_rate * weight))


def swap(value):
    return lax.ppermute(value, "mp", [(0, 1), (1, 0)])


def on_device(
    x_in,
    d_in,
    segments,
    cot_x,
    cot_d,
    w_qkv,
    w_out,
    w_in,
    w_back,
    norms,
    qkv_mom,
    qkv_sec,
    out_mom,
    out_sec,
    in_mom,
    in_sec,
    back_mom,
    back_sec,
    norm_mom,
    norm_sec,
):
    parts, owners = lax.axis_size("mp"), lax.axis_size("dp")
    me = lax.axis_index("mp")
    total, rows, width = x_in.shape
    mine = total // parts
    length = rows * parts
    own_rows, _, qkv_n = w_qkv.shape
    n_out, n_in, n_back = w_out.shape[0], w_in.shape[1], w_back.shape[0]
    hidden = parts * n_in
    here = lambda v, start, count: lax.dynamic_slice_in_dim(v, start, count, axis=0)
    by_steps = (owners, parts) == (16, 2)

    order = jnp.arange(parts, dtype=jnp.int32)
    own_segments = here(segments, me * mine, mine).reshape(mine, 1, length)

    if parts == 2:
        other = 1 - me
        step = max(mine // 2, 1)
        chunks = list(range(0, mine, step))
        send_x = [here(x_in, other * mine + at, step) for at in chunks]
        order = jnp.stack([me, other, *place()]).astype(jnp.int32)
    shard = jnp.concatenate([w_in, w_back.T, w_out.T], axis=1).astype(bf16)

    def arrange(shards):
        columns = zip(*(jnp.split(v, [n_in, n_in + n_back], axis=1) for v in shards))
        columns = [c for kind in columns for c in kind]
        columns.append(jnp.pad(norms.T.astype(bf16), ((0, 0), (0, PAIR - norms.shape[0]))))
        return jnp.concatenate(columns, axis=1)

    if by_steps:
        shard_qkv = w_qkv.astype(bf16).reshape(own_rows, 3 * qkv_n)
        early = own_segments, order
        plane, got, got_x, columns, early = gather_by_steps(
            shard_qkv, send_x, shard, lambda theirs: arrange([shard, theirs]), early
        )
        qkv, (own_segments, order) = (plane, got), early
    else:
        got = lax.all_gather(w_qkv.astype(bf16), ("dp", "mp"), axis=0)
        got = got.reshape(owners, parts, own_rows, 3, qkv_n)
        qkv = got.transpose(0, 2, 3, 1, 4).reshape(width, 3 * width)
        got_x = [swap(v) for v in send_x] if parts == 2 else None
        columns = arrange([shard, swap(shard)] if parts == 2 else list(lax.all_gather(shard, "mp", axis=0)))
    weights = lax.all_gather(columns, "dp", axis=0, tiled=True)

    qkv_shape = (owners, parts, own_rows, 3 * qkv_n)

    def tokens(places, mixes, before, last):
        return token_block(order, places, mixes, x_in, d_in, cot_x, cot_d, weights, hidden, parts, before, last)

    if parts == 2:
        forward, own_mix = [], None
        for i, at in enumerate(chunks):
            x = (x_in, got_x[i])
            kept, (own_mix, sent, *made) = attend_forward(order, at, step, x, qkv, own_segments, own_mix)
            qkv = made[0] if made else qkv
            forward.append((x, kept, sent, swap(sent)))
        before, got_gm = (), []
        for i, at in enumerate(chunks):
            mixes, places = [forward[i][3]], [lambda order, at=at: order[1] * mine + at]
            if i == 0:
                mixes, places = [own_mix] + mixes, [lambda order: order[0] * mine] + places
            before, gms = tokens(places, mixes, before, i == len(chunks) - 1)
            own_gm = gms[0] if i == 0 else own_gm
            got_gm.append(swap(gms[-1]))
        x_out, d_out, x_grad, packed = before
        qkv_grad, got_dx = None, []
        for i, at in enumerate(chunks):
            x, kept, sent, _ = forward[i]
            last = qkv_shape if i == len(chunks) - 1 else None
            (x_grad, dx), qkv_grad = attend_backward(
                order, at, mine, x, (own_mix, sent), (own_gm, got_gm[i]), qkv, kept, x_grad, qkv_grad, last, by_steps and last is not None
            )
            if got_dx:
                qkv_grad, got_dx[-1] = lax.optimization_barrier((qkv_grad, got_dx[-1]))
            got_dx.append(dx if last else swap(dx))
    else:

        def to_sequences(v):
            got = lax.all_to_all(v.reshape(parts, mine, rows, width), "mp", 0, 0)
            return got.transpose(1, 0, 2, 3).reshape(mine, length, width)

        def to_positions(v):
            sent = v.reshape(mine, parts, rows, width).transpose(1, 0, 2, 3)
            return lax.all_to_all(sent, "mp", 0, 0).reshape(total, rows, width)

        x = (to_sequences(x_in),)
        kept, (mix,) = attend_forward(order, 0, mine, x, qkv, own_segments, None)
        (x_out, d_out, grad_r1, packed), (gm,) = tokens([lambda order: 0], [to_positions(mix)], (), True)
        go = (to_sequences(gm),)
        (dx,), qkv_grad = attend_backward(order, 0, mine, x, (mix,), go, qkv, kept, None, None, qkv_shape)
        x_grad = grad_r1 + to_positions(dx).astype(f32)

    got = lax.psum_scatter(packed, "dp", scatter_dimension=1, tiled=True)

    states = (
        (w_qkv, qkv_mom, qkv_sec),
        (w_out, out_mom, out_sec),
        (w_in, in_mom, in_sec),
        (w_back, back_mom, back_sec),
        (norms, norm_mom, norm_sec),
    )
    if by_steps:
        own, theirs, got_dx[-1] = scatter_by_steps(*qkv_grad, got_dx[-1], got[1])
        turns = ((1, 0, 2), (1, 0), (0, 1), (1, 0), (0, 1))
        turned = [v.transpose(turn) for state, turn in zip(states, turns) for v in state]
        new = update(own, got, theirs, turned)
        new = [v.transpose(turns[i // 3]) for i, v in enumerate(new)]
    else:
        if parts == 2:
            got_dx[-1] = swap(got_dx[-1])
            grads = got[0].astype(f32) + swap(got[1]).astype(f32)
        else:
            grads = lax.psum_scatter(got, "mp", scatter_dimension=0, tiled=True)[0].astype(f32)
        in_g, back_g, norm_g, out_g = jnp.split(grads, [n_in, n_in + n_back, n_in + n_back + PAIR], axis=1)
        got = lax.psum_scatter(qkv_grad.reshape(owners, -1), "dp", scatter_dimension=0, tiled=True)
        qkv_g = lax.psum_scatter(got, "mp", scatter_dimension=1, tiled=True).astype(f32)
        grads = (qkv_g.reshape(own_rows, 3, qkv_n), out_g[:, :n_out].T, in_g, back_g.T, norm_g[:, : norms.shape[0]].T)
        new = [v for (w, m, v), g, rate in zip(states, grads, RATES) for v in adam_update(w, g, m, v, rate)]
    if parts == 2:
        for at, dx in zip(chunks, got_dx):
            at = other * mine + at
            added = here(x_grad, at, step) + dx.astype(f32)
            x_grad = lax.dynamic_update_slice_in_dim(x_grad, added, at, axis=0)
    return (x_out, d_out, x_grad, *new)


def solution(mesh):
    stream = P("dp", "mp", None)
    weights = (P("dp", None, "mp"), P("mp", "dp"), P("dp", "mp"), P("mp", "dp"), P(None, "dp"))
    states = tuple(spec for spec in weights for _ in range(2))
    news = tuple(spec for spec in weights for _ in range(3))
    return jax.shard_map(
        on_device,
        mesh=mesh,
        in_specs=(stream, stream, P("dp", None), stream, stream) + weights + states,
        out_specs=(stream, stream, stream) + news,
        check_vma=False,
    )
```

```python
import functools

import jax
import jax.numpy as jnp
from jax import lax
from jax.experimental import pallas as pl
from jax.experimental.pallas import tpu as pltpu
from jax.sharding import PartitionSpec as P

STEP = 5
HD = 64
PAIR = 2 * HD
BLOCK = 256
CHUNK = 512
AHEAD = 4
BACK_AHEAD = 2
VMEM = 60 * 1024 * 1024

norm_eps = 1e-05
beta_first = 0.5
beta_second = 0.5
adam_eps = 1e-08
decay_rate = 0.01

FAR = 2.0**40
BITS = 7
EXTRA = 16
HEADS = 8

bf16 = jnp.bfloat16
f32 = jnp.float32


def dot_nn(a, b):
    return lax.dot_general(a, b, (((1,), (0,)), ((), ())), preferred_element_type=f32)


def dot_nt(a, b):
    return lax.dot_general(a, b, (((1,), (1,)), ((), ())), preferred_element_type=f32)


def dot_tn(a, b):
    return lax.dot_general(a, b, (((0,), (0,)), ((), ())), preferred_element_type=f32)


def params(**kw):
    return pltpu.CompilerParams(vmem_limit_bytes=VMEM, **kw)


def work(products, moved, exps=0):
    return pl.CostEstimate(flops=int(2 * products), bytes_accessed=int(moved), transcendentals=int(exps))


def split_three(value):
    high = value.astype(bf16).astype(f32)
    rest = value - high
    middle = rest.astype(bf16).astype(f32)
    return high, middle, (rest - middle).astype(bf16).astype(f32)


def document_rows(segments):
    row = lax.broadcasted_iota(jnp.int32, (EXTRA, segments.shape[1]), 0)
    bit = (segments >> jnp.where(row < BITS, row, row - BITS)) & 1
    used = row < 2 * BITS
    query = jnp.where(used, jnp.where(row < BITS, bit, 1 - bit), 0)
    key = jnp.where(used, jnp.where(row < BITS, 1 - bit, bit), 0)
    return query.astype(f32), key.astype(f32) * -FAR


def turned_rows(rows):
    rows = jnp.concatenate([rows, jnp.zeros((HD - rows.shape[0], rows.shape[1]), f32)], axis=0)
    return jnp.concatenate([rows, rows], axis=0).T.astype(bf16)


def first_half(shape, axis):
    return lax.broadcasted_iota(jnp.int32, shape, axis) < HD


def head_lanes(head):
    lane = lax.broadcasted_iota(jnp.int32, (1, PAIR), 1) % HD
    mine = (lane == EXTRA + head) | (lane == EXTRA + HEADS + head) | (lane == EXTRA + 2 * HEADS + head)
    return mine.astype(f32).astype(bf16)


def gather_pieces(order_ref, refs, held):
    if len(refs) == 1:
        return refs[0]
    rows = refs[0].shape[1]
    for i, ref in enumerate(refs):
        held[0, pl.ds(pl.multiple_of(order_ref[i] * rows, rows), rows), :] = ref[0]
    return held


def spread_pieces(order_ref, refs, value_ref):
    rows = refs[0].shape[1]
    for i, ref in enumerate(refs):
        ref[0] = value_ref[0, pl.ds(pl.multiple_of(order_ref[i] * rows, rows), rows), :]


def order_rows(order_ref, own_ref, got_ref, w_ref):
    z0, x0, c0, m0 = (order_ref[2 + i] for i in range(4))
    rows, cols = own_ref.shape[2], own_ref.shape[3] // 3
    for c in range(2):
        for source, here in ((own_ref, c0), (got_ref, 1 - c0)):

            @pl.when(here == c)
            def _(source=source, c=c):
                for z in range(4):
                    for x in range(2):
                        for m in range(2):
                            block = source[z ^ z0, (x ^ x0) + 2 * (m ^ m0)]
                            at = ((z * 2 + x) * 2 + c) * rows
                            for third in range(3):
                                to = third * 2 * cols + m * cols
                                w_ref[at : at + rows, to : to + cols] = block[:, third * cols : (third + 1) * cols]


def attend_forward_kernel(n, n_w, begun, *refs):
    order_ref, refs = refs[0], refs[1:]
    x_refs, w_refs, seg_ref = refs[:n], refs[n : n + n_w], refs[n + n_w]
    refs = refs[1 + n + n_w + begun :]
    q_ref, k_ref, v_ref, a_ref, kc_ref = refs[:5]
    mix_refs, refs = refs[5 : 5 + n], refs[5 + n :]
    w_ref = w_refs[0]
    if n_w == 2:
        w_ref, refs = refs[0], refs[1:]

        @pl.when(pl.program_id(0) == 0)
        def _():
            order_rows(order_ref, *w_refs, w_ref)

    lse_ref, x_held, mix_ref, qc_ref = refs
    x_ref = gather_pieces(order_ref, x_refs, x_held)
    length, width = q_ref.shape[1], q_ref.shape[2]
    query_rows, key_rows = document_rows(seg_ref[0])
    qc_ref[0], kc_ref[0] = turned_rows(query_rows), turned_rows(key_rows)
    x = x_ref[0]
    q = dot_nn(x, w_ref[:, 0:width]).astype(bf16)
    q_ref[0] = q * jnp.asarray(HD**-0.5, bf16)
    k_ref[0] = dot_nn(x, w_ref[:, width : 2 * width]).astype(bf16)
    v_ref[0] = dot_nn(x, w_ref[:, 2 * width : 3 * width]).astype(bf16)
    block = min(BLOCK, length)
    heads = width // HD

    q_code, k_code = qc_ref[0], kc_ref[0]
    lane_half = first_half((length, PAIR), 1)
    row_half = first_half((PAIR, length), 0)
    out_half = first_half((PAIR, block), 0)
    causal = lax.broadcasted_iota(jnp.int32, (block, block), 0) <= lax.broadcasted_iota(jnp.int32, (block, block), 1)
    steps = [(pair, start, odd) for pair in range(width // PAIR) for start in range(0, length, block) for odd in (0, 1)]

    def sides_of(pair):
        lanes = slice(pair * PAIR, (pair + 1) * PAIR)
        q_pair, k_pair, v_pair = q_ref[0, :, lanes], k_ref[0, :, lanes], v_ref[0, :, lanes]
        v_turned = v_pair.T
        one = jnp.ones_like(v_turned)
        even = jnp.where(lane_half, q_pair, q_code), jnp.where(lane_half, k_pair, k_code), jnp.where(row_half, v_turned, one)
        odd = jnp.where(lane_half, q_code, q_pair), jnp.where(lane_half, k_code, k_pair), jnp.where(row_half, one, v_turned)
        return even, odd

    sides, ahead = {}, []

    def start_scores(step):
        pair, start, odd = step
        if pair not in sides:
            sides[pair] = sides_of(pair)
        qa, ka, _ = sides[pair][odd]
        ahead.append(dot_nt(ka[: start + block], qa[start : start + block]))

    for step in steps[:AHEAD]:
        start_scores(step)
    parts, logs = ([], []), ([], [])
    for i, (pair, start, odd) in enumerate(steps):
        if i + AHEAD < len(steps):
            start_scores(steps[i + AHEAD])
        scores = ahead.pop(0)
        last = jnp.where(causal, scores[start:], -FAR)
        scores = jnp.concatenate([scores[:start], last], axis=0) if start else last
        top = jnp.max(scores, axis=0, keepdims=True)
        weights = jnp.exp(scores - top).astype(bf16)
        out = dot_nn(sides[pair][odd][2][:, : start + block], weights)
        total = out[0:1] if odd else out[HD : HD + 1]
        parts[odd].append(out * (1.0 / total))
        logs[odd].append(top + jnp.log(total))
        if odd and start + block == length:
            for odd in (0, 1):
                lse_ref[2 * pair + odd : 2 * pair + odd + 1, :] = jnp.concatenate(logs[odd], axis=1)
            for at, (even, odd) in enumerate(zip(*parts)):
                mixed = jnp.where(out_half, even, odd)
                mix_ref[0, at * block : (at + 1) * block, pair * PAIR : (pair + 1) * PAIR] = mixed.T.astype(bf16)
            parts, logs = ([], []), ([], [])

    spread_pieces(order_ref, mix_refs, mix_ref)
    a_ref[0] = turned_rows(jnp.concatenate([query_rows, *split_three(-lse_ref[...])], axis=0))


def own_place(mine, n, at):
    return lambda s, order: ((order[0] * mine if n == 2 else 0) + at + s, 0, 0)


def attend_forward(order, at, count, pieces, w, segments, before):
    total, _, length = segments.shape
    width, n = pieces[0].shape[2], len(pieces)
    whole = lambda s, order: (0, 0)
    row = lambda s, order: (s, 0, 0)
    after = lambda s, order: (s + at, 0, 0)
    wide, narrow = pl.BlockSpec((1, length, width), row), pl.BlockSpec((1, length, PAIR), row)
    piece = lambda m: pl.BlockSpec((1, length // n, width), m)
    parts = [pl.BlockSpec((1, length // n, width), m) for m in (after, row)[:n]]
    full = lambda count, rows, cols: jax.ShapeDtypeStruct((count, rows, cols), bf16)
    ws = list(w) if isinstance(w, tuple) else [w]
    w_shape = (width, 3 * width)
    args = [order, *pieces, *ws, segments] + ([] if before is None else [before])
    out = pl.pallas_call(
        functools.partial(attend_forward_kernel, n, len(ws), before is not None),
        grid_spec=pltpu.PrefetchScalarGridSpec(
            num_scalar_prefetch=1,
            grid=(count,),
            in_specs=[piece(own_place(total, n, at)), piece(row)][:n]
            + [pl.BlockSpec(v.shape, lambda s, order, v=v: (0,) * v.ndim) for v in ws]
            + [pl.BlockSpec((1, 1, length), after)]
            + ([] if before is None else [pl.BlockSpec(memory_space=pl.ANY)]),
            out_specs=[wide, wide, wide, narrow, narrow] + parts + [pl.BlockSpec(w_shape, whole)] * (len(ws) - 1),
            scratch_shapes=[
                pltpu.VMEM((width // HD, length), f32),
                pltpu.VMEM((1, length, width), bf16),
                pltpu.VMEM((1, length, width), bf16),
                pltpu.VMEM((1, length, PAIR), bf16),
            ],
        ),
        out_shape=[full(count, length, width)] * 3
        + [full(count, length, PAIR)] * 2
        + [full(total, length // n, width), full(count, length // n, width)][:n]
        + [jax.ShapeDtypeStruct(w_shape, bf16)] * (len(ws) - 1),
        input_output_aliases={} if before is None else {len(args) - 1: 5},
        cost_estimate=work(count * length * width * (3 * width + 8 * length), count * length * width * 12),
        compiler_params=params(),
        name="attend_forward",
    )(*args)
    return out[:5], out[5:]


def attend_backward_kernel(n, begun, last, halves, *refs):
    order_ref, refs = refs[0], refs[1:]
    x_refs, mix_refs, go_refs = (refs[i * n : (i + 1) * n] for i in range(3))
    w_ref, q_ref, k_ref, v_ref, a_ref, kc_ref = refs[3 * n : 6 + 3 * n]
    refs = refs[6 + 3 * n :]
    if n == 2:
        gr_ref, refs = refs[0], refs[1:]
    if begun:
        before_ref, refs = refs[0], refs[1:]
    dx_refs, refs = refs[:n], refs[n:]
    if halves:
        kept_ref, refs = refs[0], refs[1:]
    dw_ref, grads, delta_ref, dq_ref, x_held, mix_held, go_held, dw_sum, dx_held, w_held, sems = refs
    step = pl.program_id(0)
    fetched = [pltpu.make_async_copy(w_ref, w_held, sems.at[0])]
    if begun:
        fetched.append(pltpu.make_async_copy(before_ref, dw_sum, sems.at[1]))

    @pl.when(step == 0)
    def _():
        for copy in fetched:
            copy.start()
        if not begun:
            dw_sum[...] = jnp.zeros_like(dw_sum)

    x_ref = gather_pieces(order_ref, x_refs, x_held)
    mix_ref = gather_pieces(order_ref, mix_refs, mix_held)
    go_ref = gather_pieces(order_ref, go_refs, go_held)
    length, width = q_ref.shape[1], q_ref.shape[2]
    block = min(BLOCK, length)

    product = go_ref[0].astype(f32) * mix_ref[0].astype(f32)
    high = product.astype(bf16)
    low = (product - high.astype(f32)).astype(bf16)
    lane = lax.broadcasted_iota(jnp.int32, (width, PAIR), 1) % HD
    head = lax.broadcasted_iota(jnp.int32, (width, PAIR), 0) // HD
    third = lane - EXTRA - head
    picks = ((third == 0) | (third == HEADS) | (third == 2 * HEADS)).astype(f32).astype(bf16)
    delta = -(dot_nn(high, picks) + dot_nn(low, picks))
    high, middle, low = split_three(delta)
    lane = lax.broadcasted_iota(jnp.int32, (length, PAIR), 1) % HD
    delta_ref[...] = jnp.where(
        lane < EXTRA + HEADS, high, jnp.where(lane < EXTRA + 2 * HEADS, middle, low)
    ).astype(bf16)

    a, k_code, minus = a_ref[0], kc_ref[0], delta_ref[...]
    lane_half = first_half((length, PAIR), 1)
    row_half = first_half((PAIR, block), 0)
    causal = lax.broadcasted_iota(jnp.int32, (block, block), 0) >= lax.broadcasted_iota(jnp.int32, (block, block), 1)
    blocks = [(pair, start, odd) for pair in range(width // PAIR) for start in range(0, length, block) for odd in (0, 1)]

    def sides_of(pair):
        lanes = slice(pair * PAIR, (pair + 1) * PAIR)
        q_pair, k_pair, v_pair, go_pair = (r[0, :, lanes] for r in (q_ref, k_ref, v_ref, go_ref))
        sides = []
        for odd in (0, 1):
            mine = head_lanes(2 * pair + odd)
            both = ((q_pair, a), (k_pair, k_code + mine), (v_pair, jnp.broadcast_to(mine, v_pair.shape)), (go_pair, minus))
            sides.append([jnp.where(lane_half, other, own) if odd else jnp.where(lane_half, own, other) for own, other in both])
        return sides, q_pair.T, go_pair.T, k_pair

    sides, ahead = {}, []

    def start_products(at):
        pair, start, odd = at
        if pair not in sides:
            sides[pair] = sides_of(pair)
        qa, ka, va, ga = sides[pair][0][odd]
        stop = start + block
        ahead.append((dot_nt(qa[start:], ka[start:stop]), dot_nt(ga[start:], va[start:stop])))

    for at in blocks[:BACK_AHEAD]:
        start_products(at)
    dk, dv = ([], []), ([], [])
    for i, (pair, start, odd) in enumerate(blocks):
        if i + BACK_AHEAD < len(blocks):
            start_products(blocks[i + BACK_AHEAD])
        scores, dprobs = ahead.pop(0)
        _, q_turned, go_turned, k_pair = sides[pair]
        stop = start + block
        first = jnp.where(causal, scores[:block], -FAR)
        scores = jnp.concatenate([first, scores[block:]], axis=0) if stop < length else first
        probs = jnp.exp(scores)
        dscores = (probs * dprobs).astype(bf16)
        dv[odd].append(dot_nn(go_turned[:, start:], probs.astype(bf16)))
        dk[odd].append(dot_nn(q_turned[:, start:], dscores))
        dq_at = dot_nn(dscores, k_pair[start:stop])
        slot = 2 * (pair % 2) + odd
        if start:
            dq_ref[slot, start:, :] += dq_at
        else:
            dq_ref[slot] = dq_at
        if odd and stop == length:
            lanes = pair * PAIR
            dq = jnp.where(lane_half, dq_ref[slot - 1], dq_ref[slot]) * HD**-0.5
            grads[:, lanes : lanes + PAIR] = dq.astype(bf16)
            for value, third in ((dk, 1), (dv, 2)):
                to = third * width + lanes
                for at, (even, odd) in enumerate(zip(*value)):
                    turned = jnp.where(row_half, even, odd).T.astype(bf16)
                    grads[at * block : (at + 1) * block, to : to + PAIR] = turned
            dk, dv = ([], []), ([], [])

    @pl.when(step == 0)
    def _():
        for copy in fetched:
            copy.wait()

    dw_sum[...] += dot_tn(x_ref[0], grads[...])
    dx_held[0] = dot_nt(grads[...], w_held[...])
    if n == 2:
        rows = length // n
        pick = lambda i: dx_held[0, pl.ds(pl.multiple_of(order_ref[i] * rows, rows), rows), :]
        dx_refs[0][0] = gr_ref[0] + pick(0)
        dx_refs[1][0] = pick(1).astype(bf16)
    else:
        dx_refs[0][0] = dx_held[0].astype(bf16)

    @pl.when(step == pl.num_programs(0) - 1)
    def _():
        if halves:
            pairs, parts, rows, cols = dw_ref.shape
            cols //= 3
            for ref, core in ((kept_ref, order_ref[4]), (dw_ref, 1 - order_ref[4])):
                for i in range(pairs):
                    at = pl.ds(pl.multiple_of((2 * i + core) * rows, rows), rows)
                    for part in range(parts):
                        for third in range(3):
                            start = third * width + part * cols
                            block = dw_sum[at, start : start + cols].astype(bf16)
                            ref[i, part, :, third * cols : (third + 1) * cols] = block
        elif last:
            owners, parts, rows, cols = dw_ref.shape
            cols //= 3
            for part in range(parts):
                for third in range(3):
                    start = third * width + part * cols
                    block = dw_sum[:, start : start + cols].astype(bf16)
                    dw_ref[:, part, :, third * cols : (third + 1) * cols] = block.reshape(owners, rows, cols)
        else:
            copy = pltpu.make_async_copy(dw_sum, dw_ref, sems.at[1])
            copy.start()
            copy.wait()


def attend_backward(order, at, mine, x, mix, go, w, kept, grad_r1, before, last, halves=False):
    count, length = kept[0].shape[:2]
    width, n = w.shape[0], len(x)
    row = lambda s, order: (s, 0, 0)
    wide, narrow = pl.BlockSpec((1, length, width), row), pl.BlockSpec((1, length, PAIR), row)
    anywhere = pl.BlockSpec(memory_space=pl.ANY)
    piece = lambda m: pl.BlockSpec((1, length // n, width), m)
    part, held, own = piece(row), piece(own_place(mine, n, at)), piece(lambda s, order: (s + at, 0, 0))
    args = [order, *x, *mix, *go, w, *kept]
    specs = [held, part][:n] + [own, part][:n] * 2 + [anywhere, wide, wide, wide, narrow, narrow]
    weight_out, dw_shape = anywhere, jax.ShapeDtypeStruct(w.shape, f32)
    if last:
        weight_out = pl.BlockSpec(last, lambda s, order: (0, 0, 0, 0))
        dw_shape = jax.ShapeDtypeStruct(last, bf16)
    dw_specs, dw_shapes = [weight_out], [dw_shape]
    if halves:
        half = (last[0] // 2,) + last[1:]
        dw_specs = [pl.BlockSpec(half, lambda s, order: (0, 0, 0, 0))] * 2
        dw_shapes = [jax.ShapeDtypeStruct(half, bf16)] * 2
    dx_specs, dx_shapes = [part], [jax.ShapeDtypeStruct((count, length // n, width), bf16)]
    alias = {}
    if n == 2:
        alias[len(args)] = 0
        args.append(grad_r1)
        specs.append(held)
        dx_specs, dx_shapes = [held] + dx_specs, [jax.ShapeDtypeStruct(grad_r1.shape, f32)] + dx_shapes
    if before is not None:
        args.append(before)
        specs.append(anywhere)
    out = pl.pallas_call(
        functools.partial(attend_backward_kernel, n, before is not None, last, halves),
        grid_spec=pltpu.PrefetchScalarGridSpec(
            num_scalar_prefetch=1,
            grid=(count,),
            in_specs=specs,
            out_specs=dx_specs + dw_specs,
            scratch_shapes=[
                pltpu.VMEM((length, 3 * width), bf16),
                pltpu.VMEM((length, PAIR), bf16),
                pltpu.VMEM((4, length, PAIR), f32),
                pltpu.VMEM((1, length, width), bf16),
                pltpu.VMEM((1, length, width), bf16),
                pltpu.VMEM((1, length, width), bf16),
                pltpu.VMEM(w.shape, f32),
                pltpu.VMEM((1, length, width), f32),
                pltpu.VMEM(w.shape, bf16),
                pltpu.SemaphoreType.DMA((2,)),
            ],
        ),
        out_shape=dx_shapes + dw_shapes,
        input_output_aliases=alias,
        cost_estimate=work(count * length * width * (6 * width + 16 * length), count * length * width * 20),
        compiler_params=params(),
        name="attend_backward",
    )(*args)
    return out[:n], tuple(out[n:]) if halves else out[n]


def normalize(rows):
    center = rows - jnp.mean(rows, axis=-1, keepdims=True)
    rstd = lax.rsqrt(jnp.mean(center * center, axis=-1, keepdims=True) + norm_eps)
    return center * rstd, rstd


def normalize_back(grad, xhat, rstd, gain):
    scaled = grad * gain
    return rstd * (
        scaled - jnp.mean(scaled, axis=-1, keepdims=True) - xhat * jnp.mean(scaled * xhat, axis=-1, keepdims=True)
    )


def token_kernel(sizes, parts, begun, last, *refs):
    n, step = len(sizes), pl.program_id(0)
    order_ref, x_ref, d_ref, cx_ref, cd_ref = refs[:5]
    mix_refs, (in_ref, back_ref, out_parts_ref, norm_ref), refs = refs[5 : 5 + n], refs[5 + n : 9 + n], refs[9 + n :]
    if begun:
        sums_in, ng_in, refs = refs[3], refs[4], refs[5:]
    xo_ref, do_ref, gr_ref = refs[:3]
    gm_refs, refs = refs[3 : 3 + n], refs[3 + n :]
    if last:
        packed_ref, refs = refs[0], refs[1:]
    else:
        sums_out, ng_out, refs = refs[0], refs[1], refs[2:]
    act_ref, slope, out_ref, sums, ng_ref, sems = refs
    width, hidden = in_ref.shape
    n_out = width // parts
    chunk = min(CHUNK, hidden)
    columns = [slice(at, at + chunk) for at in range(0, hidden, chunk)]
    back_columns = [slice(hidden + at, hidden + at + chunk) for at in range(0, hidden, chunk)]
    out_columns = slice(2 * hidden, 2 * hidden + width)
    starts = [sum(sizes[:i]) for i in range(n)]

    @pl.when(step == 0)
    def _():
        if begun:
            pltpu.make_async_copy(sums_in, sums, sems.at[0]).start()
            ng_ref[...] = ng_in[...]
        else:
            sums[...] = jnp.zeros_like(sums)
            ng_ref[...] = jnp.zeros_like(ng_ref)
        for i in range(parts):
            if n_out % PAIR:
                out_ref[:, i * n_out : (i + 1) * n_out] = out_parts_ref[:, i * n_out : (i + 1) * n_out]
            else:
                to = pl.ds(pl.multiple_of(order_ref[i] * n_out, PAIR), n_out)
                out_ref[:, to] = out_parts_ref[:, i * n_out : (i + 1) * n_out]
    turned = norm_ref[...].astype(f32).T
    g1, b1, g2, b2 = (turned[i : i + 1] for i in range(4))
    mix = mix_refs[0][0]
    for ref, start in zip(mix_refs[1:], starts[1:]):
        mix = jnp.where(step >= start, ref[0], mix)
    attended = dot_nt(mix, out_ref[...])
    xhat1, rstd1 = normalize(x_ref[0].astype(f32) + attended)
    x_one = xhat1 * g1 + b1
    xb = x_one.astype(bf16)
    feed, h = None, dot_nn(xb, in_ref[:, columns[0]])
    for i, cols in enumerate(columns):
        ahead = dot_nn(xb, in_ref[:, columns[i + 1]]) if i + 1 < len(columns) else None
        cdf = 0.5 * lax.erf(h * 0.7071067811865476) + 0.5
        active = (h * cdf).astype(bf16)
        act_ref[:, cols] = active
        slope[:, cols] = cdf + h * (jnp.exp(-0.5 * (h * h)) * 0.3989422804014327)
        product = dot_nt(active, back_ref[:, cols])
        feed = product if feed is None else feed + product
        h = ahead
    xhat2, rstd2 = normalize(x_one + feed)
    xo_ref[0] = (xhat2 * g2 + b2).astype(bf16)
    do_ref[0] = (d_ref[0].astype(f32) + attended + feed).astype(bf16)
    cx, cd = cx_ref[0].astype(f32), cd_ref[0].astype(f32)
    grad_r2 = normalize_back(cx, xhat2, rstd2, g2)
    dg2, db2 = jnp.sum(cx * xhat2, axis=0, keepdims=True), jnp.sum(cx, axis=0, keepdims=True)
    gf = (grad_r2 + cd).astype(bf16)

    if begun:

        @pl.when(step == 0)
        def _():
            pltpu.make_async_copy(sums_in, sums, sems.at[0]).wait()

    gf_turned, xb_turned = gf.T, xb.T
    grad_x1, ga = grad_r2, dot_nn(gf, back_ref[:, columns[0]])
    for i, cols in enumerate(columns):
        ahead = dot_nn(gf, back_ref[:, columns[i + 1]]) if i + 1 < len(columns) else None
        gh = (ga * slope[:, cols]).astype(bf16)
        grad_x1 = grad_x1 + dot_nt(gh, in_ref[:, cols])
        sums[:, cols] += dot_nn(xb_turned, gh)
        ga = ahead

    if not last:
        early = pltpu.make_async_copy(sums.at[:, pl.ds(0, hidden)], sums_out.at[:, pl.ds(0, hidden)], sems.at[1])

        @pl.when(step == pl.num_programs(0) - 1)
        def _():
            early.start()

    for cols, to in zip(columns, back_columns):
        sums[:, to] += dot_nn(gf_turned, act_ref[:, cols])
    grad_r1 = normalize_back(grad_x1, xhat1, rstd1, g1)
    gr_ref[0] = grad_r1
    dg1, db1 = jnp.sum(grad_x1 * xhat1, axis=0, keepdims=True), jnp.sum(grad_x1, axis=0, keepdims=True)
    ng_ref[...] += jnp.concatenate([dg1, db1, dg2, db2, jnp.zeros((4, dg1.shape[1]), f32)], axis=0)
    gb = (grad_r1 + cd).astype(bf16)
    gm = dot_nn(gb, out_ref[...]).astype(bf16)
    sums[:, out_columns] += dot_tn(gb, mix)
    for ref, start, size in zip(gm_refs, starts, sizes):

        @pl.when((step >= start) & (step < start + size))
        def _(ref=ref):
            ref[0] = gm

    @pl.when(step == pl.num_programs(0) - 1)
    def _():
        if last:
            n_hidden = hidden // parts
            rest = jnp.zeros((PAIR - ng_ref.shape[0], width), f32)
            norms = jnp.concatenate([ng_ref[...], rest], axis=0).T
            for i in range(parts):
                to = 0
                own = lambda start, size: sums[:, start + i * size : start + (i + 1) * size]
                if n_out % PAIR:
                    out = own(2 * hidden, n_out)
                else:
                    out = sums[:, pl.ds(pl.multiple_of(2 * hidden + order_ref[i] * n_out, PAIR), n_out)]
                for value in (own(0, n_hidden), own(hidden, n_hidden), norms, out):
                    size = value.shape[1]
                    packed_ref[i, :, to : to + size] = value.astype(bf16)
                    to += size
        else:
            ng_out[...] = ng_ref[...]
            rest = pl.ds(hidden, hidden + width)
            copy = pltpu.make_async_copy(sums.at[:, rest], sums_out.at[:, rest], sems.at[0])
            copy.start()
            copy.wait()
            early.wait()


def token_block(order, places, mixes, x, d, cot_x, cot_d, weights, hidden, parts, before, last):
    (total, rows, width), sizes = x.shape, [m.shape[0] for m in mixes]
    n_hidden, n_out = hidden // parts, width // parts
    starts = [sum(sizes[:i]) for i in range(len(sizes))]

    def there(s, order):
        at = places[0](order) + s
        for start, place in zip(starts[1:], places[1:]):
            at = jnp.where(s < start, at, place(order) + s - start)
        return at, 0, 0

    whole = lambda s, order: (0, 0)
    one = (1, rows, width)
    full = lambda count, dtype: jax.ShapeDtypeStruct((count, rows, width), dtype)

    def within(i):
        return pl.BlockSpec(one, lambda s, order: (jnp.clip(s - starts[i], 0, sizes[i] - 1), 0, 0))

    anywhere, ng = pl.BlockSpec(memory_space=pl.ANY), pl.BlockSpec((8, width), whole)
    mix_specs = [within(i) for i in range(len(mixes))]
    sums = jax.ShapeDtypeStruct((width, 2 * hidden + width), f32)
    packed = (parts, width, 2 * n_hidden + PAIR + -(-n_out // PAIR) * PAIR)
    if last:
        sum_specs, sum_shapes = [pl.BlockSpec(packed, lambda s, order: (0, 0, 0))], [jax.ShapeDtypeStruct(packed, bf16)]
    else:
        sum_specs, sum_shapes = [anywhere, ng], [sums, jax.ShapeDtypeStruct((8, width), f32)]
    window = lambda cols, at: pl.BlockSpec((width, cols), lambda s, order: (0, at // cols))
    windows = [window(hidden, 0), window(hidden, hidden), window(width, 2 * hidden), window(PAIR, 2 * hidden + width)]
    at = 9 + len(mixes)
    count = sum(sizes)
    out = pl.pallas_call(
        functools.partial(token_kernel, tuple(sizes), parts, bool(before), last),
        grid_spec=pltpu.PrefetchScalarGridSpec(
            num_scalar_prefetch=1,
            grid=(count,),
            in_specs=[pl.BlockSpec(one, there)] * 4
            + mix_specs
            + windows
            + ([anywhere] * 4 + [ng] if before else []),
            out_specs=[pl.BlockSpec(one, there)] * 3 + mix_specs + sum_specs,
            scratch_shapes=[pltpu.VMEM((rows, hidden), bf16), pltpu.VMEM((rows, hidden), f32)]
            + [pltpu.VMEM((width, width), bf16), pltpu.VMEM(sums.shape, f32), pltpu.VMEM((8, width), f32), pltpu.SemaphoreType.DMA((2,))],
        ),
        out_shape=[full(total, bf16), full(total, bf16), full(total, f32)] + [full(c, bf16) for c in sizes] + sum_shapes,
        input_output_aliases={at + i: i for i in range(3)} if before else {},
        cost_estimate=work(count * rows * width * (9 * hidden + 3 * width), count * rows * width * 20),
        compiler_params=params(),
        name="token_block",
    )(order, x, d, cot_x, cot_d, *mixes, *[weights] * 4, *before)
    return out[:3] + out[3 + len(mixes) :], out[3 : 3 + len(mixes)]


def exchange(value, over_dp, over_mp):
    perm = [(i, i ^ (2 * over_dp + over_mp)) for i in range(32)]
    return lax.ppermute(value, ("dp", "mp"), perm)


PLANE = ((0, 0), (2, 0), (0, 1), (2, 1))


def place():
    dp, mp = lax.axis_index("dp"), lax.axis_index("mp")
    return dp >> 2, (dp >> 1) & 1, dp & 1, mp


def gather_by_steps(shard, sends, first, arrange, early):
    plane = jnp.stack([shard] + [exchange(shard, *step) for step in PLANE[1:]])
    plane, sends, first = lax.optimization_barrier((plane, sends, swap(first)))
    first = arrange(first)
    half = max(sends[0].shape[0] // 2, 1)
    got, rest = swap(sends[0][:half]), [swap(v) for v in (sends[0][half:],) if v.shape[0]]
    line = [exchange(plane, 4 * k, 0) for k in (1, 2, 3)]
    plane, got, first = lax.optimization_barrier((jnp.stack([plane] + line), got, first))
    plane, rest, early = lax.optimization_barrier((plane, rest, early))
    other = exchange(plane, 1, 0)
    got = jnp.concatenate([got] + rest, axis=0)
    return plane, other, [got] + [swap(v) for v in sends[1:]], first, early


def scatter_by_steps(kept, sent, dx, last):
    z, x, _, m = place()
    rows, cols = kept.shape[2:]
    pick = lambda v, i, axis: lax.dynamic_index_in_dim(v, i, axis=axis, keepdims=False)
    got, dx = lax.optimization_barrier((exchange(sent, 1, 0), dx))
    dx = swap(dx)
    total = (kept.astype(f32) + got.astype(f32)).reshape(4, 2, 2, rows, cols)
    total = pick(total, x, 1) + exchange(pick(total, 1 - x, 1).astype(bf16), 2, 0).astype(f32)
    got = [exchange(pick(total, z ^ k, 0).astype(bf16), 4 * k, 0) for k in (1, 2, 3)]
    total = sum((g.astype(f32) for g in got), pick(total, z, 0))
    total, dx = lax.optimization_barrier((total, dx))
    sent = jnp.concatenate([pick(total, 1 - m, 0).astype(bf16), last], axis=1)
    return pick(total, m, 0), swap(sent), dx


RATES = (0.05, 0.3, 0.05, 0.025, 0.1)


def update_kernel(own_ref, token_ref, got_ref, *refs):
    states, outs = refs[:15], refs[15:]
    cols = own_ref.shape[1]
    n_in, n_back, n_out = states[6].shape[1], states[9].shape[1], states[3].shape[1]
    qkv = own_ref[...] + got_ref[:, :cols].astype(f32)
    token = lambda at, size: token_ref[0, :, at : at + size].astype(f32) + got_ref[:, cols + at : cols + at + size].astype(f32)
    norm_at = n_in + n_back
    grads = (
        qkv,
        token(norm_at + PAIR, n_out),
        token(0, n_in),
        token(n_in, n_back),
        token(norm_at, PAIR).T[: states[12].shape[0]],
    )
    for i, (grad, rate) in enumerate(zip(grads, RATES)):
        weight, mom, sec = states[3 * i : 3 * i + 3]
        mine = outs[3 * i : 3 * i + 3]
        if i:
            for ref, value in zip(mine, adam_update(weight[...], grad, mom[...], sec[...], rate)):
                ref[...] = value
        else:
            size = cols // 3
            for third in range(3):
                part = grad[:, third * size : (third + 1) * size]
                for ref, value in zip(mine, adam_update(weight[third], part, mom[third], sec[third], rate)):
                    ref[third] = value


def update(own, token, got, states):
    vmem = pl.BlockSpec(memory_space=pltpu.VMEM)
    return pl.pallas_call(
        update_kernel,
        in_specs=[vmem] * (3 + len(states)),
        out_specs=[vmem] * len(states),
        out_shape=[jax.ShapeDtypeStruct(v.shape, f32) for v in states],
        compiler_params=params(),
        name="update",
    )(own, token, got, *states)


def adam_update(weight, grad, mom, sec, rate):
    mom_new = beta_first * mom + (1.0 - beta_first) * grad
    sec_new = beta_second * sec + (1.0 - beta_second) * grad * grad
    scaled = (
        mom_new
        / (1.0 - beta_first**STEP)
        / (jnp.sqrt(sec_new / (1.0 - beta_second**STEP)) + adam_eps)
    )
    return (mom_new, sec_new, weight - rate * (scaled + decay_rate * weight))


def swap(value):
    return lax.ppermute(value, "mp", [(0, 1), (1, 0)])


def on_device(
    x_in,
    d_in,
    segments,
    cot_x,
    cot_d,
    w_qkv,
    w_out,
    w_in,
    w_back,
    norms,
    qkv_mom,
    qkv_sec,
    out_mom,
    out_sec,
    in_mom,
    in_sec,
    back_mom,
    back_sec,
    norm_mom,
    norm_sec,
):
    parts, owners = lax.axis_size("mp"), lax.axis_size("dp")
    me = lax.axis_index("mp")
    total, rows, width = x_in.shape
    mine = total // parts
    length = rows * parts
    own_rows, _, qkv_n = w_qkv.shape
    n_out, n_in, n_back = w_out.shape[0], w_in.shape[1], w_back.shape[0]
    hidden = parts * n_in
    here = lambda v, start, count: lax.dynamic_slice_in_dim(v, start, count, axis=0)
    by_steps = (owners, parts) == (16, 2)

    order = jnp.arange(parts, dtype=jnp.int32)
    own_segments = here(segments, me * mine, mine).reshape(mine, 1, length)

    if parts == 2:
        other = 1 - me
        step = max(mine // 2, 1)
        chunks = list(range(0, mine, step))
        send_x = [here(x_in, other * mine + at, step) for at in chunks]
        order = jnp.stack([me, other, *place()]).astype(jnp.int32)
    shard = jnp.concatenate([w_in, w_back.T, w_out.T], axis=1).astype(bf16)

    def arrange(shards):
        columns = zip(*(jnp.split(v, [n_in, n_in + n_back], axis=1) for v in shards))
        columns = [c for kind in columns for c in kind]
        columns.append(jnp.pad(norms.T.astype(bf16), ((0, 0), (0, PAIR - norms.shape[0]))))
        return jnp.concatenate(columns, axis=1)

    if by_steps:
        shard_qkv = w_qkv.astype(bf16).reshape(own_rows, 3 * qkv_n)
        early = own_segments, order
        plane, got, got_x, columns, early = gather_by_steps(
            shard_qkv, send_x, shard, lambda theirs: arrange([shard, theirs]), early
        )
        qkv, (own_segments, order) = (plane, got), early
    else:
        got = lax.all_gather(w_qkv.astype(bf16), ("dp", "mp"), axis=0)
        got = got.reshape(owners, parts, own_rows, 3, qkv_n)
        qkv = got.transpose(0, 2, 3, 1, 4).reshape(width, 3 * width)
        got_x = [swap(v) for v in send_x] if parts == 2 else None
        columns = arrange([shard, swap(shard)] if parts == 2 else list(lax.all_gather(shard, "mp", axis=0)))
    weights = lax.all_gather(columns, "dp", axis=0, tiled=True)

    qkv_shape = (owners, parts, own_rows, 3 * qkv_n)

    def tokens(places, mixes, before, last):
        return token_block(order, places, mixes, x_in, d_in, cot_x, cot_d, weights, hidden, parts, before, last)

    if parts == 2:
        forward, own_mix = [], None
        for i, at in enumerate(chunks):
            x = (x_in, got_x[i])
            kept, (own_mix, sent, *made) = attend_forward(order, at, step, x, qkv, own_segments, own_mix)
            qkv = made[0] if made else qkv
            forward.append((x, kept, sent, swap(sent)))
        before, got_gm = (), []
        for i, at in enumerate(chunks):
            mixes, places = [forward[i][3]], [lambda order, at=at: order[1] * mine + at]
            if i == 0:
                mixes, places = [own_mix] + mixes, [lambda order: order[0] * mine] + places
            before, gms = tokens(places, mixes, before, i == len(chunks) - 1)
            own_gm = gms[0] if i == 0 else own_gm
            got_gm.append(swap(gms[-1]))
        x_out, d_out, x_grad, packed = before
        qkv_grad, got_dx = None, []
        for i, at in enumerate(chunks):
            x, kept, sent, _ = forward[i]
            last = qkv_shape if i == len(chunks) - 1 else None
            (x_grad, dx), qkv_grad = attend_backward(
                order, at, mine, x, (own_mix, sent), (own_gm, got_gm[i]), qkv, kept, x_grad, qkv_grad, last, by_steps and last is not None
            )
            if got_dx:
                qkv_grad, got_dx[-1] = lax.optimization_barrier((qkv_grad, got_dx[-1]))
            got_dx.append(dx if last else swap(dx))
    else:

        def to_sequences(v):
            got = lax.all_to_all(v.reshape(parts, mine, rows, width), "mp", 0, 0)
            return got.transpose(1, 0, 2, 3).reshape(mine, length, width)

        def to_positions(v):
            sent = v.reshape(mine, parts, rows, width).transpose(1, 0, 2, 3)
            return lax.all_to_all(sent, "mp", 0, 0).reshape(total, rows, width)

        x = (to_sequences(x_in),)
        kept, (mix,) = attend_forward(order, 0, mine, x, qkv, own_segments, None)
        (x_out, d_out, grad_r1, packed), (gm,) = tokens([lambda order: 0], [to_positions(mix)], (), True)
        go = (to_sequences(gm),)
        (dx,), qkv_grad = attend_backward(order, 0, mine, x, (mix,), go, qkv, kept, None, None, qkv_shape)
        x_grad = grad_r1 + to_positions(dx).astype(f32)

    got = lax.psum_scatter(packed, "dp", scatter_dimension=1, tiled=True)

    states = (
        (w_qkv, qkv_mom, qkv_sec),
        (w_out, out_mom, out_sec),
        (w_in, in_mom, in_sec),
        (w_back, back_mom, back_sec),
        (norms, norm_mom, norm_sec),
    )
    if by_steps:
        own, theirs, got_dx[-1] = scatter_by_steps(*qkv_grad, got_dx[-1], got[1])
        turns = ((1, 0, 2), (1, 0), (0, 1), (1, 0), (0, 1))
        turned = [v.transpose(turn) for state, turn in zip(states, turns) for v in state]
        new = update(own, got, theirs, turned)
        new = [v.transpose(turns[i // 3]) for i, v in enumerate(new)]
    else:
        if parts == 2:
            got_dx[-1] = swap(got_dx[-1])
            grads = got[0].astype(f32) + swap(got[1]).astype(f32)
        else:
            grads = lax.psum_scatter(got, "mp", scatter_dimension=0, tiled=True)[0].astype(f32)
        in_g, back_g, norm_g, out_g = jnp.split(grads, [n_in, n_in + n_back, n_in + n_back + PAIR], axis=1)
        got = lax.psum_scatter(qkv_grad.reshape(owners, -1), "dp", scatter_dimension=0, tiled=True)
        qkv_g = lax.psum_scatter(got, "mp", scatter_dimension=1, tiled=True).astype(f32)
        grads = (qkv_g.reshape(own_rows, 3, qkv_n), out_g[:, :n_out].T, in_g, back_g.T, norm_g[:, : norms.shape[0]].T)
        new = [v for (w, m, v), g, rate in zip(states, grads, RATES) for v in adam_update(w, g, m, v, rate)]
    if parts == 2:
        for at, dx in zip(chunks, got_dx):
            at = other * mine + at
            added = here(x_grad, at, step) + dx.astype(f32)
            x_grad = lax.dynamic_update_slice_in_dim(x_grad, added, at, axis=0)
    return (x_out, d_out, x_grad, *new)


def solution(mesh):
    stream = P("dp", "mp", None)
    weights = (P("dp", None, "mp"), P("mp", "dp"), P("dp", "mp"), P("mp", "dp"), P(None, "dp"))
    states = tuple(spec for spec in weights for _ in range(2))
    news = tuple(spec for spec in weights for _ in range(3))
    return jax.shard_map(
        on_device,
        mesh=mesh,
        in_specs=(stream, stream, P("dp", None), stream, stream) + weights + states,
        out_specs=(stream, stream, stream) + news,
        check_vma=False,
    )
```

```python
import functools

import jax
import jax.numpy as jnp
from jax import lax
from jax.experimental import pallas as pl
from jax.experimental.pallas import tpu as pltpu
from jax.sharding import PartitionSpec as P

STEP = 5
HD = 64
PAIR = 2 * HD
BLOCK = 256
CHUNK = 512
AHEAD = 4
BACK_AHEAD = 2
VMEM = 60 * 1024 * 1024

norm_eps = 1e-05
beta_first = 0.5
beta_second = 0.5
adam_eps = 1e-08
decay_rate = 0.01

FAR = 2.0**40
BITS = 7
EXTRA = 16
HEADS = 8

bf16 = jnp.bfloat16
f32 = jnp.float32


def dot_nn(a, b):
    return lax.dot_general(a, b, (((1,), (0,)), ((), ())), preferred_element_type=f32)


def dot_nt(a, b):
    return lax.dot_general(a, b, (((1,), (1,)), ((), ())), preferred_element_type=f32)


def dot_tn(a, b):
    return lax.dot_general(a, b, (((0,), (0,)), ((), ())), preferred_element_type=f32)


def params(limit=VMEM):
    return pltpu.CompilerParams(vmem_limit_bytes=limit)


def work(products, moved, exps=0):
    return pl.CostEstimate(flops=int(2 * products), bytes_accessed=int(moved), transcendentals=int(exps))


def split_three(value):
    high = value.astype(bf16).astype(f32)
    rest = value - high
    middle = rest.astype(bf16).astype(f32)
    return high, middle, (rest - middle).astype(bf16).astype(f32)


def document_rows(segments):
    row = lax.broadcasted_iota(jnp.int32, (EXTRA, segments.shape[1]), 0)
    bit = (segments >> jnp.where(row < BITS, row, row - BITS)) & 1
    used = row < 2 * BITS
    query = jnp.where(used, jnp.where(row < BITS, bit, 1 - bit), 0)
    key = jnp.where(used, jnp.where(row < BITS, 1 - bit, bit), 0)
    return query.astype(f32), key.astype(f32) * -FAR


def turned_rows(rows):
    rows = jnp.concatenate([rows, jnp.zeros((HD - rows.shape[0], rows.shape[1]), f32)], axis=0)
    return jnp.concatenate([rows, rows], axis=0).T.astype(bf16)


def first_half(shape, axis):
    return lax.broadcasted_iota(jnp.int32, shape, axis) < HD


def head_lanes(head):
    lane = lax.broadcasted_iota(jnp.int32, (1, PAIR), 1) % HD
    mine = (lane == EXTRA + head) | (lane == EXTRA + HEADS + head) | (lane == EXTRA + 2 * HEADS + head)
    return mine.astype(f32).astype(bf16)


def gather_pieces(order_ref, refs, held):
    if len(refs) == 1:
        return refs[0]
    rows = refs[0].shape[1]
    for i, ref in enumerate(refs):
        held[0, pl.ds(pl.multiple_of(order_ref[i] * rows, rows), rows), :] = ref[0]
    return held


def spread_pieces(order_ref, refs, value_ref):
    rows = refs[0].shape[1]
    for i, ref in enumerate(refs):
        ref[0] = value_ref[0, pl.ds(pl.multiple_of(order_ref[i] * rows, rows), rows), :]


def order_rows(order_ref, own_ref, got_ref, w_ref):
    z0, x0, c0, m0 = (order_ref[2 + i] for i in range(4))
    rows, cols = own_ref.shape[2], own_ref.shape[3] // 3
    for c in range(2):
        for source, here in ((own_ref, c0), (got_ref, 1 - c0)):

            @pl.when(here == c)
            def _(source=source, c=c):
                for z in range(4):
                    for x in range(2):
                        for m in range(2):
                            block = source[z ^ z0, (x ^ x0) + 2 * (m ^ m0)]
                            at = ((z * 2 + x) * 2 + c) * rows
                            for third in range(3):
                                to = third * 2 * cols + m * cols
                                w_ref[at : at + rows, to : to + cols] = block[:, third * cols : (third + 1) * cols]


def attend_forward_kernel(n, n_w, begun, *refs):
    order_ref, refs = refs[0], refs[1:]
    x_refs, w_refs, seg_ref = refs[:n], refs[n : n + n_w], refs[n + n_w]
    refs = refs[1 + n + n_w + begun :]
    q_ref, k_ref, v_ref, a_ref, kc_ref = refs[:5]
    mix_refs, refs = refs[5 : 5 + n], refs[5 + n :]
    w_ref = w_refs[0]
    if n_w == 2:
        w_ref, refs = refs[0], refs[1:]

        @pl.when(pl.program_id(0) == 0)
        def _():
            order_rows(order_ref, *w_refs, w_ref)

    lse_ref, x_held, mix_ref, qc_ref = refs
    x_ref = gather_pieces(order_ref, x_refs, x_held)
    length, width = q_ref.shape[1], q_ref.shape[2]
    query_rows, key_rows = document_rows(seg_ref[0])
    qc_ref[0], kc_ref[0] = turned_rows(query_rows), turned_rows(key_rows)
    x = x_ref[0]
    q = dot_nn(x, w_ref[:, 0:width]).astype(bf16)
    q_ref[0] = q * jnp.asarray(HD**-0.5, bf16)
    k_ref[0] = dot_nn(x, w_ref[:, width : 2 * width]).astype(bf16)
    v_ref[0] = dot_nn(x, w_ref[:, 2 * width : 3 * width]).astype(bf16)
    block = min(BLOCK, length)
    heads = width // HD

    q_code, k_code = qc_ref[0], kc_ref[0]
    lane_half = first_half((length, PAIR), 1)
    row_half = first_half((PAIR, length), 0)
    out_half = first_half((PAIR, block), 0)
    causal = lax.broadcasted_iota(jnp.int32, (block, block), 0) <= lax.broadcasted_iota(jnp.int32, (block, block), 1)
    steps = [(pair, start, odd) for pair in range(width // PAIR) for start in range(0, length, block) for odd in (0, 1)]

    def sides_of(pair):
        lanes = slice(pair * PAIR, (pair + 1) * PAIR)
        q_pair, k_pair, v_pair = q_ref[0, :, lanes], k_ref[0, :, lanes], v_ref[0, :, lanes]
        v_turned = v_pair.T
        one = jnp.ones_like(v_turned)
        even = jnp.where(lane_half, q_pair, q_code), jnp.where(lane_half, k_pair, k_code), jnp.where(row_half, v_turned, one)
        odd = jnp.where(lane_half, q_code, q_pair), jnp.where(lane_half, k_code, k_pair), jnp.where(row_half, one, v_turned)
        return even, odd

    sides, ahead = {}, []

    def start_scores(step):
        pair, start, odd = step
        if pair not in sides:
            sides[pair] = sides_of(pair)
        qa, ka, _ = sides[pair][odd]
        ahead.append(dot_nt(ka[: start + block], qa[start : start + block]))

    for step in steps[:AHEAD]:
        start_scores(step)
    parts, logs = ([], []), ([], [])
    for i, (pair, start, odd) in enumerate(steps):
        if i + AHEAD < len(steps):
            start_scores(steps[i + AHEAD])
        scores = ahead.pop(0)
        last = jnp.where(causal, scores[start:], -FAR)
        scores = jnp.concatenate([scores[:start], last], axis=0) if start else last
        top = jnp.max(scores, axis=0, keepdims=True)
        weights = jnp.exp(scores - top).astype(bf16)
        out = dot_nn(sides[pair][odd][2][:, : start + block], weights)
        total = out[0:1] if odd else out[HD : HD + 1]
        parts[odd].append(out * (1.0 / total))
        logs[odd].append(top + jnp.log(total))
        if odd and start + block == length:
            for odd in (0, 1):
                lse_ref[2 * pair + odd : 2 * pair + odd + 1, :] = jnp.concatenate(logs[odd], axis=1)
            for at, (even, odd) in enumerate(zip(*parts)):
                mixed = jnp.where(out_half, even, odd)
                mix_ref[0, at * block : (at + 1) * block, pair * PAIR : (pair + 1) * PAIR] = mixed.T.astype(bf16)
            parts, logs = ([], []), ([], [])

    spread_pieces(order_ref, mix_refs, mix_ref)
    a_ref[0] = turned_rows(jnp.concatenate([query_rows, *split_three(-lse_ref[...])], axis=0))


def own_place(mine, n, at):
    return lambda s, order: ((order[0] * mine if n == 2 else 0) + at + s, 0, 0)


def attend_forward(order, at, count, pieces, w, segments, before):
    total, _, length = segments.shape
    width, n = pieces[0].shape[2], len(pieces)
    whole = lambda s, order: (0, 0)
    row = lambda s, order: (s, 0, 0)
    after = lambda s, order: (s + at, 0, 0)
    wide, narrow = pl.BlockSpec((1, length, width), row), pl.BlockSpec((1, length, PAIR), row)
    piece = lambda m: pl.BlockSpec((1, length // n, width), m)
    parts = [pl.BlockSpec((1, length // n, width), m) for m in (after, row)[:n]]
    full = lambda count, rows, cols: jax.ShapeDtypeStruct((count, rows, cols), bf16)
    ws = list(w) if isinstance(w, tuple) else [w]
    w_shape = (width, 3 * width)
    args = [order, *pieces, *ws, segments] + ([] if before is None else [before])
    out = pl.pallas_call(
        functools.partial(attend_forward_kernel, n, len(ws), before is not None),
        grid_spec=pltpu.PrefetchScalarGridSpec(
            num_scalar_prefetch=1,
            grid=(count,),
            in_specs=[piece(own_place(total, n, at)), piece(row)][:n]
            + [pl.BlockSpec(v.shape, lambda s, order, v=v: (0,) * v.ndim) for v in ws]
            + [pl.BlockSpec((1, 1, length), after)]
            + ([] if before is None else [pl.BlockSpec(memory_space=pl.ANY)]),
            out_specs=[wide, wide, wide, narrow, narrow] + parts + [pl.BlockSpec(w_shape, whole)] * (len(ws) - 1),
            scratch_shapes=[
                pltpu.VMEM((width // HD, length), f32),
                pltpu.VMEM((1, length, width), bf16),
                pltpu.VMEM((1, length, width), bf16),
                pltpu.VMEM((1, length, PAIR), bf16),
            ],
        ),
        out_shape=[full(count, length, width)] * 3
        + [full(count, length, PAIR)] * 2
        + [full(total, length // n, width), full(count, length // n, width)][:n]
        + [jax.ShapeDtypeStruct(w_shape, bf16)] * (len(ws) - 1),
        input_output_aliases={} if before is None else {len(args) - 1: 5},
        cost_estimate=work(count * length * width * (3 * width + 8 * length), count * length * width * 12),
        compiler_params=params(),
        name="attend_forward",
    )(*args)
    return out[:5], out[5:]


def attend_backward_kernel(n, begun, last, halves, *refs):
    order_ref, refs = refs[0], refs[1:]
    x_refs, mix_refs, go_refs = (refs[i * n : (i + 1) * n] for i in range(3))
    w_ref, q_ref, k_ref, v_ref, a_ref, kc_ref = refs[3 * n : 6 + 3 * n]
    refs = refs[6 + 3 * n :]
    if n == 2:
        gr_ref, refs = refs[0], refs[1:]
    if begun:
        before_ref, refs = refs[0], refs[1:]
    dx_refs, refs = refs[:n], refs[n:]
    if halves:
        kept_ref, refs = refs[0], refs[1:]
    dw_ref, grads, delta_ref, dq_ref, x_held, mix_held, go_held, dw_sum, dx_held, w_held, sems = refs
    step = pl.program_id(0)
    fetched = [pltpu.make_async_copy(w_ref, w_held, sems.at[0])]
    if begun:
        fetched.append(pltpu.make_async_copy(before_ref, dw_sum, sems.at[1]))

    @pl.when(step == 0)
    def _():
        for copy in fetched:
            copy.start()
        if not begun:
            dw_sum[...] = jnp.zeros_like(dw_sum)

    x_ref = gather_pieces(order_ref, x_refs, x_held)
    mix_ref = gather_pieces(order_ref, mix_refs, mix_held)
    go_ref = gather_pieces(order_ref, go_refs, go_held)
    length, width = q_ref.shape[1], q_ref.shape[2]
    block = min(BLOCK, length)

    product = go_ref[0].astype(f32) * mix_ref[0].astype(f32)
    high = product.astype(bf16)
    low = (product - high.astype(f32)).astype(bf16)
    lane = lax.broadcasted_iota(jnp.int32, (width, PAIR), 1) % HD
    head = lax.broadcasted_iota(jnp.int32, (width, PAIR), 0) // HD
    third = lane - EXTRA - head
    picks = ((third == 0) | (third == HEADS) | (third == 2 * HEADS)).astype(f32).astype(bf16)
    delta = -(dot_nn(high, picks) + dot_nn(low, picks))
    high, middle, low = split_three(delta)
    lane = lax.broadcasted_iota(jnp.int32, (length, PAIR), 1) % HD
    delta_ref[...] = jnp.where(
        lane < EXTRA + HEADS, high, jnp.where(lane < EXTRA + 2 * HEADS, middle, low)
    ).astype(bf16)

    a, k_code, minus = a_ref[0], kc_ref[0], delta_ref[...]
    lane_half = first_half((length, PAIR), 1)
    row_half = first_half((PAIR, block), 0)
    causal = lax.broadcasted_iota(jnp.int32, (block, block), 0) >= lax.broadcasted_iota(jnp.int32, (block, block), 1)
    blocks = [(pair, start, odd) for pair in range(width // PAIR) for start in range(0, length, block) for odd in (0, 1)]

    def sides_of(pair):
        lanes = slice(pair * PAIR, (pair + 1) * PAIR)
        q_pair, k_pair, v_pair, go_pair = (r[0, :, lanes] for r in (q_ref, k_ref, v_ref, go_ref))
        sides = []
        for odd in (0, 1):
            mine = head_lanes(2 * pair + odd)
            both = ((q_pair, a), (k_pair, k_code + mine), (v_pair, jnp.broadcast_to(mine, v_pair.shape)), (go_pair, minus))
            sides.append([jnp.where(lane_half, other, own) if odd else jnp.where(lane_half, own, other) for own, other in both])
        return sides, q_pair.T, go_pair.T, k_pair

    sides, ahead = {}, []

    def start_products(at):
        pair, start, odd = at
        if pair not in sides:
            sides[pair] = sides_of(pair)
        qa, ka, va, ga = sides[pair][0][odd]
        stop = start + block
        ahead.append((dot_nt(qa[start:], ka[start:stop]), dot_nt(ga[start:], va[start:stop])))

    for at in blocks[:BACK_AHEAD]:
        start_products(at)
    dk, dv = ([], []), ([], [])
    for i, (pair, start, odd) in enumerate(blocks):
        if i + BACK_AHEAD < len(blocks):
            start_products(blocks[i + BACK_AHEAD])
        scores, dprobs = ahead.pop(0)
        _, q_turned, go_turned, k_pair = sides[pair]
        stop = start + block
        first = jnp.where(causal, scores[:block], -FAR)
        scores = jnp.concatenate([first, scores[block:]], axis=0) if stop < length else first
        probs = jnp.exp(scores)
        dscores = (probs * dprobs).astype(bf16)
        dv[odd].append(dot_nn(go_turned[:, start:], probs.astype(bf16)))
        dk[odd].append(dot_nn(q_turned[:, start:], dscores))
        dq_at = dot_nn(dscores, k_pair[start:stop])
        slot = 2 * (pair % 2) + odd
        if start:
            dq_ref[slot, start:, :] += dq_at
        else:
            dq_ref[slot] = dq_at
        if odd and stop == length:
            lanes = pair * PAIR
            dq = jnp.where(lane_half, dq_ref[slot - 1], dq_ref[slot]) * HD**-0.5
            grads[:, lanes : lanes + PAIR] = dq.astype(bf16)
            for value, third in ((dk, 1), (dv, 2)):
                to = third * width + lanes
                for at, (even, odd) in enumerate(zip(*value)):
                    turned = jnp.where(row_half, even, odd).T.astype(bf16)
                    grads[at * block : (at + 1) * block, to : to + PAIR] = turned
            dk, dv = ([], []), ([], [])

    @pl.when(step == 0)
    def _():
        for copy in fetched:
            copy.wait()

    dw_sum[...] += dot_tn(x_ref[0], grads[...])
    dx_held[0] = dot_nt(grads[...], w_held[...])
    if n == 2:
        rows = length // n
        pick = lambda i: dx_held[0, pl.ds(pl.multiple_of(order_ref[i] * rows, rows), rows), :]
        dx_refs[0][0] = gr_ref[0] + pick(0)
        dx_refs[1][0] = pick(1).astype(bf16)
    else:
        dx_refs[0][0] = dx_held[0].astype(bf16)

    @pl.when(step == pl.num_programs(0) - 1)
    def _():
        if halves:
            pairs, parts, rows, cols = dw_ref.shape
            cols //= 3
            for ref, core in ((kept_ref, order_ref[4]), (dw_ref, 1 - order_ref[4])):
                for i in range(pairs):
                    at = pl.ds(pl.multiple_of((2 * i + core) * rows, rows), rows)
                    for part in range(parts):
                        for third in range(3):
                            start = third * width + part * cols
                            block = dw_sum[at, start : start + cols].astype(bf16)
                            ref[i, part, :, third * cols : (third + 1) * cols] = block
        elif last:
            owners, parts, rows, cols = dw_ref.shape
            cols //= 3
            for part in range(parts):
                for third in range(3):
                    start = third * width + part * cols
                    block = dw_sum[:, start : start + cols].astype(bf16)
                    dw_ref[:, part, :, third * cols : (third + 1) * cols] = block.reshape(owners, rows, cols)
        else:
            copy = pltpu.make_async_copy(dw_sum, dw_ref, sems.at[1])
            copy.start()
            copy.wait()


def attend_backward(order, at, mine, x, mix, go, w, kept, grad_r1, before, last, halves=False):
    count, length = kept[0].shape[:2]
    width, n = w.shape[0], len(x)
    row = lambda s, order: (s, 0, 0)
    wide, narrow = pl.BlockSpec((1, length, width), row), pl.BlockSpec((1, length, PAIR), row)
    anywhere = pl.BlockSpec(memory_space=pl.ANY)
    piece = lambda m: pl.BlockSpec((1, length // n, width), m)
    part, held, own = piece(row), piece(own_place(mine, n, at)), piece(lambda s, order: (s + at, 0, 0))
    args = [order, *x, *mix, *go, w, *kept]
    specs = [held, part][:n] + [own, part][:n] * 2 + [anywhere, wide, wide, wide, narrow, narrow]
    weight_out, dw_shape = anywhere, jax.ShapeDtypeStruct(w.shape, f32)
    if last:
        weight_out = pl.BlockSpec(last, lambda s, order: (0, 0, 0, 0))
        dw_shape = jax.ShapeDtypeStruct(last, bf16)
    dw_specs, dw_shapes = [weight_out], [dw_shape]
    if halves:
        half = (last[0] // 2,) + last[1:]
        dw_specs = [pl.BlockSpec(half, lambda s, order: (0, 0, 0, 0))] * 2
        dw_shapes = [jax.ShapeDtypeStruct(half, bf16)] * 2
    dx_specs, dx_shapes = [part], [jax.ShapeDtypeStruct((count, length // n, width), bf16)]
    alias = {}
    if n == 2:
        alias[len(args)] = 0
        args.append(grad_r1)
        specs.append(held)
        dx_specs, dx_shapes = [held] + dx_specs, [jax.ShapeDtypeStruct(grad_r1.shape, f32)] + dx_shapes
    if before is not None:
        args.append(before)
        specs.append(anywhere)
    out = pl.pallas_call(
        functools.partial(attend_backward_kernel, n, before is not None, last, halves),
        grid_spec=pltpu.PrefetchScalarGridSpec(
            num_scalar_prefetch=1,
            grid=(count,),
            in_specs=specs,
            out_specs=dx_specs + dw_specs,
            scratch_shapes=[
                pltpu.VMEM((length, 3 * width), bf16),
                pltpu.VMEM((length, PAIR), bf16),
                pltpu.VMEM((4, length, PAIR), f32),
                pltpu.VMEM((1, length, width), bf16),
                pltpu.VMEM((1, length, width), bf16),
                pltpu.VMEM((1, length, width), bf16),
                pltpu.VMEM(w.shape, f32),
                pltpu.VMEM((1, length, width), f32),
                pltpu.VMEM(w.shape, bf16),
                pltpu.SemaphoreType.DMA((2,)),
            ],
        ),
        out_shape=dx_shapes + dw_shapes,
        input_output_aliases=alias,
        cost_estimate=work(count * length * width * (6 * width + 16 * length), count * length * width * 20),
        compiler_params=params(50 * 1024 * 1024),
        name="attend_backward",
    )(*args)
    return out[:n], tuple(out[n:]) if halves else out[n]


def normalize(rows):
    center = rows - jnp.mean(rows, axis=-1, keepdims=True)
    rstd = lax.rsqrt(jnp.mean(center * center, axis=-1, keepdims=True) + norm_eps)
    return center * rstd, rstd


def normalize_back(grad, xhat, rstd, gain):
    scaled = grad * gain
    return rstd * (
        scaled - jnp.mean(scaled, axis=-1, keepdims=True) - xhat * jnp.mean(scaled * xhat, axis=-1, keepdims=True)
    )


def token_kernel(sizes, parts, begun, last, *refs):
    n, step = len(sizes), pl.program_id(0)
    order_ref, x_ref, d_ref, cx_ref, cd_ref = refs[:5]
    mix_refs, (in_ref, back_ref, out_parts_ref, norm_ref), refs = refs[5 : 5 + n], refs[5 + n : 9 + n], refs[9 + n :]
    if begun:
        sums_in, ng_in, refs = refs[3], refs[4], refs[5:]
    xo_ref, do_ref, gr_ref = refs[:3]
    gm_refs, refs = refs[3 : 3 + n], refs[3 + n :]
    if last:
        packed_ref, refs = refs[0], refs[1:]
    else:
        sums_out, ng_out, refs = refs[0], refs[1], refs[2:]
    act_ref, slope, out_ref, sums, ng_ref, sems = refs
    width, hidden = in_ref.shape
    n_out = width // parts
    chunk = min(CHUNK, hidden)
    columns = [slice(at, at + chunk) for at in range(0, hidden, chunk)]
    back_columns = [slice(hidden + at, hidden + at + chunk) for at in range(0, hidden, chunk)]
    out_columns = slice(2 * hidden, 2 * hidden + width)
    starts = [sum(sizes[:i]) for i in range(n)]

    @pl.when(step == 0)
    def _():
        if begun:
            pltpu.make_async_copy(sums_in, sums, sems.at[0]).start()
            ng_ref[...] = ng_in[...]
        else:
            sums[...] = jnp.zeros_like(sums)
            ng_ref[...] = jnp.zeros_like(ng_ref)
        for i in range(parts):
            if n_out % PAIR:
                out_ref[:, i * n_out : (i + 1) * n_out] = out_parts_ref[:, i * n_out : (i + 1) * n_out]
            else:
                to = pl.ds(pl.multiple_of(order_ref[i] * n_out, PAIR), n_out)
                out_ref[:, to] = out_parts_ref[:, i * n_out : (i + 1) * n_out]
    turned = norm_ref[...].astype(f32).T
    g1, b1, g2, b2 = (turned[i : i + 1] for i in range(4))
    mix = mix_refs[0][0]
    for ref, start in zip(mix_refs[1:], starts[1:]):
        mix = jnp.where(step >= start, ref[0], mix)
    attended = dot_nt(mix, out_ref[...])
    xhat1, rstd1 = normalize(x_ref[0].astype(f32) + attended)
    x_one = xhat1 * g1 + b1
    xb = x_one.astype(bf16)
    feed, h = None, dot_nn(xb, in_ref[:, columns[0]])
    for i, cols in enumerate(columns):
        ahead = dot_nn(xb, in_ref[:, columns[i + 1]]) if i + 1 < len(columns) else None
        cdf = 0.5 * lax.erf(h * 0.7071067811865476) + 0.5
        active = (h * cdf).astype(bf16)
        act_ref[:, cols] = active
        slope[:, cols] = cdf + h * (jnp.exp(-0.5 * (h * h)) * 0.3989422804014327)
        product = dot_nt(active, back_ref[:, cols])
        feed = product if feed is None else feed + product
        h = ahead
    xhat2, rstd2 = normalize(x_one + feed)
    xo_ref[0] = (xhat2 * g2 + b2).astype(bf16)
    do_ref[0] = (d_ref[0].astype(f32) + attended + feed).astype(bf16)
    cx, cd = cx_ref[0].astype(f32), cd_ref[0].astype(f32)
    grad_r2 = normalize_back(cx, xhat2, rstd2, g2)
    dg2, db2 = jnp.sum(cx * xhat2, axis=0, keepdims=True), jnp.sum(cx, axis=0, keepdims=True)
    gf = (grad_r2 + cd).astype(bf16)

    if begun:

        @pl.when(step == 0)
        def _():
            pltpu.make_async_copy(sums_in, sums, sems.at[0]).wait()

    gf_turned, xb_turned = gf.T, xb.T
    grad_x1, ga = grad_r2, dot_nn(gf, back_ref[:, columns[0]])
    for i, cols in enumerate(columns):
        ahead = dot_nn(gf, back_ref[:, columns[i + 1]]) if i + 1 < len(columns) else None
        gh = (ga * slope[:, cols]).astype(bf16)
        grad_x1 = grad_x1 + dot_nt(gh, in_ref[:, cols])
        sums[:, cols] += dot_nn(xb_turned, gh)
        ga = ahead

    if not last:
        early = pltpu.make_async_copy(sums.at[:, pl.ds(0, hidden)], sums_out.at[:, pl.ds(0, hidden)], sems.at[1])

        @pl.when(step == pl.num_programs(0) - 1)
        def _():
            early.start()

    for cols, to in zip(columns, back_columns):
        sums[:, to] += dot_nn(gf_turned, act_ref[:, cols])
    grad_r1 = normalize_back(grad_x1, xhat1, rstd1, g1)
    gr_ref[0] = grad_r1
    dg1, db1 = jnp.sum(grad_x1 * xhat1, axis=0, keepdims=True), jnp.sum(grad_x1, axis=0, keepdims=True)
    ng_ref[...] += jnp.concatenate([dg1, db1, dg2, db2, jnp.zeros((4, dg1.shape[1]), f32)], axis=0)
    gb = (grad_r1 + cd).astype(bf16)
    gm = dot_nn(gb, out_ref[...]).astype(bf16)
    sums[:, out_columns] += dot_tn(gb, mix)
    for ref, start, size in zip(gm_refs, starts, sizes):

        @pl.when((step >= start) & (step < start + size))
        def _(ref=ref):
            ref[0] = gm

    @pl.when(step == pl.num_programs(0) - 1)
    def _():
        if last:
            n_hidden = hidden // parts
            rest = jnp.zeros((PAIR - ng_ref.shape[0], width), f32)
            norms = jnp.concatenate([ng_ref[...], rest], axis=0).T
            for i in range(parts):
                to = 0
                own = lambda start, size: sums[:, start + i * size : start + (i + 1) * size]
                if n_out % PAIR:
                    out = own(2 * hidden, n_out)
                else:
                    out = sums[:, pl.ds(pl.multiple_of(2 * hidden + order_ref[i] * n_out, PAIR), n_out)]
                for value in (own(0, n_hidden), own(hidden, n_hidden), norms, out):
                    size = value.shape[1]
                    packed_ref[i, :, to : to + size] = value.astype(bf16)
                    to += size
        else:
            ng_out[...] = ng_ref[...]
            rest = pl.ds(hidden, hidden + width)
            copy = pltpu.make_async_copy(sums.at[:, rest], sums_out.at[:, rest], sems.at[0])
            copy.start()
            copy.wait()
            early.wait()


def token_block(order, places, mixes, x, d, cot_x, cot_d, weights, hidden, parts, before, last):
    (total, rows, width), sizes = x.shape, [m.shape[0] for m in mixes]
    n_hidden, n_out = hidden // parts, width // parts
    starts = [sum(sizes[:i]) for i in range(len(sizes))]

    def there(s, order):
        at = places[0](order) + s
        for start, place in zip(starts[1:], places[1:]):
            at = jnp.where(s < start, at, place(order) + s - start)
        return at, 0, 0

    whole = lambda s, order: (0, 0)
    one = (1, rows, width)
    full = lambda count, dtype: jax.ShapeDtypeStruct((count, rows, width), dtype)

    def within(i):
        return pl.BlockSpec(one, lambda s, order: (jnp.clip(s - starts[i], 0, sizes[i] - 1), 0, 0))

    anywhere, ng = pl.BlockSpec(memory_space=pl.ANY), pl.BlockSpec((8, width), whole)
    mix_specs = [within(i) for i in range(len(mixes))]
    sums = jax.ShapeDtypeStruct((width, 2 * hidden + width), f32)
    packed = (parts, width, 2 * n_hidden + PAIR + -(-n_out // PAIR) * PAIR)
    if last:
        sum_specs, sum_shapes = [pl.BlockSpec(packed, lambda s, order: (0, 0, 0))], [jax.ShapeDtypeStruct(packed, bf16)]
    else:
        sum_specs, sum_shapes = [anywhere, ng], [sums, jax.ShapeDtypeStruct((8, width), f32)]
    window = lambda cols, at: pl.BlockSpec((width, cols), lambda s, order: (0, at // cols))
    windows = [window(hidden, 0), window(hidden, hidden), window(width, 2 * hidden), window(PAIR, 2 * hidden + width)]
    at = 9 + len(mixes)
    count = sum(sizes)
    out = pl.pallas_call(
        functools.partial(token_kernel, tuple(sizes), parts, bool(before), last),
        grid_spec=pltpu.PrefetchScalarGridSpec(
            num_scalar_prefetch=1,
            grid=(count,),
            in_specs=[pl.BlockSpec(one, there)] * 4
            + mix_specs
            + windows
            + ([anywhere] * 4 + [ng] if before else []),
            out_specs=[pl.BlockSpec(one, there)] * 3 + mix_specs + sum_specs,
            scratch_shapes=[pltpu.VMEM((rows, hidden), bf16), pltpu.VMEM((rows, hidden), f32)]
            + [pltpu.VMEM((width, width), bf16), pltpu.VMEM(sums.shape, f32), pltpu.VMEM((8, width), f32), pltpu.SemaphoreType.DMA((2,))],
        ),
        out_shape=[full(total, bf16), full(total, bf16), full(total, f32)] + [full(c, bf16) for c in sizes] + sum_shapes,
        input_output_aliases={at + i: i for i in range(3)} if before else {},
        cost_estimate=work(count * rows * width * (9 * hidden + 3 * width), count * rows * width * 20),
        compiler_params=params(),
        name="token_block",
    )(order, x, d, cot_x, cot_d, *mixes, *[weights] * 4, *before)
    return out[:3] + out[3 + len(mixes) :], out[3 : 3 + len(mixes)]


def exchange(value, over_dp, over_mp):
    perm = [(i, i ^ (2 * over_dp + over_mp)) for i in range(32)]
    return lax.ppermute(value, ("dp", "mp"), perm)


PLANE = ((0, 0), (2, 0), (0, 1), (2, 1))


def place():
    dp, mp = lax.axis_index("dp"), lax.axis_index("mp")
    return dp >> 2, (dp >> 1) & 1, dp & 1, mp


def gather_by_steps(shard, sends, first, arrange, early):
    plane = jnp.stack([shard] + [exchange(shard, *step) for step in PLANE[1:]])
    plane, sends, first = lax.optimization_barrier((plane, sends, swap(first)))
    first = arrange(first)
    half = max(sends[0].shape[0] // 2, 1)
    got, rest = swap(sends[0][:half]), [swap(v) for v in (sends[0][half:],) if v.shape[0]]
    line = [exchange(plane, 4 * k, 0) for k in (1, 2, 3)]
    plane, got, first = lax.optimization_barrier((jnp.stack([plane] + line), got, first))
    plane, rest, early = lax.optimization_barrier((plane, rest, early))
    other = exchange(plane, 1, 0)
    got = jnp.concatenate([got] + rest, axis=0)
    return plane, other, [got] + [swap(v) for v in sends[1:]], first, early


def scatter_by_steps(kept, sent, dx, last):
    z, x, _, m = place()
    rows, cols = kept.shape[2:]
    pick = lambda v, i, axis: lax.dynamic_index_in_dim(v, i, axis=axis, keepdims=False)
    got, dx = lax.optimization_barrier((exchange(sent, 1, 0), dx))
    dx = swap(dx)
    total = (kept.astype(f32) + got.astype(f32)).reshape(4, 2, 2, rows, cols)
    total = pick(total, x, 1) + exchange(pick(total, 1 - x, 1).astype(bf16), 2, 0).astype(f32)
    got = [exchange(pick(total, z ^ k, 0).astype(bf16), 4 * k, 0) for k in (1, 2, 3)]
    total = sum((g.astype(f32) for g in got), pick(total, z, 0))
    total, dx = lax.optimization_barrier((total, dx))
    sent = jnp.concatenate([pick(total, 1 - m, 0).astype(bf16), last], axis=1)
    return pick(total, m, 0), swap(sent), dx


RATES = (0.05, 0.3, 0.05, 0.025, 0.1)


def update_kernel(own_ref, token_ref, got_ref, *refs):
    states, outs = refs[:15], refs[15:]
    cols = own_ref.shape[1]
    n_in, n_back, n_out = states[6].shape[1], states[9].shape[1], states[3].shape[1]
    qkv = own_ref[...] + got_ref[:, :cols].astype(f32)
    token = lambda at, size: token_ref[0, :, at : at + size].astype(f32) + got_ref[:, cols + at : cols + at + size].astype(f32)
    norm_at = n_in + n_back
    grads = (
        qkv,
        token(norm_at + PAIR, n_out),
        token(0, n_in),
        token(n_in, n_back),
        token(norm_at, PAIR).T[: states[12].shape[0]],
    )
    for i, (grad, rate) in enumerate(zip(grads, RATES)):
        weight, mom, sec = states[3 * i : 3 * i + 3]
        mine = outs[3 * i : 3 * i + 3]
        if i:
            for ref, value in zip(mine, adam_update(weight[...], grad, mom[...], sec[...], rate)):
                ref[...] = value
        else:
            size = cols // 3
            for third in range(3):
                part = grad[:, third * size : (third + 1) * size]
                for ref, value in zip(mine, adam_update(weight[third], part, mom[third], sec[third], rate)):
                    ref[third] = value


def update(own, token, got, states):
    vmem = pl.BlockSpec(memory_space=pltpu.VMEM)
    return pl.pallas_call(
        update_kernel,
        in_specs=[vmem] * (3 + len(states)),
        out_specs=[vmem] * len(states),
        out_shape=[jax.ShapeDtypeStruct(v.shape, f32) for v in states],
        compiler_params=params(),
        name="update",
    )(own, token, got, *states)


def adam_update(weight, grad, mom, sec, rate):
    mom_new = beta_first * mom + (1.0 - beta_first) * grad
    sec_new = beta_second * sec + (1.0 - beta_second) * grad * grad
    scaled = (
        mom_new
        / (1.0 - beta_first**STEP)
        / (jnp.sqrt(sec_new / (1.0 - beta_second**STEP)) + adam_eps)
    )
    return (mom_new, sec_new, weight - rate * (scaled + decay_rate * weight))


def swap(value):
    return lax.ppermute(value, "mp", [(0, 1), (1, 0)])


def on_device(
    x_in,
    d_in,
    segments,
    cot_x,
    cot_d,
    w_qkv,
    w_out,
    w_in,
    w_back,
    norms,
    qkv_mom,
    qkv_sec,
    out_mom,
    out_sec,
    in_mom,
    in_sec,
    back_mom,
    back_sec,
    norm_mom,
    norm_sec,
):
    parts, owners = lax.axis_size("mp"), lax.axis_size("dp")
    me = lax.axis_index("mp")
    total, rows, width = x_in.shape
    mine = total // parts
    length = rows * parts
    own_rows, _, qkv_n = w_qkv.shape
    n_out, n_in, n_back = w_out.shape[0], w_in.shape[1], w_back.shape[0]
    hidden = parts * n_in
    here = lambda v, start, count: lax.dynamic_slice_in_dim(v, start, count, axis=0)
    by_steps = (owners, parts) == (16, 2)

    order = jnp.arange(parts, dtype=jnp.int32)
    own_segments = here(segments, me * mine, mine).reshape(mine, 1, length)

    if parts == 2:
        other = 1 - me
        step = max(mine // 2, 1)
        chunks = list(range(0, mine, step))
        send_x = [here(x_in, other * mine + at, step) for at in chunks]
        order = jnp.stack([me, other, *place()]).astype(jnp.int32)
    shard = jnp.concatenate([w_in, w_back.T, w_out.T], axis=1).astype(bf16)

    def arrange(shards):
        columns = zip(*(jnp.split(v, [n_in, n_in + n_back], axis=1) for v in shards))
        columns = [c for kind in columns for c in kind]
        columns.append(jnp.pad(norms.T.astype(bf16), ((0, 0), (0, PAIR - norms.shape[0]))))
        return jnp.concatenate(columns, axis=1)

    if by_steps:
        shard_qkv = w_qkv.astype(bf16).reshape(own_rows, 3 * qkv_n)
        early = own_segments, order
        plane, got, got_x, columns, early = gather_by_steps(
            shard_qkv, send_x, shard, lambda theirs: arrange([shard, theirs]), early
        )
        qkv, (own_segments, order) = (plane, got), early
    else:
        got = lax.all_gather(w_qkv.astype(bf16), ("dp", "mp"), axis=0)
        got = got.reshape(owners, parts, own_rows, 3, qkv_n)
        qkv = got.transpose(0, 2, 3, 1, 4).reshape(width, 3 * width)
        got_x = [swap(v) for v in send_x] if parts == 2 else None
        columns = arrange([shard, swap(shard)] if parts == 2 else list(lax.all_gather(shard, "mp", axis=0)))
    weights = lax.all_gather(columns, "dp", axis=0, tiled=True)

    qkv_shape = (owners, parts, own_rows, 3 * qkv_n)

    def tokens(places, mixes, before, last):
        return token_block(order, places, mixes, x_in, d_in, cot_x, cot_d, weights, hidden, parts, before, last)

    if parts == 2:
        forward, own_mix = [], None
        for i, at in enumerate(chunks):
            x = (x_in, got_x[i])
            kept, (own_mix, sent, *made) = attend_forward(order, at, step, x, qkv, own_segments, own_mix)
            qkv = made[0] if made else qkv
            forward.append((x, kept, sent, swap(sent)))
        before, got_gm = (), []
        for i, at in enumerate(chunks):
            mixes, places = [forward[i][3]], [lambda order, at=at: order[1] * mine + at]
            if i == 0:
                mixes, places = [own_mix] + mixes, [lambda order: order[0] * mine] + places
            before, gms = tokens(places, mixes, before, i == len(chunks) - 1)
            own_gm = gms[0] if i == 0 else own_gm
            got_gm.append(swap(gms[-1]))
        x_out, d_out, x_grad, packed = before
        qkv_grad, got_dx = None, []
        for i, at in enumerate(chunks):
            x, kept, sent, _ = forward[i]
            last = qkv_shape if i == len(chunks) - 1 else None
            (x_grad, dx), qkv_grad = attend_backward(
                order, at, mine, x, (own_mix, sent), (own_gm, got_gm[i]), qkv, kept, x_grad, qkv_grad, last, by_steps and last is not None
            )
            if got_dx:
                qkv_grad, got_dx[-1] = lax.optimization_barrier((qkv_grad, got_dx[-1]))
            got_dx.append(dx if last else swap(dx))
    else:

        def to_sequences(v):
            got = lax.all_to_all(v.reshape(parts, mine, rows, width), "mp", 0, 0)
            return got.transpose(1, 0, 2, 3).reshape(mine, length, width)

        def to_positions(v):
            sent = v.reshape(mine, parts, rows, width).transpose(1, 0, 2, 3)
            return lax.all_to_all(sent, "mp", 0, 0).reshape(total, rows, width)

        x = (to_sequences(x_in),)
        kept, (mix,) = attend_forward(order, 0, mine, x, qkv, own_segments, None)
        (x_out, d_out, grad_r1, packed), (gm,) = tokens([lambda order: 0], [to_positions(mix)], (), True)
        go = (to_sequences(gm),)
        (dx,), qkv_grad = attend_backward(order, 0, mine, x, (mix,), go, qkv, kept, None, None, qkv_shape)
        x_grad = grad_r1 + to_positions(dx).astype(f32)

    got = lax.psum_scatter(packed, "dp", scatter_dimension=1, tiled=True)

    states = (
        (w_qkv, qkv_mom, qkv_sec),
        (w_out, out_mom, out_sec),
        (w_in, in_mom, in_sec),
        (w_back, back_mom, back_sec),
        (norms, norm_mom, norm_sec),
    )
    if by_steps:
        own, theirs, got_dx[-1] = scatter_by_steps(*qkv_grad, got_dx[-1], got[1])
        turns = ((1, 0, 2), (1, 0), (0, 1), (1, 0), (0, 1))
        turned = [v.transpose(turn) for state, turn in zip(states, turns) for v in state]
        new = update(own, got, theirs, turned)
        new = [v.transpose(turns[i // 3]) for i, v in enumerate(new)]
    else:
        if parts == 2:
            got_dx[-1] = swap(got_dx[-1])
            grads = got[0].astype(f32) + swap(got[1]).astype(f32)
        else:
            grads = lax.psum_scatter(got, "mp", scatter_dimension=0, tiled=True)[0].astype(f32)
        in_g, back_g, norm_g, out_g = jnp.split(grads, [n_in, n_in + n_back, n_in + n_back + PAIR], axis=1)
        got = lax.psum_scatter(qkv_grad.reshape(owners, -1), "dp", scatter_dimension=0, tiled=True)
        qkv_g = lax.psum_scatter(got, "mp", scatter_dimension=1, tiled=True).astype(f32)
        grads = (qkv_g.reshape(own_rows, 3, qkv_n), out_g[:, :n_out].T, in_g, back_g.T, norm_g[:, : norms.shape[0]].T)
        new = [v for (w, m, v), g, rate in zip(states, grads, RATES) for v in adam_update(w, g, m, v, rate)]
    if parts == 2:
        for at, dx in zip(chunks, got_dx):
            at = other * mine + at
            added = here(x_grad, at, step) + dx.astype(f32)
            x_grad = lax.dynamic_update_slice_in_dim(x_grad, added, at, axis=0)
    return (x_out, d_out, x_grad, *new)


def solution(mesh):
    stream = P("dp", "mp", None)
    weights = (P("dp", None, "mp"), P("mp", "dp"), P("dp", "mp"), P("mp", "dp"), P(None, "dp"))
    states = tuple(spec for spec in weights for _ in range(2))
    news = tuple(spec for spec in weights for _ in range(3))
    return jax.shard_map(
        on_device,
        mesh=mesh,
        in_specs=(stream, stream, P("dp", None), stream, stream) + weights + states,
        out_specs=(stream, stream, stream) + news,
        check_vma=False,
    )
```
